128 devices in a mesh: seq: 16 (over x, y), head: 8 (over z, core).
Axes of the slice: x: 4, y: 4, z: 4, core: 2. Of those that a mesh axis runs over, the one named last changes fastest.
Arguments:
- query_rows: bfloat16 [16384, 2048], P('seq', 'head'), may hold values from -6 to 6
- key_rows: bfloat16 [16384, 2048], P('seq', 'head'), may hold values from -6 to 6
- value_rows: bfloat16 [16384, 2048], P('seq', 'head'), may hold values from -6 to 6
- norm_gain: float32 [2048], P('head'), may hold values from 0.5 to 1.5
- grad_out: bfloat16 [16384, 2048], P('seq', 'head'), may hold values from -6 to 6
- doc_lengths: int32 [3], replicated, may hold values from 1 to 12288, 16384 in all
- kept_blocks: int32 [16, 3, 8], replicated, may hold values from -1 to 15, as said below
Outputs:
- layer_out: bfloat16 [16384, 2048], P('seq', 'head')
- grad_queries: bfloat16 [16384, 2048], P('seq', 'head')
- grad_keys: bfloat16 [16384, 2048], P('seq', 'head')
- grad_values: bfloat16 [16384, 2048], P('seq', 'head')
- grad_gain: float32 [2048], P('head')
The draws below stay inside these ranges and needn't reach their ends.
Inputs may be any that keep to these rules, and one draw needn't show every extreme that they name: `kept_blocks`: entry [s, l, :] lists distinct blocks of 64 positions, numbered within shard s, that shard s retains for level l, followed by -1 in the unused slots; at least half of the 8 slots are used, and for every level some shard uses all 8.
All inputs are finite; a program needn't handle non-finite values.
Results may differ from the reference program's by a relative error of at most 0.04.
Values may be sent and summed in bfloat16 or wider, within the bound.
A program may use at most 128 MiB of HBM per device.

```python
import math
import jax
import jax.numpy as jnp
import numpy as np
from jax import lax

DH = 128
TOK_DEV = 1024
SEG = 512
BLOCK = 64
KEEP = 8
LEVELS = 3
DOCS = 3
HEADS = 16
WIDTH = 2048
TOKENS = 16384
N_SEQ = 16


def draw_query_rows(key, part):
    key = jax.random.fold_in(key, 11)
    base_draw = jnp.clip(jax.random.normal(key, (TOKENS, HEADS * DH), jnp.float32), -6.0, 6.0)
    return base_draw.astype(jnp.bfloat16)


def draw_key_rows(key, part):
    key = jax.random.fold_in(key, 12)
    base_draw = jnp.clip(jax.random.normal(key, (TOKENS, HEADS * DH), jnp.float32), -6.0, 6.0)
    return base_draw.astype(jnp.bfloat16)


def draw_value_rows(key, part):
    key = jax.random.fold_in(key, 13)
    head_of_column = (jnp.arange(HEADS * DH, dtype=jnp.int32) // DH).astype(jnp.float32)
    rise = head_of_column / max(HEADS - 1, 1)
    noise = jax.random.normal(key, (TOKENS, HEADS * DH), jnp.float32)
    shift = 0.5 + 1.5 * rise
    return jnp.clip(noise + shift[None, :], -6.0, 6.0).astype(jnp.bfloat16)


def draw_kept_blocks(key, part):
    key = jax.random.fold_in(key, 21)
    order_key, count_key, full_key = jax.random.split(key, 3)
    block_total = TOK_DEV // BLOCK
    order_keys = jax.random.split(order_key, N_SEQ * LEVELS)
    block_orders = jax.vmap(lambda one_key: jax.random.permutation(one_key, block_total))(order_keys)[:, :KEEP]
    block_orders = block_orders.reshape(N_SEQ, LEVELS, KEEP).astype(jnp.int32)
    counts = jax.random.randint(count_key, (N_SEQ, LEVELS), max(KEEP // 2, 1), KEEP + 1)
    full_shard = jax.random.randint(full_key, (LEVELS,), 0, N_SEQ)
    shard_ids = jnp.arange(N_SEQ, dtype=jnp.int32)
    counts = jnp.where(shard_ids[:, None] == full_shard[None, :], KEEP, counts)
    slot_ids = jnp.arange(KEEP, dtype=jnp.int32)
    return jnp.where(slot_ids[None, None, :] < counts[:, :, None], block_orders, -1).astype(jnp.int32)


def shard_levels(key, extent, cuts, low, top_value):
    factor_of = 1.0
    for dim, parts in cuts:
        draws = jax.random.uniform(jax.random.fold_in(jax.random.fold_in(key, 6), dim), (parts,), jnp.float32, low / len(cuts), top_value / len(cuts))
        factor_of = factor_of * jnp.repeat(jnp.exp(draws), extent[dim] // parts).reshape((-1,) + (1,) * (len(extent) - 1 - dim))
    return factor_of


def length_profile(number_of, total, bound, skew):
    portions = [(1 << 20) // math.isqrt(grade ** skew) + 1 for grade in range(2, number_of + 1)]
    rest, given = total - bound - (number_of - 1), [1] * (number_of - 1)
    while rest > 0:
        movable = [i for i in range(number_of - 1) if given[i] < bound]
        pool, budget = sum([portions[i] for i in movable]), rest
        for i in movable:
            addition = min(bound - given[i], max(1, budget * portions[i] // pool), rest)
            given[i] = given[i] + addition
            rest = rest - addition
    return np.array([bound] + given)


def uneven(rng, count, total, limit, skew):
    if count == 2:
        one = jax.random.randint(rng, (), max(1, total - limit), min(limit, total - 1) + 1)
        return jnp.stack([one, total - one])
    tallies = jnp.asarray(length_profile(count, total, limit, skew), jnp.int32)
    couples = (count - 1) // 2
    source_of, sink = tallies[1:1 + 2 * couples:2], tallies[2:2 + 2 * couples:2]
    room = jnp.minimum(source_of - 1, limit - sink)
    shifted = jax.random.randint(jax.random.fold_in(rng, 1), (couples,), 0, 1 << 20) % (room + 1)
    tallies = tallies.at[1:1 + 2 * couples:2].set(source_of - shifted).at[2:2 + 2 * couples:2].set(sink + shifted)
    return tallies[jax.random.permutation(jax.random.fold_in(rng, 2), count)]


def bell_draw(own_key, dims, spread, reach, cuts=(), kind=jnp.bfloat16):
    factor_of = shard_levels(own_key, dims, cuts, -0.22, 0.18) if cuts else 1.0
    values = jax.random.normal(own_key, dims, jnp.float32) * spread * factor_of
    return jnp.minimum(jnp.maximum(values, -reach), reach).astype(kind)


def setup_inputs(seed: int = 0) -> dict:
    seeds = jax.random.split(jax.random.key(seed), 8)
    query_rows = draw_query_rows(jax.random.fold_in(seeds[7], 71), 0)
    key_rows = draw_key_rows(jax.random.fold_in(seeds[7], 71), 0)
    value_rows = draw_value_rows(jax.random.fold_in(seeds[7], 71), 0)
    norm_gain = jnp.clip(1.0 + 0.1 * jax.random.normal(seeds[3], (WIDTH,), jnp.float32), 0.5, 1.5)
    grad_out = bell_draw(seeds[4], (TOKENS, WIDTH), 1.0, 6.0, ((0, 16), (1, 8)))
    doc_lengths = uneven(seeds[5], DOCS, TOKENS, 3 * TOKENS // 4, 0).astype(jnp.int32)
    kept_blocks = draw_kept_blocks(jax.random.fold_in(seeds[7], 71), 0)
    return dict(query_rows=query_rows, key_rows=key_rows, value_rows=value_rows, norm_gain=norm_gain, grad_out=grad_out, doc_lengths=doc_lengths, kept_blocks=kept_blocks)


NEG_FILL = -1e+30
NORM_EPS = 1e-05

def doc_index(positions, starts):
    return lax.optimization_barrier(jnp.sum((starts[None, :] <= positions[:, None]).astype(jnp.int32), axis=1)) - 1

def masked_scores(query_part, key_part, visible, score_scale):
    raw_scores = jnp.einsum('bihd,bjhd->bhij', query_part.astype(jnp.float32), key_part.astype(jnp.float32), precision=lax.Precision.HIGHEST)
    return jnp.where(visible[:, None], raw_scores * score_scale, NEG_FILL)

def token_major(statistic):
    group_batch, head_count, query_count = statistic.shape
    return jnp.transpose(statistic, (0, 2, 1)).reshape(group_batch * query_count, head_count)

def group_major(statistic, group_batch):
    token_total, head_count = statistic.shape
    return jnp.transpose(statistic.reshape(group_batch, token_total // group_batch, head_count), (0, 2, 1))[..., None]

def product_f32(form, left_part, right_part):
    return jnp.einsum(form, left_part.astype(jnp.float32), right_part.astype(jnp.float32), precision=lax.Precision.HIGHEST)

def reference(query_rows, key_rows, value_rows, norm_gain, grad_out, doc_lengths, kept_blocks):
    score_scale = DH ** (-0.5)
    seg_count = TOK_DEV // SEG
    kept_count = KEEP * BLOCK
    offsets_in = jnp.arange(BLOCK, dtype=jnp.int32)
    doc_starts = jnp.cumsum(doc_lengths) - doc_lengths
    all_docs = doc_index(jnp.arange(TOKENS, dtype=jnp.int32), doc_starts)
    gain_full = norm_gain.astype(jnp.float32)

    def block_rows(shard_id, which_level):
        listed = kept_blocks[shard_id, which_level]
        live_rows = jnp.repeat(listed >= 0, BLOCK)
        row_ids = (jnp.maximum(listed, 0)[:, None] * BLOCK + offsets_in[None, :]).reshape(kept_count)
        return (row_ids.astype(jnp.int32), live_rows)

    def one_shard(shard_id):
        row_start = (shard_id * TOK_DEV).astype(jnp.int32)
        own_docs = lax.dynamic_slice_in_dim(all_docs, row_start, TOK_DEV, 0)
        queries = lax.dynamic_slice_in_dim(query_rows, row_start, TOK_DEV, 0).reshape(TOK_DEV, HEADS, DH)
        keys_here = lax.dynamic_slice_in_dim(key_rows, row_start, TOK_DEV, 0)
        values_here = lax.dynamic_slice_in_dim(value_rows, row_start, TOK_DEV, 0)
        dout_here = lax.dynamic_slice_in_dim(grad_out, row_start, TOK_DEV, 0)
        seg_docs = own_docs.reshape(seg_count, SEG)
        key_groups = [(keys_here.reshape(seg_count, SEG, HEADS, DH), values_here.reshape(seg_count, SEG, HEADS, DH), seg_docs[:, :, None] == seg_docs[:, None, :], seg_count)]
        far_ids = []
        for which_level in range(LEVELS):
            partner = jnp.bitwise_xor(shard_id, 1 << which_level).astype(jnp.int32)
            row_ids, live_rows = block_rows(partner, which_level)
            far_rows = (partner * TOK_DEV + row_ids).astype(jnp.int32)
            visible = live_rows[None, :] & (own_docs[:, None] == all_docs[far_rows][None, :])
            key_groups.append((key_rows[far_rows].reshape(1, kept_count, HEADS, DH), value_rows[far_rows].reshape(1, kept_count, HEADS, DH), visible[None], 1))
            far_ids.append(far_rows)
        run_max = jnp.full((TOK_DEV, HEADS), NEG_FILL, jnp.float32)
        run_sum = jnp.zeros((TOK_DEV, HEADS), jnp.float32)
        for key_part, value_part, visible, group_batch in key_groups:
            query_part = queries.reshape(group_batch, TOK_DEV // group_batch, HEADS, DH)
            scores = masked_scores(query_part, key_part, visible, score_scale)
            local_max = lax.optimization_barrier(jnp.max(scores, axis=3, keepdims=True))
            local_sum = lax.optimization_barrier(jnp.sum(jnp.where(visible[:, None], jnp.exp(scores - local_max), 0.0), axis=3))
            group_max = token_major(local_max[..., 0])
            new_max = jnp.maximum(run_max, group_max)
            run_sum = run_sum * jnp.exp(run_max - new_max) + token_major(local_sum) * jnp.exp(group_max - new_max)
            run_max = new_max
        log_total = run_max + jnp.log(run_sum)
        attn_sum = jnp.zeros((TOK_DEV, HEADS, DH), jnp.float32)
        for key_part, value_part, visible, group_batch in key_groups:
            query_part = queries.reshape(group_batch, TOK_DEV // group_batch, HEADS, DH)
            scores = masked_scores(query_part, key_part, visible, score_scale)
            weights = jnp.where(visible[:, None], jnp.exp(scores - group_major(log_total, group_batch)), 0.0)
            weights_low = weights.astype(jnp.bfloat16)
            attn_sum = attn_sum + product_f32('bhij,bjhd->bihd', weights_low, value_part).reshape(TOK_DEV, HEADS, DH)
        attended = attn_sum.reshape(TOK_DEV, WIDTH).astype(jnp.bfloat16)
        attended_f = attended.astype(jnp.float32)
        mean_rows = lax.optimization_barrier(jnp.mean(attended_f, axis=1, keepdims=True))
        centred = attended_f - mean_rows
        inv_std = lax.rsqrt(lax.optimization_barrier(jnp.mean(centred * centred, axis=1, keepdims=True)) + NORM_EPS)
        normed = centred * inv_std
        layer_out = (normed * gain_full[None, :]).astype(jnp.bfloat16)
        dout_f = dout_here.astype(jnp.float32)
        gain_part = lax.optimization_barrier(jnp.sum(dout_f * normed, axis=0))
        scaled = dout_f * gain_full[None, :]
        grad_attended = (inv_std * (scaled - lax.optimization_barrier(jnp.mean(scaled, axis=1, keepdims=True)) - normed * lax.optimization_barrier(jnp.mean(scaled * normed, axis=1, keepdims=True)))).astype(jnp.bfloat16)
        dout_heads = grad_attended.reshape(TOK_DEV, HEADS, DH)
        row_delta = lax.optimization_barrier(jnp.sum(dout_heads.astype(jnp.float32) * attended.reshape(TOK_DEV, HEADS, DH).astype(jnp.float32), axis=2))
        query_grad = jnp.zeros((TOK_DEV, HEADS, DH), jnp.float32)
        far_grads = []
        for group_number, (key_part, value_part, visible, group_batch) in enumerate(key_groups):
            query_part = queries.reshape(group_batch, TOK_DEV // group_batch, HEADS, DH)
            dout_part = dout_heads.reshape(group_batch, TOK_DEV // group_batch, HEADS, DH)
            scores = masked_scores(query_part, key_part, visible, score_scale)
            weights = jnp.where(visible[:, None], jnp.exp(scores - group_major(log_total, group_batch)), 0.0)
            weights_low = weights.astype(jnp.bfloat16)
            dprob = product_f32('bihd,bjhd->bhij', dout_part, value_part)
            dscore = (weights * (dprob - group_major(row_delta, group_batch)) * score_scale).astype(jnp.bfloat16)
            query_grad = query_grad + product_f32('bhij,bjhd->bihd', dscore, key_part).reshape(TOK_DEV, HEADS, DH)
            key_grad = product_f32('bhij,bihd->bjhd', dscore, query_part).reshape(-1, WIDTH)
            value_grad = product_f32('bhij,bihd->bjhd', weights_low, dout_part).reshape(-1, WIDTH)
            if group_number == 0:
                key_local, value_local = (key_grad, value_grad)
            else:
                far_grads.append(jnp.stack([key_grad, value_grad]))
        return (layer_out, query_grad.reshape(TOK_DEV, WIDTH).astype(jnp.bfloat16), key_local, value_local, jnp.stack(far_grads), jnp.stack(far_ids), gain_part)
    results = lax.map(one_shard, jnp.arange(N_SEQ, dtype=jnp.int32))
    layer_out = results[0].reshape(TOKENS, WIDTH)
    grad_queries = results[1].reshape(TOKENS, WIDTH)
    far_rows = results[5].reshape(-1)
    grad_keys = results[2].reshape(TOKENS, WIDTH).at[far_rows].add(results[4][:, :, 0].reshape(-1, WIDTH))
    grad_values = results[3].reshape(TOKENS, WIDTH).at[far_rows].add(results[4][:, :, 1].reshape(-1, WIDTH))
    grad_gain = lax.optimization_barrier(jnp.sum(results[6], axis=0))
    return (layer_out, grad_queries, grad_keys.astype(jnp.bfloat16), grad_values.astype(jnp.bfloat16), grad_gain)
```

```python
import functools

import jax
import jax.numpy as jnp
from jax import lax
from jax.experimental import pallas as pl
from jax.experimental.pallas import tpu as pltpu
from jax.sharding import PartitionSpec as P

DH = 128
TOK = 1024
SEG = 512
BLOCK = 64
KEEP = 8
LEVELS = 3
KEPT = KEEP * BLOCK
CHUNK = 256
NCH = KEPT // CHUNK
TILE = 256
WIDTH = 2048
HEADS_DEV = 2
COLS = HEADS_DEV * DH
N_SEQ = 16
N_HEAD = 8
NORM_EPS = 1e-05
SCALE = DH**-0.5
LOG2E = 1.4426950408889634
BIG = 2.0**100
LOW = -(2.0**99)
MESH = pl.DeviceIdType.MESH
F32 = jnp.float32
BF16 = jnp.bfloat16


def dot(a, b, ca, cb):
    return lax.dot_general(a, b, (((ca,), (cb,)), ((), ())), preferred_element_type=F32)


def turned(x):
    return jnp.transpose(x.astype(F32)).astype(x.dtype)


def flipped(index, bit):
    return index + bit * (1 - 2 * lax.rem(index // bit, 2))


def level_bit(level):
    return 1 + level + level // 2


def kernel(
    kept,
    lengths,
    q_ref,
    k_ref,
    v_ref,
    gain_ref,
    g_ref,
    lo_ref,
    dq_ref,
    dk_ref,
    dv_ref,
    gg_ref,
    qa,
    mk_loc,
    mk_far,
    kv_out,
    kv_in,
    gr_out,
    gr_in0,
    gr_in1,
    gr_in2,
    kt_loc,
    vt_loc,
    kt_far,
    vt_far,
    p_loc,
    p_far,
    m_run,
    m_loc,
    m_far,
    acc,
    inv_l,
    at,
    gt,
    gc,
    st,
    res,
    dot_,
    delta,
    dqt,
    dkv,
    gsum,
    inv_slot,
    kv_ss,
    kv_rs,
    gr_ss,
    gr_rs,
    st_ss,
    st_rs,
    gg_ss,
    gg_rs,
):
    me = lax.axis_index("seq")
    col = lax.axis_index("head")

    barrier = pltpu.get_barrier_semaphore()
    for bit in (1, 2, 4, 8):
        pl.semaphore_signal(barrier, inc=1, device_id=(flipped(me, bit), col), device_id_type=MESH)
    for d in range(1, N_HEAD):
        pl.semaphore_signal(
            barrier, inc=1, device_id=(me, lax.rem(col + d, N_HEAD)), device_id_type=MESH
        )

    for level in range(LEVELS):
        for slot in range(KEEP):
            block = jnp.maximum(kept[me, level, slot], 0)
            kv_out[level, slot * BLOCK : (slot + 1) * BLOCK, 0:COLS] = k_ref[block]
            kv_out[level, slot * BLOCK : (slot + 1) * BLOCK, COLS:] = v_ref[block]
    pl.semaphore_wait(barrier, 4 + N_HEAD - 1)

    def kv_copy(level, c):
        rows = pl.ds(pl.multiple_of(c * CHUNK, CHUNK), CHUNK)
        return pltpu.make_async_remote_copy(
            src_ref=kv_out.at[level, rows],
            dst_ref=kv_in.at[level, rows],
            send_sem=kv_ss.at[level, c],
            recv_sem=kv_rs.at[level, c],
            device_id=(flipped(me, level_bit(level)), col),
            device_id_type=MESH,
        )

    gr_in = (gr_in0, gr_in1, gr_in2)

    def gr_copy(level, c):
        return pltpu.make_async_remote_copy(
            src_ref=gr_out.at[level, pl.ds(c * (CHUNK // BLOCK), CHUNK // BLOCK)],
            dst_ref=gr_in[level].at[pl.ds(c * (CHUNK // BLOCK), CHUNK // BLOCK)],
            send_sem=gr_ss.at[level, c],
            recv_sem=gr_rs.at[level, c],
            device_id=(flipped(me, level_bit(level)), col),
            device_id_type=MESH,
        )

    for c in range(NCH):
        for level in (2, 0, 1):
            kv_copy(level, c).start()

    start1 = lengths[0]
    start2 = lengths[0] + lengths[1]

    def doc_of(pos):
        return (pos >= start1).astype(jnp.int32) + (pos >= start2).astype(jnp.int32)

    lane = lax.broadcasted_iota(jnp.int32, (BLOCK, DH), 1)
    row = lax.broadcasted_iota(jnp.int32, (BLOCK, DH), 0)
    for b in range(TOK // BLOCK):
        rows = slice(b * BLOCK, (b + 1) * BLOCK)
        docs = doc_of(me * TOK + b * BLOCK + row)
        same = docs == lane
        mq = jnp.where(same, 1.0, 0.0).astype(BF16)
        mk_loc[rows, :] = jnp.where(same | (lane >= 3), 0.0, -BIG).astype(BF16)
        for h in range(HEADS_DEV):
            qa[h, rows, DH:] = mq
            qa[h, rows, 0:DH] = q_ref[rows, h * DH : (h + 1) * DH]
    for level in range(LEVELS):
        partner = flipped(me, level_bit(level))
        for slot in range(KEEP):
            listed = kept[partner, level, slot]
            docs = doc_of(partner * TOK + jnp.maximum(listed, 0) * BLOCK + row)
            docs = docs - 3 * jnp.minimum(listed, 0)
            same = docs == lane
            mk_far[level, slot * BLOCK : (slot + 1) * BLOCK, :] = jnp.where(
                same | (lane >= 3), 0.0, -BIG
            ).astype(BF16)

    ones = jnp.ones((16, TOK), BF16)
    for h in range(HEADS_DEV):
        vt_loc[h, DH:, :] = ones
        for level in range(LEVELS):
            vt_far[level, h, DH:, :] = ones[:, 0:KEPT]

    for t in range(TOK // TILE):
        cols = slice(t * TILE, (t + 1) * TILE)
        blocks = slice(t * (TILE // BLOCK), (t + 1) * (TILE // BLOCK))
        kt_loc[:, cols] = turned(k_ref[blocks].reshape(TILE, COLS))
        vt = turned(v_ref[blocks].reshape(TILE, COLS))
        for h in range(HEADS_DEV):
            vt_loc[h, 0:DH, cols] = vt[h * DH : (h + 1) * DH]

    coef = SCALE * LOG2E

    @pl.loop(0, TOK // SEG)
    def _(t):
        keys = pl.ds(pl.multiple_of(t * SEG, SEG), SEG)
        blocks = pl.ds(t * (SEG // BLOCK), SEG // BLOCK)
        for h in range(HEADS_DEV):
            k = k_ref[blocks, :, h * DH : (h + 1) * DH].reshape(SEG, DH)
            ka = jnp.concatenate([k, mk_loc[keys, :]], axis=1)
            vt = vt_loc[h, :, keys]
            for j in range(SEG // TILE):
                qs = pl.ds(pl.multiple_of(t * SEG + j * TILE, TILE), TILE)
                s = dot(ka, qa[h, qs, :], 1, 1)
                m = jnp.maximum(jnp.max(s, axis=0, keepdims=True), LOW)
                p = jnp.exp2((s - m) * coef).astype(BF16)
                p_loc[h, :, qs] = p
                m_run[h, :, qs] = m
                m_loc[h, :, qs] = m
                acc[h, :, qs] = dot(vt, p, 1, 0)

    gc[...] = jnp.transpose(jnp.broadcast_to(gain_ref[...], (DH, COLS)))
    for t in range(TOK // TILE):
        cols = slice(t * TILE, (t + 1) * TILE)
        gt[:, cols] = jnp.transpose(g_ref[cols, :].astype(F32))

    @pl.loop(0, LEVELS * (TOK // BLOCK))
    def _(i):
        level = i // (TOK // BLOCK)
        b = lax.rem(i, TOK // BLOCK)
        found = jnp.int32(-1)
        for slot in range(KEEP):
            off = kept[me, level, slot] - b
            found = jnp.maximum(found, (slot + 1) * (1 - jnp.minimum(off * off, 1)) - 1)
        inv_slot[i] = found

    @pl.loop(0, LEVELS * NCH)
    def _(t):
        level = lax.rem(t + 2, 3)
        c = t // 3
        kv_copy(level, c).wait()
        rows = pl.ds(pl.multiple_of(c * CHUNK, CHUNK), CHUNK)
        kt_far[level, :, rows] = turned(kv_in[level, rows, 0:COLS])
        vt = turned(kv_in[level, rows, COLS:])
        for h in range(HEADS_DEV):
            vt_far[level, h, 0:DH, rows] = vt[h * DH : (h + 1) * DH]
        for h in range(HEADS_DEV):
            ka = jnp.concatenate(
                [kv_in[level, rows, h * DH : (h + 1) * DH], mk_far[level, rows, :]], axis=1
            )
            vta = vt_far[level, h, :, rows]
            for j in range(TOK // TILE):
                qs = slice(j * TILE, (j + 1) * TILE)
                s = dot(ka, qa[h, qs, :], 1, 1)
                m_old = m_run[h, :, qs]
                m = jnp.maximum(jnp.max(s, axis=0, keepdims=True), m_old)
                p = jnp.exp2((s - m) * coef).astype(BF16)
                p_far[level, h, rows, qs] = p
                m_run[h, :, qs] = m
                m_far[level, c, h, :, qs] = m
                acc[h, :, qs] = acc[h, :, qs] * jnp.exp2((m_old - m) * coef) + dot(vta, p, 1, 0)

    for i in range(TOK // DH):
        qs = slice(i * DH, (i + 1) * DH)
        total = jnp.zeros((1, DH), F32)
        for h in range(HEADS_DEV):
            inv = 1.0 / acc[h, DH : DH + 1, qs]
            inv_l[h, :, qs] = inv
            a = (acc[h, 0:DH, qs] * inv).astype(BF16).astype(F32)
            at[h * DH : (h + 1) * DH, qs] = a
            total = total + jnp.sum(a, axis=0, keepdims=True)
        mean = total * (1.0 / COLS)
        centred = at[:, qs] - mean
        scaled = gt[:, qs] * gc[...]
        st[0, i : i + 1, 0:128] = mean
        st[0, i : i + 1, 128:256] = jnp.sum(centred * centred, axis=0, keepdims=True)
        st[0, i : i + 1, 256:384] = jnp.sum(scaled, axis=0, keepdims=True)
        st[0, i : i + 1, 384:512] = jnp.sum(scaled * centred, axis=0, keepdims=True)

    def st_copy(d):
        return pltpu.make_async_remote_copy(
            src_ref=st.at[0],
            dst_ref=st.at[d],
            send_sem=st_ss.at[d],
            recv_sem=st_rs.at[d],
            device_id=(me, lax.rem(col + d, N_HEAD)),
            device_id_type=MESH,
        )

    for d in range(1, N_HEAD):
        st_copy(d).start()
    for d in range(1, N_HEAD):
        st_copy(d).wait()

    mean = st[0, :, 0:128]
    for d in range(1, N_HEAD):
        mean = mean + st[d, :, 0:128]
    mean = mean * (1.0 / N_HEAD)
    square = jnp.zeros((8, DH), F32)
    plain = jnp.zeros((8, DH), F32)
    cross = jnp.zeros((8, DH), F32)
    for d in range(N_HEAD):
        off = st[d, :, 0:128] - mean
        square = square + (st[d, :, 128:256] + COLS * (off * off))
        plain = plain + st[d, :, 256:384]
        cross = cross + (st[d, :, 384:512] + off * st[d, :, 256:384])
    inv_std = lax.rsqrt(square * (1.0 / WIDTH) + NORM_EPS)
    res[:, 0:128] = mean
    res[:, 128:256] = inv_std
    res[:, 256:384] = plain * (1.0 / WIDTH)
    res[:, 384:512] = inv_std * cross * (1.0 / WIDTH)

    for i in range(TOK // DH):
        qs = slice(i * DH, (i + 1) * DH)
        inv_std = res[i : i + 1, 128:256]
        normed = (at[:, qs] - res[i : i + 1, 0:128]) * inv_std
        scaled = gt[:, qs] * gc[...]
        do = inv_std * (scaled - res[i : i + 1, 256:384] - normed * res[i : i + 1, 384:512])
        do = do.astype(BF16)
        dot_[:, qs] = do
        both = do.astype(F32) * at[:, qs]
        for h in range(HEADS_DEV):
            delta[h, :, qs] = jnp.sum(both[h * DH : (h + 1) * DH], axis=0, keepdims=True)

    def back(h, qs, m, v, kt, p):
        factor = jnp.exp2((m - m_run[h, :, qs]) * coef) * inv_l[h, :, qs]
        do = (dot_[h * DH : (h + 1) * DH, qs].astype(F32) * factor).astype(BF16)
        dp = dot(v, do, 1, 0)
        ds = (p.astype(F32) * (dp - factor * delta[h, :, qs])).astype(BF16)
        dq = dot(kt, ds, 1, 0)
        dk = dot(ds, qa[h, qs, 0:DH], 1, 0)
        dv = dot(p, do, 1, 1)
        return dq, dk, dv

    dqt[...] = jnp.zeros_like(dqt)

    @pl.loop(0, LEVELS * NCH)
    def _(t):
        level = lax.rem(4 - lax.rem(t, 3), 3)
        c = t // 3
        rows = pl.ds(pl.multiple_of(c * CHUNK, CHUNK), CHUNK)
        for h in range(HEADS_DEV):
            hs = slice(h * DH, (h + 1) * DH)
            v = kv_in[level, rows, COLS + h * DH : COLS + (h + 1) * DH]
            kt = kt_far[level, hs, rows]
            dk_sum = jnp.zeros((CHUNK, DH), F32)
            dv_sum = jnp.zeros((CHUNK, DH), F32)
            for j in range(TOK // TILE):
                qs = slice(j * TILE, (j + 1) * TILE)
                dq, dk, dv = back(h, qs, m_far[level, c, h, :, qs], v, kt, p_far[level, h, rows, qs])
                dqt[hs, qs] += dq
                dk_sum = dk_sum + dk
                dv_sum = dv_sum + dv
            blocks = pl.ds(c * (CHUNK // BLOCK), CHUNK // BLOCK)
            vs = slice(COLS + h * DH, COLS + (h + 1) * DH)
            shape = (CHUNK // BLOCK, BLOCK, DH)
            gr_out[level, blocks, :, hs] = (dk_sum * SCALE).astype(BF16).reshape(shape)
            gr_out[level, blocks, :, vs] = dv_sum.astype(BF16).reshape(shape)
        for one in range(LEVELS):
            pl.when(level == one)(lambda one=one: gr_copy(one, c).start())

    gain_part = jnp.zeros((COLS, DH), F32)
    for i in range(TOK // DH):
        qs = slice(i * DH, (i + 1) * DH)
        normed = (at[:, qs] - res[i : i + 1, 0:128]) * res[i : i + 1, 128:256]
        gain_part = gain_part + gt[:, qs] * normed
        lo_ref[qs, :] = jnp.transpose(normed * gc[...]).astype(BF16)
    gsum[0] = jnp.broadcast_to(
        jnp.sum(jnp.transpose(gain_part), axis=0, keepdims=True), (8, COLS)
    )

    def gg_copy(stage):
        return pltpu.make_async_remote_copy(
            src_ref=gsum.at[2 * stage],
            dst_ref=gsum.at[2 * stage + 1],
            send_sem=gg_ss.at[stage],
            recv_sem=gg_rs.at[stage],
            device_id=(flipped(me, 1 << stage), col),
            device_id_type=MESH,
        )

    gg_copy(0).start()

    @pl.loop(0, TOK // SEG)
    def _(t):
        keys = pl.ds(pl.multiple_of(t * SEG, SEG), SEG)
        blocks = pl.ds(t * (SEG // BLOCK), SEG // BLOCK)
        for h in range(HEADS_DEV):
            hs = slice(h * DH, (h + 1) * DH)
            v = v_ref[blocks, :, hs].reshape(SEG, DH)
            kt = kt_loc[hs, keys]
            dk_sum = jnp.zeros((SEG, DH), F32)
            dv_sum = jnp.zeros((SEG, DH), F32)
            for j in range(SEG // TILE):
                qs = pl.ds(pl.multiple_of(t * SEG + j * TILE, TILE), TILE)
                dq, dk, dv = back(h, qs, m_loc[h, :, qs], v, kt, p_loc[h, :, qs])
                dqt[hs, qs] += dq
                dk_sum = dk_sum + dk
                dv_sum = dv_sum + dv
            dkv[keys, hs] = dk_sum * SCALE
            dkv[keys, COLS + h * DH : COLS + (h + 1) * DH] = dv_sum

    for stage in range(4):
        gg_copy(stage).wait()
        gsum[2 * stage + 2] = gsum[2 * stage] + gsum[2 * stage + 1]
        if stage < 3:
            gg_copy(stage + 1).start()
        for t in range(stage, TOK // TILE, 4):
            cols = slice(t * TILE, (t + 1) * TILE)
            dq_ref[cols, :] = jnp.transpose(dqt[:, cols] * SCALE).astype(BF16)
    gg_ref[...] = gsum[8, 0:1, :]

    for level in (2, 0, 1):
        for c in range(NCH):
            gr_copy(level, c).wait()

        @pl.loop(0, TOK // BLOCK)
        def _(b):
            slot = inv_slot[level * (TOK // BLOCK) + b]
            rows = pl.ds(pl.multiple_of(b * BLOCK, BLOCK), BLOCK)
            part = gr_in[level][jnp.maximum(slot, 0)].astype(F32)
            total = dkv[rows, :] + part * jnp.minimum(slot + 1, 1).astype(F32)
            if level == 1:
                dk_ref[rows, :] = total[:, 0:COLS].astype(BF16)
                dv_ref[rows, :] = total[:, COLS:].astype(BF16)
            else:
                dkv[rows, :] = total


def local(query_rows, key_rows, value_rows, norm_gain, grad_out, doc_lengths, kept_blocks):
    vmem = pl.BlockSpec(memory_space=pltpu.VMEM)
    smem = pl.BlockSpec(memory_space=pltpu.SMEM)
    rows = jax.ShapeDtypeStruct((TOK, COLS), BF16)
    dma = pltpu.SemaphoreType.DMA
    scratch = [
        pltpu.VMEM((HEADS_DEV, TOK, 2 * DH), BF16),
        pltpu.VMEM((TOK, DH), BF16),
        pltpu.VMEM((LEVELS, KEPT, DH), BF16),
        pltpu.VMEM((LEVELS, KEPT, 2 * COLS), BF16),
        pltpu.VMEM((LEVELS, KEPT, 2 * COLS), BF16),
        pltpu.VMEM((LEVELS, KEEP, BLOCK, 2 * COLS), BF16),
        pltpu.VMEM((KEEP, BLOCK, 2 * COLS), BF16),
        pltpu.VMEM((KEEP, BLOCK, 2 * COLS), BF16),
        pltpu.VMEM((KEEP, BLOCK, 2 * COLS), BF16),
        pltpu.VMEM((COLS, TOK), BF16),
        pltpu.VMEM((HEADS_DEV, DH + 16, TOK), BF16),
        pltpu.VMEM((LEVELS, COLS, KEPT), BF16),
        pltpu.VMEM((LEVELS, HEADS_DEV, DH + 16, KEPT), BF16),
        pltpu.VMEM((HEADS_DEV, SEG, TOK), BF16),
        pltpu.VMEM((LEVELS, HEADS_DEV, KEPT, TOK), BF16),
        pltpu.VMEM((HEADS_DEV, 1, TOK), F32),
        pltpu.VMEM((HEADS_DEV, 1, TOK), F32),
        pltpu.VMEM((LEVELS, NCH, HEADS_DEV, 1, TOK), F32),
        pltpu.VMEM((HEADS_DEV, DH + 16, TOK), F32),
        pltpu.VMEM((HEADS_DEV, 1, TOK), F32),
        pltpu.VMEM((COLS, TOK), F32),
        pltpu.VMEM((COLS, TOK), F32),
        pltpu.VMEM((COLS, DH), F32),
        pltpu.VMEM((N_HEAD, 8, 512), F32),
        pltpu.VMEM((8, 512), F32),
        pltpu.VMEM((COLS, TOK), BF16),
        pltpu.VMEM((HEADS_DEV, 1, TOK), F32),
        pltpu.VMEM((COLS, TOK), F32),
        pltpu.VMEM((TOK, 2 * COLS), F32),
        pltpu.VMEM((9, 8, COLS), F32),
        pltpu.SMEM((LEVELS * (TOK // BLOCK),), jnp.int32),
        dma((LEVELS, NCH)),
        dma((LEVELS, NCH)),
        dma((LEVELS, NCH)),
        dma((LEVELS, NCH)),
        dma((N_HEAD,)),
        dma((N_HEAD,)),
        dma((4,)),
        dma((4,)),
    ]
    out = pl.pallas_call(
        kernel,
        out_shape=[rows, rows, rows, rows, jax.ShapeDtypeStruct((1, COLS), F32)],
        in_specs=[smem, smem, vmem, vmem, vmem, vmem, vmem],
        out_specs=[vmem] * 5,
        scratch_shapes=scratch,
        compiler_params=pltpu.CompilerParams(
            collective_id=0, has_side_effects=True, vmem_limit_bytes=56 * 1024 * 1024
        ),
        name="attention",
    )(
        kept_blocks,
        doc_lengths,
        query_rows,
        key_rows.reshape(TOK // BLOCK, BLOCK, COLS),
        value_rows.reshape(TOK // BLOCK, BLOCK, COLS),
        norm_gain.reshape(1, COLS),
        grad_out,
    )
    return out[0], out[1], out[2], out[3], out[4].reshape(COLS)


def solution(mesh):
    rows = P("seq", "head")
    in_specs = (rows, rows, rows, P("head"), rows, P(), P())
    out_specs = (rows, rows, rows, rows, P("head"))
    return jax.shard_map(local, mesh=mesh, in_specs=in_specs, out_specs=out_specs, check_vma=False)
```

```python
import functools

import jax
import jax.numpy as jnp
from jax import lax
from jax.experimental import pallas as pl
from jax.experimental.pallas import tpu as pltpu
from jax.sharding import PartitionSpec as P

DH = 128
TOK = 1024
SEG = 512
BLOCK = 64
KEEP = 8
LEVELS = 3
KEPT = KEEP * BLOCK
CHUNK = 256
NCH = KEPT // CHUNK
TILE = 256
WIDTH = 2048
HEADS_DEV = 2
COLS = HEADS_DEV * DH
N_SEQ = 16
N_HEAD = 8
NORM_EPS = 1e-05
SCALE = DH**-0.5
LOG2E = 1.4426950408889634
BIG = 2.0**100
LOW = -(2.0**99)
MESH = pl.DeviceIdType.MESH
F32 = jnp.float32
BF16 = jnp.bfloat16


def dot(a, b, ca, cb):
    return lax.dot_general(a, b, (((ca,), (cb,)), ((), ())), preferred_element_type=F32)


def turned(x):
    return jnp.transpose(x.astype(F32)).astype(x.dtype)


def flipped(index, bit):
    return index + bit * (1 - 2 * lax.rem(index // bit, 2))


def level_bit(level):
    return 1 + level + level // 2


def kernel(
    kept,
    lengths,
    q_hbm,
    k_hbm,
    v_hbm,
    gain_hbm,
    g_hbm,
    lo_hbm,
    dq_hbm,
    part_hbm,
    gr_hbm,
    gg_ref,
    q_ref,
    k_ref,
    v_ref,
    gain_ref,
    g_ref,
    lo_ref,
    dq_ref,
    qa,
    mk_loc,
    mk_far,
    kv_out,
    kv_in,
    gr_out,
    gr_in2,
    kt_loc,
    vt_loc,
    kt_far,
    vt_far,
    p_loc,
    p_far,
    m_run,
    m_loc,
    m_far,
    acc,
    inv_l,
    at,
    gt,
    gc,
    st,
    res,
    dot_,
    delta,
    dqt,
    dkv,
    gsum,
    inv_slot,
    kv_ss,
    kv_rs,
    gr_ss,
    gr_rs,
    st_ss,
    st_rs,
    gg_ss,
    gg_rs,
    io,
):
    me = lax.axis_index("seq")
    col = lax.axis_index("head")

    barrier = pltpu.get_barrier_semaphore()
    for bit in (1, 2, 4, 8):
        pl.semaphore_signal(barrier, inc=1, device_id=(flipped(me, bit), col), device_id_type=MESH)
    for d in range(1, N_HEAD):
        pl.semaphore_signal(
            barrier, inc=1, device_id=(me, lax.rem(col + d, N_HEAD)), device_id_type=MESH
        )

    loads = [
        pltpu.make_async_copy(src, dst, io.at[i])
        for i, (src, dst) in enumerate(
            (
                (k_hbm, k_ref),
                (v_hbm, v_ref),
                (q_hbm, q_ref),
                (g_hbm, g_ref),
                (gain_hbm, gain_ref),
            )
        )
    ]
    for load in loads:
        load.start()
    loads[0].wait()
    loads[1].wait()

    for level in range(LEVELS):
        for slot in range(KEEP):
            block = jnp.maximum(kept[level, slot, me], 0)
            kv_out[level, slot * BLOCK : (slot + 1) * BLOCK, 0:COLS] = k_ref[block]
            kv_out[level, slot * BLOCK : (slot + 1) * BLOCK, COLS:] = v_ref[block]
    pl.semaphore_wait(barrier, 4 + N_HEAD - 1)

    def kv_copy(level, c):
        rows = pl.ds(pl.multiple_of(c * CHUNK, CHUNK), CHUNK)
        return pltpu.make_async_remote_copy(
            src_ref=kv_out.at[level, rows],
            dst_ref=kv_in.at[level, rows],
            send_sem=kv_ss.at[level, c],
            recv_sem=kv_rs.at[level, c],
            device_id=(flipped(me, level_bit(level)), col),
            device_id_type=MESH,
        )

    def gr_copy(level, c, h):
        blocks = pl.ds(c * (CHUNK // BLOCK), CHUNK // BLOCK)
        dst = gr_in2 if level == 2 else gr_hbm.at[level]
        return pltpu.make_async_remote_copy(
            src_ref=gr_out.at[level, h, blocks],
            dst_ref=dst.at[h, blocks],
            send_sem=gr_ss.at[level, c, h],
            recv_sem=gr_rs.at[level, c, h],
            device_id=(flipped(me, level_bit(level)), col),
            device_id_type=MESH,
        )

    for c in range(NCH):
        for level in (2, 0, 1):
            kv_copy(level, c).start()

    for load in loads[2:]:
        load.wait()
    start1 = lengths[0]
    start2 = lengths[0] + lengths[1]

    def doc_of(pos):
        return (pos >= start1).astype(jnp.int32) + (pos >= start2).astype(jnp.int32)

    lane = lax.broadcasted_iota(jnp.int32, (BLOCK, DH), 1)
    row = lax.broadcasted_iota(jnp.int32, (BLOCK, DH), 0)
    for b in range(TOK // BLOCK):
        rows = slice(b * BLOCK, (b + 1) * BLOCK)
        docs = doc_of(me * TOK + b * BLOCK + row)
        same = docs == lane
        mq = jnp.where(same, 1.0, 0.0).astype(BF16)
        mk_loc[rows, :] = jnp.where(same | (lane >= 3), 0.0, -BIG).astype(BF16)
        for h in range(HEADS_DEV):
            qa[h, rows, DH:] = mq
            qa[h, rows, 0:DH] = q_ref[rows, h * DH : (h + 1) * DH]
    for level in range(LEVELS):
        partner = flipped(me, level_bit(level))
        for slot in range(KEEP):
            listed = kept[level, slot, partner]
            docs = doc_of(partner * TOK + jnp.maximum(listed, 0) * BLOCK + row)
            docs = docs - 3 * jnp.minimum(listed, 0)
            same = docs == lane
            mk_far[level, slot * BLOCK : (slot + 1) * BLOCK, :] = jnp.where(
                same | (lane >= 3), 0.0, -BIG
            ).astype(BF16)

    ones = jnp.ones((16, TOK), BF16)
    for h in range(HEADS_DEV):
        vt_loc[h, DH:, :] = ones
        for level in range(LEVELS):
            vt_far[level, h, DH:, :] = ones[:, 0:KEPT]

    for t in range(TOK // TILE):
        cols = slice(t * TILE, (t + 1) * TILE)
        blocks = slice(t * (TILE // BLOCK), (t + 1) * (TILE // BLOCK))
        kt_loc[:, cols] = turned(k_ref[blocks].reshape(TILE, COLS))
        vt = turned(v_ref[blocks].reshape(TILE, COLS))
        for h in range(HEADS_DEV):
            vt_loc[h, 0:DH, cols] = vt[h * DH : (h + 1) * DH]

    coef = SCALE * LOG2E

    @pl.loop(0, TOK // SEG)
    def _(t):
        keys = pl.ds(pl.multiple_of(t * SEG, SEG), SEG)
        blocks = pl.ds(t * (SEG // BLOCK), SEG // BLOCK)
        for h in range(HEADS_DEV):
            k = k_ref[blocks, :, h * DH : (h + 1) * DH].reshape(SEG, DH)
            ka = jnp.concatenate([k, mk_loc[keys, :]], axis=1)
            vt = vt_loc[h, :, keys]
            for j in range(SEG // TILE):
                qs = pl.ds(pl.multiple_of(t * SEG + j * TILE, TILE), TILE)
                s = dot(ka, qa[h, qs, :], 1, 1)
                m = jnp.maximum(jnp.max(s, axis=0, keepdims=True), LOW)
                p = jnp.exp2((s - m) * coef).astype(BF16)
                p_loc[h, :, qs] = p
                m_run[h, :, qs] = m
                m_loc[h, :, qs] = m
                acc[h, :, qs] = dot(vt, p, 1, 0)

    gc[...] = jnp.transpose(jnp.broadcast_to(gain_ref[...], (DH, COLS)))
    for t in range(TOK // TILE):
        cols = slice(t * TILE, (t + 1) * TILE)
        gt[:, cols] = jnp.transpose(g_ref[cols, :].astype(F32))

    @pl.loop(0, TOK // BLOCK)
    def _(b):
        found = jnp.int32(-1)
        for slot in range(KEEP):
            off = kept[2, slot, me] - b
            found = jnp.maximum(found, (slot + 1) * (1 - jnp.minimum(off * off, 1)) - 1)
        inv_slot[b] = found

    @pl.loop(0, LEVELS * NCH)
    def _(t):
        level = lax.rem(t + 2, 3)
        c = t // 3
        kv_copy(level, c).wait()
        rows = pl.ds(pl.multiple_of(c * CHUNK, CHUNK), CHUNK)
        kt_far[level, :, rows] = turned(kv_in[level, rows, 0:COLS])
        vt = turned(kv_in[level, rows, COLS:])
        for h in range(HEADS_DEV):
            vt_far[level, h, 0:DH, rows] = vt[h * DH : (h + 1) * DH]
        for h in range(HEADS_DEV):
            ka = jnp.concatenate(
                [kv_in[level, rows, h * DH : (h + 1) * DH], mk_far[level, rows, :]], axis=1
            )
            vta = vt_far[level, h, :, rows]
            for j in range(TOK // TILE):
                qs = slice(j * TILE, (j + 1) * TILE)
                s = dot(ka, qa[h, qs, :], 1, 1)
                m_old = m_run[h, :, qs]
                m = jnp.maximum(jnp.max(s, axis=0, keepdims=True), m_old)
                p = jnp.exp2((s - m) * coef).astype(BF16)
                p_far[level, h, rows, qs] = p
                m_run[h, :, qs] = m
                m_far[level, c, h, :, qs] = m
                acc[h, :, qs] = acc[h, :, qs] * jnp.exp2((m_old - m) * coef) + dot(vta, p, 1, 0)

    for i in range(TOK // DH):
        qs = slice(i * DH, (i + 1) * DH)
        total = jnp.zeros((1, DH), F32)
        for h in range(HEADS_DEV):
            inv = 1.0 / acc[h, DH : DH + 1, qs]
            inv_l[h, :, qs] = inv
            a = (acc[h, 0:DH, qs] * inv).astype(BF16).astype(F32)
            at[h * DH : (h + 1) * DH, qs] = a
            total = total + jnp.sum(a, axis=0, keepdims=True)
        mean = total * (1.0 / COLS)
        centred = at[:, qs] - mean
        scaled = gt[:, qs] * gc[...]
        st[0, i : i + 1, 0:128] = mean
        st[0, i : i + 1, 128:256] = jnp.sum(centred * centred, axis=0, keepdims=True)
        st[0, i : i + 1, 256:384] = jnp.sum(scaled, axis=0, keepdims=True)
        st[0, i : i + 1, 384:512] = jnp.sum(scaled * centred, axis=0, keepdims=True)

    def st_copy(d):
        return pltpu.make_async_remote_copy(
            src_ref=st.at[0],
            dst_ref=st.at[d],
            send_sem=st_ss.at[d],
            recv_sem=st_rs.at[d],
            device_id=(me, lax.rem(col + d, N_HEAD)),
            device_id_type=MESH,
        )

    for d in range(1, N_HEAD):
        st_copy(d).start()
    for d in range(1, N_HEAD):
        st_copy(d).wait()

    mean = st[0, :, 0:128]
    for d in range(1, N_HEAD):
        mean = mean + st[d, :, 0:128]
    mean = mean * (1.0 / N_HEAD)
    square = jnp.zeros((8, DH), F32)
    plain = jnp.zeros((8, DH), F32)
    cross = jnp.zeros((8, DH), F32)
    for d in range(N_HEAD):
        off = st[d, :, 0:128] - mean
        square = square + (st[d, :, 128:256] + COLS * (off * off))
        plain = plain + st[d, :, 256:384]
        cross = cross + (st[d, :, 384:512] + off * st[d, :, 256:384])
    inv_std = lax.rsqrt(square * (1.0 / WIDTH) + NORM_EPS)
    res[:, 0:128] = mean
    res[:, 128:256] = inv_std
    res[:, 256:384] = plain * (1.0 / WIDTH)
    res[:, 384:512] = inv_std * cross * (1.0 / WIDTH)

    gain_part = jnp.zeros((COLS, DH), F32)
    for i in range(TOK // DH):
        qs = slice(i * DH, (i + 1) * DH)
        inv_std = res[i : i + 1, 128:256]
        normed = (at[:, qs] - res[i : i + 1, 0:128]) * inv_std
        scaled = gt[:, qs] * gc[...]
        do = inv_std * (scaled - res[i : i + 1, 256:384] - normed * res[i : i + 1, 384:512])
        do = do.astype(BF16)
        dot_[:, qs] = do
        gain_part = gain_part + gt[:, qs] * normed
        both = do.astype(F32) * at[:, qs]
        for h in range(HEADS_DEV):
            delta[h, :, qs] = jnp.sum(both[h * DH : (h + 1) * DH], axis=0, keepdims=True)

    def back(h, qs, m, v, kt, p):
        factor = jnp.exp2((m - m_run[h, :, qs]) * coef) * inv_l[h, :, qs]
        do = (dot_[h * DH : (h + 1) * DH, qs].astype(F32) * factor).astype(BF16)
        dp = dot(v, do, 1, 0)
        ds = (p.astype(F32) * (dp - factor * delta[h, :, qs])).astype(BF16)
        dq = dot(kt, ds, 1, 0)
        dk = dot(ds, qa[h, qs, 0:DH], 1, 0)
        dv = dot(p, do, 1, 1)
        return dq, dk, dv

    dqt[...] = jnp.zeros_like(dqt)

    gsum[0] = jnp.broadcast_to(jnp.sum(jnp.transpose(gain_part), axis=0, keepdims=True), (8, COLS))

    def gg_copy(stage):
        return pltpu.make_async_remote_copy(
            src_ref=gsum.at[2 * stage],
            dst_ref=gsum.at[2 * stage + 1],
            send_sem=gg_ss.at[stage],
            recv_sem=gg_rs.at[stage],
            device_id=(flipped(me, 1 << stage), col),
            device_id_type=MESH,
        )

    def gg_end(stage):
        gg_copy(stage).wait()
        gsum[2 * stage + 2] = gsum[2 * stage] + gsum[2 * stage + 1]
        if stage < 3:
            gg_copy(stage + 1).start()

    gg_copy(0).start()

    @pl.loop(0, LEVELS * NCH)
    def _(t):
        level = lax.rem(t, 3)
        c = t // 3
        rows = pl.ds(pl.multiple_of(c * CHUNK, CHUNK), CHUNK)
        for h in range(HEADS_DEV):
            hs = slice(h * DH, (h + 1) * DH)
            v = kv_in[level, rows, COLS + h * DH : COLS + (h + 1) * DH]
            kt = kt_far[level, hs, rows]
            dk_sum = jnp.zeros((CHUNK, DH), F32)
            dv_sum = jnp.zeros((CHUNK, DH), F32)
            for j in range(TOK // TILE):
                qs = slice(j * TILE, (j + 1) * TILE)
                dq, dk, dv = back(h, qs, m_far[level, c, h, :, qs], v, kt, p_far[level, h, rows, qs])
                dqt[hs, qs] += dq
                dk_sum = dk_sum + dk
                dv_sum = dv_sum + dv
            blocks = pl.ds(c * (CHUNK // BLOCK), CHUNK // BLOCK)
            shape = (CHUNK // BLOCK, BLOCK, DH)
            gr_out[level, h, blocks, :, 0:DH] = (dk_sum * SCALE).astype(BF16).reshape(shape)
            gr_out[level, h, blocks, :, DH:] = dv_sum.astype(BF16).reshape(shape)
            if h == 0:
                pl.when(t == 0)(lambda: gg_end(0))
                pl.when(t == 1)(lambda: gg_end(2))
            else:
                pl.when(t == 0)(lambda: gg_end(1))
            for one in range(LEVELS):
                pl.when(level == one)(lambda one=one, h=h: gr_copy(one, c, h).start())

    for i in range(TOK // DH):
        qs = slice(i * DH, (i + 1) * DH)
        normed = (at[:, qs] - res[i : i + 1, 0:128]) * res[i : i + 1, 128:256]
        lo_ref[qs, :] = jnp.transpose(normed * gc[...]).astype(BF16)
    lo_copy = pltpu.make_async_copy(lo_ref, lo_hbm, io.at[0])
    lo_copy.start()

    @pl.loop(0, TOK // SEG)
    def _(t):
        keys = pl.ds(pl.multiple_of(t * SEG, SEG), SEG)
        blocks = pl.ds(t * (SEG // BLOCK), SEG // BLOCK)
        for h in range(HEADS_DEV):
            hs = slice(h * DH, (h + 1) * DH)
            v = v_ref[blocks, :, hs].reshape(SEG, DH)
            kt = kt_loc[hs, keys]
            dk_sum = jnp.zeros((SEG, DH), F32)
            dv_sum = jnp.zeros((SEG, DH), F32)
            for j in range(SEG // TILE):
                qs = pl.ds(pl.multiple_of(t * SEG + j * TILE, TILE), TILE)
                dq, dk, dv = back(h, qs, m_loc[h, :, qs], v, kt, p_loc[h, :, qs])
                dqt[hs, qs] += dq
                dk_sum = dk_sum + dk
                dv_sum = dv_sum + dv
            dkv[keys, hs] = dk_sum * SCALE
            dkv[keys, COLS + h * DH : COLS + (h + 1) * DH] = dv_sum

    for t in range(TOK // TILE):
        cols = slice(t * TILE, (t + 1) * TILE)
        dq_ref[cols, :] = jnp.transpose(dqt[:, cols] * SCALE).astype(BF16)
    dq_copy = pltpu.make_async_copy(dq_ref, dq_hbm, io.at[1])
    dq_copy.start()
    gg_end(3)
    gg_ref[...] = gsum[8, 0:1, :]

    for c in range(NCH):
        for h in range(HEADS_DEV):
            gr_copy(2, c, h).wait()

    @pl.loop(0, TOK // BLOCK)
    def _(b):
        slot = inv_slot[b]
        rows = pl.ds(pl.multiple_of(b * BLOCK, BLOCK), BLOCK)
        used = jnp.minimum(slot + 1, 1).astype(F32)
        for h in range(HEADS_DEV):
            part = gr_in2[h, jnp.maximum(slot, 0)].astype(F32) * used
            dkv[rows, h * DH : (h + 1) * DH] += part[:, 0:DH]
            dkv[rows, COLS + h * DH : COLS + (h + 1) * DH] += part[:, DH:]

    part_copy = pltpu.make_async_copy(dkv, part_hbm, io.at[2])
    part_copy.start()
    for c in range(NCH):
        for level in range(2):
            for h in range(HEADS_DEV):
                gr_copy(level, c, h).wait()
    lo_copy.wait()
    dq_copy.wait()
    part_copy.wait()


def finish(
    kept, lo_in, dq_in, part_in, gr_in, gg_in, lo_ref, dq_ref, dk_ref, dv_ref, gg_ref
):
    me = lax.axis_index("seq")
    step = pl.program_id(0)
    lo_ref[...] = lo_in[...]
    dq_ref[...] = dq_in[...]
    gg_ref[...] = gg_in[...]
    for i in range(TILE // BLOCK):
        rows = slice(i * BLOCK, (i + 1) * BLOCK)
        block = step * (TILE // BLOCK) + i
        total = part_in[rows, :]
        dk = [total[:, h * DH : (h + 1) * DH] for h in range(HEADS_DEV)]
        dv = [total[:, COLS + h * DH : COLS + (h + 1) * DH] for h in range(HEADS_DEV)]
        for level in range(2):
            found = jnp.int32(-1)
            for slot in range(KEEP):
                found = jnp.where(kept[level, slot, me] == block, jnp.int32(slot), found)
            used = jnp.minimum(found + 1, 1).astype(F32)
            for h in range(HEADS_DEV):
                part = gr_in[level, h, jnp.maximum(found, 0)].astype(F32) * used
                dk[h] = dk[h] + part[:, 0:DH]
                dv[h] = dv[h] + part[:, DH:]
        for h in range(HEADS_DEV):
            dk_ref[rows, h * DH : (h + 1) * DH] = dk[h].astype(BF16)
            dv_ref[rows, h * DH : (h + 1) * DH] = dv[h].astype(BF16)


def local(query_rows, key_rows, value_rows, norm_gain, grad_out, doc_lengths, kept_blocks):
    vmem = pl.BlockSpec(memory_space=pltpu.VMEM)
    smem = pl.BlockSpec(memory_space=pltpu.SMEM)
    hbm = pl.BlockSpec(memory_space=pl.ANY)
    rows = jax.ShapeDtypeStruct((TOK, COLS), BF16)
    dma = pltpu.SemaphoreType.DMA
    scratch = [
        pltpu.VMEM((TOK, COLS), BF16),
        pltpu.VMEM((TOK // BLOCK, BLOCK, COLS), BF16),
        pltpu.VMEM((TOK // BLOCK, BLOCK, COLS), BF16),
        pltpu.VMEM((1, COLS), F32),
        pltpu.VMEM((TOK, COLS), BF16),
        pltpu.VMEM((TOK, COLS), BF16),
        pltpu.VMEM((TOK, COLS), BF16),
        pltpu.VMEM((HEADS_DEV, TOK, 2 * DH), BF16),
        pltpu.VMEM((TOK, DH), BF16),
        pltpu.VMEM((LEVELS, KEPT, DH), BF16),
        pltpu.VMEM((LEVELS, KEPT, 2 * COLS), BF16),
        pltpu.VMEM((LEVELS, KEPT, 2 * COLS), BF16),
        pltpu.VMEM((LEVELS, HEADS_DEV, KEEP, BLOCK, 2 * DH), BF16),
        pltpu.VMEM((HEADS_DEV, KEEP, BLOCK, 2 * DH), BF16),
        pltpu.VMEM((COLS, TOK), BF16),
        pltpu.VMEM((HEADS_DEV, DH + 16, TOK), BF16),
        pltpu.VMEM((LEVELS, COLS, KEPT), BF16),
        pltpu.VMEM((LEVELS, HEADS_DEV, DH + 16, KEPT), BF16),
        pltpu.VMEM((HEADS_DEV, SEG, TOK), BF16),
        pltpu.VMEM((LEVELS, HEADS_DEV, KEPT, TOK), BF16),
        pltpu.VMEM((HEADS_DEV, 1, TOK), F32),
        pltpu.VMEM((HEADS_DEV, 1, TOK), F32),
        pltpu.VMEM((LEVELS, NCH, HEADS_DEV, 1, TOK), F32),
        pltpu.VMEM((HEADS_DEV, DH + 16, TOK), F32),
        pltpu.VMEM((HEADS_DEV, 1, TOK), F32),
        pltpu.VMEM((COLS, TOK), F32),
        pltpu.VMEM((COLS, TOK), F32),
        pltpu.VMEM((COLS, DH), F32),
        pltpu.VMEM((N_HEAD, 8, 512), F32),
        pltpu.VMEM((8, 512), F32),
        pltpu.VMEM((COLS, TOK), BF16),
        pltpu.VMEM((HEADS_DEV, 1, TOK), F32),
        pltpu.VMEM((COLS, TOK), F32),
        pltpu.VMEM((TOK, 2 * COLS), F32),
        pltpu.VMEM((9, 8, COLS), F32),
        pltpu.SMEM((TOK // BLOCK,), jnp.int32),
        dma((LEVELS, NCH)),
        dma((LEVELS, NCH)),
        dma((LEVELS, NCH, HEADS_DEV)),
        dma((LEVELS, NCH, HEADS_DEV)),
        dma((N_HEAD,)),
        dma((N_HEAD,)),
        dma((4,)),
        dma((4,)),
        dma((5,)),
    ]
    kept = jnp.transpose(kept_blocks, (1, 2, 0))
    gain_row = jax.ShapeDtypeStruct((1, COLS), F32)
    lo, dq, part, returned, gain = pl.pallas_call(
        kernel,
        out_shape=[
            rows,
            rows,
            jax.ShapeDtypeStruct((TOK, 2 * COLS), F32),
            jax.ShapeDtypeStruct((2, HEADS_DEV, KEEP, BLOCK, 2 * DH), BF16),
            gain_row,
        ],
        in_specs=[smem, smem] + [hbm] * 5,
        out_specs=[hbm] * 4 + [vmem],
        scratch_shapes=scratch,
        compiler_params=pltpu.CompilerParams(
            collective_id=0, has_side_effects=True, vmem_limit_bytes=56 * 1024 * 1024
        ),
        name="attention",
    )(
        kept,
        doc_lengths,
        query_rows,
        key_rows.reshape(TOK // BLOCK, BLOCK, COLS),
        value_rows.reshape(TOK // BLOCK, BLOCK, COLS),
        norm_gain.reshape(1, COLS),
        grad_out,
    )
    tile = pl.BlockSpec((TILE, COLS), lambda i: (i, 0))
    gain_spec = pl.BlockSpec((1, COLS), lambda i: (0, 0))
    lo, dq, dk, dv, gain = pl.pallas_call(
        finish,
        grid=(TOK // TILE,),
        out_shape=[rows, rows, rows, rows, gain_row],
        in_specs=[
            smem,
            tile,
            tile,
            pl.BlockSpec((TILE, 2 * COLS), lambda i: (i, 0)),
            pl.BlockSpec(returned.shape, lambda i: (0, 0, 0, 0, 0)),
            gain_spec,
        ],
        out_specs=[tile, tile, tile, tile, gain_spec],
        compiler_params=pltpu.CompilerParams(vmem_limit_bytes=60 * 1024 * 1024),
        name="finish",
    )(kept, lo, dq, part, returned, gain)
    return lo, dq, dk, dv, gain.reshape(COLS)


def solution(mesh):
    rows = P("seq", "head")
    in_specs = (rows, rows, rows, P("head"), rows, P(), P())
    out_specs = (rows, rows, rows, rows, P("head"))
    return jax.shard_map(local, mesh=mesh, in_specs=in_specs, out_specs=out_specs, check_vma=False)
```

```python
import functools

import jax
import jax.numpy as jnp
from jax import lax
from jax.experimental import pallas as pl
from jax.experimental.pallas import tpu as pltpu
from jax.sharding import PartitionSpec as P

DH = 128
TOK = 1024
SEG = 512
BLOCK = 64
KEEP = 8
LEVELS = 3
KEPT = KEEP * BLOCK
CHUNK = 256
NCH = KEPT // CHUNK
TILE = 256
WIDTH = 2048
HEADS_DEV = 2
COLS = HEADS_DEV * DH
N_SEQ = 16
N_HEAD = 8
NORM_EPS = 1e-05
SCALE = DH**-0.5
LOG2E = 1.4426950408889634
BIG = 2.0**100
LOW = -(2.0**99)
MESH = pl.DeviceIdType.MESH
F32 = jnp.float32
BF16 = jnp.bfloat16


def dot(a, b, ca, cb):
    return lax.dot_general(a, b, (((ca,), (cb,)), ((), ())), preferred_element_type=F32)


def turned(x):
    return jnp.transpose(x.astype(F32)).astype(x.dtype)


def flipped(index, bit):
    return index + bit * (1 - 2 * lax.rem(index // bit, 2))


def level_bit(level):
    return 1 + level + level // 2


def kernel(
    kept_hbm,
    lengths,
    q_hbm,
    k_hbm,
    v_hbm,
    gain_hbm,
    g_hbm,
    lo_hbm,
    dq_hbm,
    part_hbm,
    gr_hbm,
    gg_ref,
    kept,
    q_ref,
    k_ref,
    v_ref,
    gain_ref,
    g_ref,
    lo_ref,
    dq_ref,
    qa,
    mk_loc,
    mk_far,
    kv_out,
    kv_in,
    gr_out,
    gr_in2,
    kt_loc,
    vt_loc,
    kt_far,
    vt_far,
    p_loc,
    p_far,
    m_run,
    m_loc,
    m_far,
    acc,
    inv_l,
    at,
    gt,
    gc,
    st,
    res,
    dot_,
    delta,
    dqt,
    dkv,
    gsum,
    inv_slot,
    kv_ss,
    kv_rs,
    gr_ss,
    gr_rs,
    st_ss,
    st_rs,
    gg_ss,
    gg_rs,
    io,
):
    me = lax.axis_index("seq")
    col = lax.axis_index("head")

    barrier = pltpu.get_barrier_semaphore()
    for bit in (1, 2, 4, 8):
        pl.semaphore_signal(barrier, inc=1, device_id=(flipped(me, bit), col), device_id_type=MESH)
    for d in range(1, N_HEAD):
        pl.semaphore_signal(
            barrier, inc=1, device_id=(me, lax.rem(col + d, N_HEAD)), device_id_type=MESH
        )

    loads = [
        pltpu.make_async_copy(src, dst, io.at[i])
        for i, (src, dst) in enumerate(
            (
                (k_hbm, k_ref),
                (v_hbm, v_ref),
                (kept_hbm, kept),
                (q_hbm, q_ref),
                (g_hbm, g_ref),
                (gain_hbm, gain_ref),
            )
        )
    ]
    for load in loads:
        load.start()
    for load in loads[:3]:
        load.wait()

    for level in range(LEVELS):
        for slot in range(KEEP):
            block = jnp.maximum(kept[level, slot, me], 0)
            kv_out[level, slot * BLOCK : (slot + 1) * BLOCK, 0:COLS] = k_ref[block]
            kv_out[level, slot * BLOCK : (slot + 1) * BLOCK, COLS:] = v_ref[block]
    pl.semaphore_wait(barrier, 4 + N_HEAD - 1)

    def kv_copy(level, c):
        rows = pl.ds(pl.multiple_of(c * CHUNK, CHUNK), CHUNK)
        return pltpu.make_async_remote_copy(
            src_ref=kv_out.at[level, rows],
            dst_ref=kv_in.at[level, rows],
            send_sem=kv_ss.at[level, c],
            recv_sem=kv_rs.at[level, c],
            device_id=(flipped(me, level_bit(level)), col),
            device_id_type=MESH,
        )

    def gr_copy(level, c, h):
        blocks = pl.ds(c * (CHUNK // BLOCK), CHUNK // BLOCK)
        dst = gr_in2 if level == 2 else gr_hbm.at[level]
        return pltpu.make_async_remote_copy(
            src_ref=gr_out.at[level, h, blocks],
            dst_ref=dst.at[h, blocks],
            send_sem=gr_ss.at[level, c, h],
            recv_sem=gr_rs.at[level, c, h],
            device_id=(flipped(me, level_bit(level)), col),
            device_id_type=MESH,
        )

    for c in range(NCH):
        for level in (2, 0, 1):
            kv_copy(level, c).start()

    for load in loads[3:]:
        load.wait()
    start1 = lengths[0]
    start2 = lengths[0] + lengths[1]

    def doc_of(pos):
        return (pos >= start1).astype(jnp.int32) + (pos >= start2).astype(jnp.int32)

    lane = lax.broadcasted_iota(jnp.int32, (BLOCK, DH), 1)
    row = lax.broadcasted_iota(jnp.int32, (BLOCK, DH), 0)
    for b in range(TOK // BLOCK):
        rows = slice(b * BLOCK, (b + 1) * BLOCK)
        docs = doc_of(me * TOK + b * BLOCK + row)
        same = docs == lane
        mq = jnp.where(same, 1.0, 0.0).astype(BF16)
        mk_loc[rows, :] = jnp.where(same | (lane >= 3), 0.0, -BIG).astype(BF16)
        for h in range(HEADS_DEV):
            qa[h, rows, DH:] = mq
            qa[h, rows, 0:DH] = q_ref[rows, h * DH : (h + 1) * DH]
    for level in range(LEVELS):
        partner = flipped(me, level_bit(level))
        for slot in range(KEEP):
            listed = kept[level, slot, partner]
            docs = doc_of(partner * TOK + jnp.maximum(listed, 0) * BLOCK + row)
            docs = docs - 3 * jnp.minimum(listed, 0)
            same = docs == lane
            mk_far[level, slot * BLOCK : (slot + 1) * BLOCK, :] = jnp.where(
                same | (lane >= 3), 0.0, -BIG
            ).astype(BF16)

    ones = jnp.ones((16, TOK), BF16)
    for h in range(HEADS_DEV):
        vt_loc[h, DH:, :] = ones
        for level in range(LEVELS):
            vt_far[level, h, DH:, :] = ones[:, 0:KEPT]

    for t in range(TOK // TILE):
        cols = slice(t * TILE, (t + 1) * TILE)
        blocks = slice(t * (TILE // BLOCK), (t + 1) * (TILE // BLOCK))
        kt_loc[:, cols] = turned(k_ref[blocks].reshape(TILE, COLS))
        vt = turned(v_ref[blocks].reshape(TILE, COLS))
        for h in range(HEADS_DEV):
            vt_loc[h, 0:DH, cols] = vt[h * DH : (h + 1) * DH]

    coef = SCALE * LOG2E

    @pl.loop(0, TOK // SEG)
    def _(t):
        keys = pl.ds(pl.multiple_of(t * SEG, SEG), SEG)
        blocks = pl.ds(t * (SEG // BLOCK), SEG // BLOCK)
        for h in range(HEADS_DEV):
            k = k_ref[blocks, :, h * DH : (h + 1) * DH].reshape(SEG, DH)
            ka = jnp.concatenate([k, mk_loc[keys, :]], axis=1)
            vt = vt_loc[h, :, keys]
            for j in range(SEG // TILE):
                qs = pl.ds(pl.multiple_of(t * SEG + j * TILE, TILE), TILE)
                s = dot(ka, qa[h, qs, :], 1, 1)
                m = jnp.maximum(jnp.max(s, axis=0, keepdims=True), LOW)
                p = jnp.exp2((s - m) * coef).astype(BF16)
                p_loc[h, :, qs] = p
                m_run[h, :, qs] = m
                m_loc[h, :, qs] = m
                acc[h, :, qs] = dot(vt, p, 1, 0)

    gc[...] = jnp.transpose(jnp.broadcast_to(gain_ref[...], (DH, COLS)))
    for t in range(TOK // TILE):
        cols = slice(t * TILE, (t + 1) * TILE)
        gt[:, cols] = jnp.transpose(g_ref[cols, :].astype(F32))

    @pl.loop(0, TOK // BLOCK)
    def _(b):
        found = jnp.int32(-1)
        for slot in range(KEEP):
            off = kept[2, slot, me] - b
            found = jnp.maximum(found, (slot + 1) * (1 - jnp.minimum(off * off, 1)) - 1)
        inv_slot[b] = found

    @pl.loop(0, LEVELS * NCH)
    def _(t):
        level = lax.rem(t + 2, 3)
        c = t // 3
        kv_copy(level, c).wait()
        rows = pl.ds(pl.multiple_of(c * CHUNK, CHUNK), CHUNK)
        kt_far[level, :, rows] = turned(kv_in[level, rows, 0:COLS])
        vt = turned(kv_in[level, rows, COLS:])
        for h in range(HEADS_DEV):
            vt_far[level, h, 0:DH, rows] = vt[h * DH : (h + 1) * DH]
        for h in range(HEADS_DEV):
            ka = jnp.concatenate(
                [kv_in[level, rows, h * DH : (h + 1) * DH], mk_far[level, rows, :]], axis=1
            )
            vta = vt_far[level, h, :, rows]
            for j in range(TOK // TILE):
                qs = slice(j * TILE, (j + 1) * TILE)
                s = dot(ka, qa[h, qs, :], 1, 1)
                m_old = m_run[h, :, qs]
                m = jnp.maximum(jnp.max(s, axis=0, keepdims=True), m_old)
                p = jnp.exp2((s - m) * coef).astype(BF16)
                p_far[level, h, rows, qs] = p
                m_run[h, :, qs] = m
                m_far[level, c, h, :, qs] = m
                acc[h, :, qs] = acc[h, :, qs] * jnp.exp2((m_old - m) * coef) + dot(vta, p, 1, 0)

    for i in range(TOK // DH):
        qs = slice(i * DH, (i + 1) * DH)
        total = jnp.zeros((1, DH), F32)
        for h in range(HEADS_DEV):
            inv = 1.0 / acc[h, DH : DH + 1, qs]
            inv_l[h, :, qs] = inv
            a = (acc[h, 0:DH, qs] * inv).astype(BF16).astype(F32)
            at[h * DH : (h + 1) * DH, qs] = a
            total = total + jnp.sum(a, axis=0, keepdims=True)
        mean = total * (1.0 / COLS)
        centred = at[:, qs] - mean
        scaled = gt[:, qs] * gc[...]
        st[0, i : i + 1, 0:128] = mean
        st[0, i : i + 1, 128:256] = jnp.sum(centred * centred, axis=0, keepdims=True)
        st[0, i : i + 1, 256:384] = jnp.sum(scaled, axis=0, keepdims=True)
        st[0, i : i + 1, 384:512] = jnp.sum(scaled * centred, axis=0, keepdims=True)

    def st_copy(d):
        return pltpu.make_async_remote_copy(
            src_ref=st.at[0],
            dst_ref=st.at[d],
            send_sem=st_ss.at[d],
            recv_sem=st_rs.at[d],
            device_id=(me, lax.rem(col + d, N_HEAD)),
            device_id_type=MESH,
        )

    for d in range(1, N_HEAD):
        st_copy(d).start()
    for d in range(1, N_HEAD):
        st_copy(d).wait()

    mean = st[0, :, 0:128]
    for d in range(1, N_HEAD):
        mean = mean + st[d, :, 0:128]
    mean = mean * (1.0 / N_HEAD)
    square = jnp.zeros((8, DH), F32)
    plain = jnp.zeros((8, DH), F32)
    cross = jnp.zeros((8, DH), F32)
    for d in range(N_HEAD):
        off = st[d, :, 0:128] - mean
        square = square + (st[d, :, 128:256] + COLS * (off * off))
        plain = plain + st[d, :, 256:384]
        cross = cross + (st[d, :, 384:512] + off * st[d, :, 256:384])
    inv_std = lax.rsqrt(square * (1.0 / WIDTH) + NORM_EPS)
    res[:, 0:128] = mean
    res[:, 128:256] = inv_std
    res[:, 256:384] = plain * (1.0 / WIDTH)
    res[:, 384:512] = inv_std * cross * (1.0 / WIDTH)

    gain_part = jnp.zeros((COLS, DH), F32)
    for i in range(TOK // DH):
        qs = slice(i * DH, (i + 1) * DH)
        inv_std = res[i : i + 1, 128:256]
        normed = (at[:, qs] - res[i : i + 1, 0:128]) * inv_std
        scaled = gt[:, qs] * gc[...]
        do = inv_std * (scaled - res[i : i + 1, 256:384] - normed * res[i : i + 1, 384:512])
        do = do.astype(BF16)
        dot_[:, qs] = do
        gain_part = gain_part + gt[:, qs] * normed
        both = do.astype(F32) * at[:, qs]
        for h in range(HEADS_DEV):
            delta[h, :, qs] = jnp.sum(both[h * DH : (h + 1) * DH], axis=0, keepdims=True)

    def back(h, qs, m, v, kt, p):
        factor = jnp.exp2((m - m_run[h, :, qs]) * coef) * inv_l[h, :, qs]
        do = (dot_[h * DH : (h + 1) * DH, qs].astype(F32) * factor).astype(BF16)
        dp = dot(v, do, 1, 0)
        ds = (p.astype(F32) * (dp - factor * delta[h, :, qs])).astype(BF16)
        dq = dot(kt, ds, 1, 0)
        dk = dot(ds, qa[h, qs, 0:DH], 1, 0)
        dv = dot(p, do, 1, 1)
        return dq, dk, dv

    dqt[...] = jnp.zeros_like(dqt)

    gsum[0] = jnp.broadcast_to(jnp.sum(jnp.transpose(gain_part), axis=0, keepdims=True), (8, COLS))

    def gg_copy(stage):
        return pltpu.make_async_remote_copy(
            src_ref=gsum.at[2 * stage],
            dst_ref=gsum.at[2 * stage + 1],
            send_sem=gg_ss.at[stage],
            recv_sem=gg_rs.at[stage],
            device_id=(flipped(me, 1 << stage), col),
            device_id_type=MESH,
        )

    def gg_end(stage):
        gg_copy(stage).wait()
        gsum[2 * stage + 2] = gsum[2 * stage] + gsum[2 * stage + 1]
        if stage < 3:
            gg_copy(stage + 1).start()

    gg_copy(0).start()

    @pl.loop(0, LEVELS * NCH)
    def _(t):
        level = lax.rem(t, 3)
        c = t // 3
        rows = pl.ds(pl.multiple_of(c * CHUNK, CHUNK), CHUNK)
        for h in range(HEADS_DEV):
            hs = slice(h * DH, (h + 1) * DH)
            v = kv_in[level, rows, COLS + h * DH : COLS + (h + 1) * DH]
            kt = kt_far[level, hs, rows]
            dk_sum = jnp.zeros((CHUNK, DH), F32)
            dv_sum = jnp.zeros((CHUNK, DH), F32)
            for j in range(TOK // TILE):
                qs = slice(j * TILE, (j + 1) * TILE)
                dq, dk, dv = back(h, qs, m_far[level, c, h, :, qs], v, kt, p_far[level, h, rows, qs])
                dqt[hs, qs] += dq
                dk_sum = dk_sum + dk
                dv_sum = dv_sum + dv
            blocks = pl.ds(c * (CHUNK // BLOCK), CHUNK // BLOCK)
            shape = (CHUNK // BLOCK, BLOCK, DH)
            gr_out[level, h, blocks, :, 0:DH] = (dk_sum * SCALE).astype(BF16).reshape(shape)
            gr_out[level, h, blocks, :, DH:] = dv_sum.astype(BF16).reshape(shape)
            if h == 0:
                pl.when(t == 0)(lambda: gg_end(0))
                pl.when(t == 1)(lambda: gg_end(2))
            else:
                pl.when(t == 0)(lambda: gg_end(1))
            for one in range(LEVELS):
                pl.when(level == one)(lambda one=one, h=h: gr_copy(one, c, h).start())

    for i in range(TOK // DH):
        qs = slice(i * DH, (i + 1) * DH)
        normed = (at[:, qs] - res[i : i + 1, 0:128]) * res[i : i + 1, 128:256]
        lo_ref[qs, :] = jnp.transpose(normed * gc[...]).astype(BF16)
    lo_copy = pltpu.make_async_copy(lo_ref, lo_hbm, io.at[0])
    lo_copy.start()

    @pl.loop(0, TOK // SEG)
    def _(t):
        keys = pl.ds(pl.multiple_of(t * SEG, SEG), SEG)
        blocks = pl.ds(t * (SEG // BLOCK), SEG // BLOCK)
        for h in range(HEADS_DEV):
            hs = slice(h * DH, (h + 1) * DH)
            v = v_ref[blocks, :, hs].reshape(SEG, DH)
            kt = kt_loc[hs, keys]
            dk_sum = jnp.zeros((SEG, DH), F32)
            dv_sum = jnp.zeros((SEG, DH), F32)
            for j in range(SEG // TILE):
                qs = pl.ds(pl.multiple_of(t * SEG + j * TILE, TILE), TILE)
                dq, dk, dv = back(h, qs, m_loc[h, :, qs], v, kt, p_loc[h, :, qs])
                dqt[hs, qs] += dq
                dk_sum = dk_sum + dk
                dv_sum = dv_sum + dv
            dkv[keys, hs] = dk_sum * SCALE
            dkv[keys, COLS + h * DH : COLS + (h + 1) * DH] = dv_sum

    for t in range(TOK // TILE):
        cols = slice(t * TILE, (t + 1) * TILE)
        dq_ref[cols, :] = jnp.transpose(dqt[:, cols] * SCALE).astype(BF16)
    dq_copy = pltpu.make_async_copy(dq_ref, dq_hbm, io.at[1])
    dq_copy.start()
    gg_end(3)
    gg_ref[...] = gsum[8, 0:1, :]

    for c in range(NCH):
        for h in range(HEADS_DEV):
            gr_copy(2, c, h).wait()

    @pl.loop(0, TOK // BLOCK)
    def _(b):
        slot = inv_slot[b]
        rows = pl.ds(pl.multiple_of(b * BLOCK, BLOCK), BLOCK)
        used = jnp.minimum(slot + 1, 1).astype(F32)
        for h in range(HEADS_DEV):
            part = gr_in2[h, jnp.maximum(slot, 0)].astype(F32) * used
            dkv[rows, h * DH : (h + 1) * DH] += part[:, 0:DH]
            dkv[rows, COLS + h * DH : COLS + (h + 1) * DH] += part[:, DH:]

    part_copy = pltpu.make_async_copy(dkv, part_hbm, io.at[2])
    part_copy.start()
    for c in range(NCH):
        for level in range(2):
            for h in range(HEADS_DEV):
                gr_copy(level, c, h).wait()
    lo_copy.wait()
    dq_copy.wait()
    part_copy.wait()


def finish(
    kept, lo_in, dq_in, part_in, gr_in, gg_in, lo_ref, dq_ref, dk_ref, dv_ref, gg_ref, dk, dv, sems
):
    me = lax.axis_index("seq")
    gg_ref[...] = gg_in[...]
    copies = []

    def send(src, dst, i, lane):
        rows = pl.ds(i * TILE, TILE)
        copy = pltpu.make_async_copy(src.at[rows], dst.at[rows], sems.at[lane, i])
        copy.start()
        copies.append(copy)

    for i in range(TOK // TILE):
        send(lo_in, lo_ref, i, 0)
        send(dq_in, dq_ref, i, 1)
    for i in range(TOK // TILE):
        for b in range(i * (TILE // BLOCK), (i + 1) * (TILE // BLOCK)):
            rows = slice(b * BLOCK, (b + 1) * BLOCK)
            total = part_in[rows, :]
            key = [total[:, h * DH : (h + 1) * DH] for h in range(HEADS_DEV)]
            value = [total[:, COLS + h * DH : COLS + (h + 1) * DH] for h in range(HEADS_DEV)]
            for level in range(2):
                found = jnp.int32(-1)
                for slot in range(KEEP):
                    found = jnp.where(kept[level, slot, me] == b, jnp.int32(slot), found)
                used = jnp.minimum(found + 1, 1).astype(F32)
                for h in range(HEADS_DEV):
                    part = gr_in[level, h, jnp.maximum(found, 0)].astype(F32) * used
                    key[h] = key[h] + part[:, 0:DH]
                    value[h] = value[h] + part[:, DH:]
            for h in range(HEADS_DEV):
                dk[rows, h * DH : (h + 1) * DH] = key[h].astype(BF16)
                dv[rows, h * DH : (h + 1) * DH] = value[h].astype(BF16)
        send(dk, dk_ref, i, 2)
        send(dv, dv_ref, i, 3)
    for copy in copies:
        copy.wait()


def local(query_rows, key_rows, value_rows, norm_gain, grad_out, doc_lengths, kept_blocks):
    vmem = pl.BlockSpec(memory_space=pltpu.VMEM)
    smem = pl.BlockSpec(memory_space=pltpu.SMEM)
    hbm = pl.BlockSpec(memory_space=pltpu.HBM)
    some = pl.BlockSpec(memory_space=pl.ANY)
    rows = jax.ShapeDtypeStruct((TOK, COLS), BF16)
    dma = pltpu.SemaphoreType.DMA
    scratch = [
        pltpu.SMEM((LEVELS, KEEP, N_SEQ), jnp.int32),
        pltpu.VMEM((TOK, COLS), BF16),
        pltpu.VMEM((TOK // BLOCK, BLOCK, COLS), BF16),
        pltpu.VMEM((TOK // BLOCK, BLOCK, COLS), BF16),
        pltpu.VMEM((1, COLS), F32),
        pltpu.VMEM((TOK, COLS), BF16),
        pltpu.VMEM((TOK, COLS), BF16),
        pltpu.VMEM((TOK, COLS), BF16),
        pltpu.VMEM((HEADS_DEV, TOK, 2 * DH), BF16),
        pltpu.VMEM((TOK, DH), BF16),
        pltpu.VMEM((LEVELS, KEPT, DH), BF16),
        pltpu.VMEM((LEVELS, KEPT, 2 * COLS), BF16),
        pltpu.VMEM((LEVELS, KEPT, 2 * COLS), BF16),
        pltpu.VMEM((LEVELS, HEADS_DEV, KEEP, BLOCK, 2 * DH), BF16),
        pltpu.VMEM((HEADS_DEV, KEEP, BLOCK, 2 * DH), BF16),
        pltpu.VMEM((COLS, TOK), BF16),
        pltpu.VMEM((HEADS_DEV, DH + 16, TOK), BF16),
        pltpu.VMEM((LEVELS, COLS, KEPT), BF16),
        pltpu.VMEM((LEVELS, HEADS_DEV, DH + 16, KEPT), BF16),
        pltpu.VMEM((HEADS_DEV, SEG, TOK), BF16),
        pltpu.VMEM((LEVELS, HEADS_DEV, KEPT, TOK), BF16),
        pltpu.VMEM((HEADS_DEV, 1, TOK), F32),
        pltpu.VMEM((HEADS_DEV, 1, TOK), F32),
        pltpu.VMEM((LEVELS, NCH, HEADS_DEV, 1, TOK), F32),
        pltpu.VMEM((HEADS_DEV, DH + 16, TOK), F32),
        pltpu.VMEM((HEADS_DEV, 1, TOK), F32),
        pltpu.VMEM((COLS, TOK), F32),
        pltpu.VMEM((COLS, TOK), F32),
        pltpu.VMEM((COLS, DH), F32),
        pltpu.VMEM((N_HEAD, 8, 512), F32),
        pltpu.VMEM((8, 512), F32),
        pltpu.VMEM((COLS, TOK), BF16),
        pltpu.VMEM((HEADS_DEV, 1, TOK), F32),
        pltpu.VMEM((COLS, TOK), F32),
        pltpu.VMEM((TOK, 2 * COLS), F32),
        pltpu.VMEM((9, 8, COLS), F32),
        pltpu.SMEM((TOK // BLOCK,), jnp.int32),
        dma((LEVELS, NCH)),
        dma((LEVELS, NCH)),
        dma((LEVELS, NCH, HEADS_DEV)),
        dma((LEVELS, NCH, HEADS_DEV)),
        dma((N_HEAD,)),
        dma((N_HEAD,)),
        dma((4,)),
        dma((4,)),
        dma((6,)),
    ]
    kept = jnp.transpose(kept_blocks, (1, 2, 0))
    gain_row = jax.ShapeDtypeStruct((1, COLS), F32)
    lo, dq, part, returned, gain = pl.pallas_call(
        kernel,
        out_shape=[
            pltpu.VMEM((TOK, COLS), BF16),
            pltpu.VMEM((TOK, COLS), BF16),
            pltpu.VMEM((TOK, 2 * COLS), F32),
            pltpu.VMEM((2, HEADS_DEV, KEEP, BLOCK, 2 * DH), BF16),
            pltpu.VMEM((1, COLS), F32),
        ],
        in_specs=[hbm, smem] + [hbm] * 5,
        out_specs=[some] * 4 + [vmem],
        scratch_shapes=scratch,
        compiler_params=pltpu.CompilerParams(
            collective_id=0, has_side_effects=True, vmem_limit_bytes=44 * 1024 * 1024
        ),
        name="attention",
    )(
        *(
            pltpu.with_memory_space_constraint(x, pltpu.HBM)
            for x in (
                kept,
                doc_lengths,
                query_rows,
                key_rows.reshape(TOK // BLOCK, BLOCK, COLS),
                value_rows.reshape(TOK // BLOCK, BLOCK, COLS),
                norm_gain.reshape(1, COLS),
                grad_out,
            )
        )
    )
    lo, dq, dk, dv, gain = pl.pallas_call(
        finish,
        out_shape=[rows, rows, rows, rows, gain_row],
        in_specs=[smem] + [vmem] * 5,
        out_specs=[hbm] * 4 + [vmem],
        scratch_shapes=[
            pltpu.VMEM((TOK, COLS), BF16),
            pltpu.VMEM((TOK, COLS), BF16),
            dma((4, TOK // TILE)),
        ],
        compiler_params=pltpu.CompilerParams(vmem_limit_bytes=12 * 1024 * 1024),
        name="finish",
    )(pltpu.with_memory_space_constraint(kept, pltpu.HBM), lo, dq, part, returned, gain)
    return lo, dq, dk, dv, gain.reshape(COLS)


def solution(mesh):
    rows = P("seq", "head")
    in_specs = (rows, rows, rows, P("head"), rows, P(), P())
    out_specs = (rows, rows, rows, rows, P("head"))
    return jax.shard_map(local, mesh=mesh, in_specs=in_specs, out_specs=out_specs, check_vma=False)
```

```python
import functools

import jax
import jax.numpy as jnp
from jax import lax
from jax.experimental import pallas as pl
from jax.experimental.pallas import tpu as pltpu
from jax.sharding import PartitionSpec as P

DH = 128
TOK = 1024
SEG = 512
BLOCK = 64
KEEP = 8
LEVELS = 3
KEPT = KEEP * BLOCK
CHUNK = 256
NCH = KEPT // CHUNK
TILE = 256
WIDTH = 2048
HEADS_DEV = 2
COLS = HEADS_DEV * DH
N_SEQ = 16
N_HEAD = 8
NORM_EPS = 1e-05
SCALE = DH**-0.5
LOG2E = 1.4426950408889634
BIG = 2.0**100
LOW = -(2.0**99)
MESH = pl.DeviceIdType.MESH
F32 = jnp.float32
BF16 = jnp.bfloat16


def dot(a, b, ca, cb):
    return lax.dot_general(a, b, (((ca,), (cb,)), ((), ())), preferred_element_type=F32)


def turned(x):
    return jnp.transpose(x.astype(F32)).astype(x.dtype)


def flipped(index, bit):
    return index + bit * (1 - 2 * lax.rem(index // bit, 2))


def level_bit(level):
    return 1 + level + level // 2


def kernel(
    kept_hbm,
    lengths,
    q_hbm,
    k_hbm,
    v_hbm,
    gain_hbm,
    g_hbm,
    lo_hbm,
    dq_hbm,
    part_hbm,
    gr_hbm,
    gg_ref,
    kept,
    q_ref,
    k_ref,
    v_ref,
    gain_ref,
    g_ref,
    lo_ref,
    dq_ref,
    qa,
    mk_loc,
    mk_far,
    kv_out,
    kv_in,
    gr_out,
    gr_in2,
    kt_loc,
    vt_loc,
    kt_far,
    vt_far,
    p_loc,
    p_far,
    m_run,
    m_loc,
    m_far,
    acc,
    inv_l,
    at,
    gt,
    gc,
    st,
    early,
    res,
    dot_,
    delta,
    dqt,
    dkv,
    gsum,
    inv_slot,
    kv_ss,
    kv_rs,
    gr_ss,
    gr_rs,
    st_ss,
    st_rs,
    gg_ss,
    gg_rs,
    io,
):
    me = lax.axis_index("seq")
    col = lax.axis_index("head")

    barrier = pltpu.get_barrier_semaphore()
    for bit in (1, 2, 4, 8):
        pl.semaphore_signal(barrier, inc=1, device_id=(flipped(me, bit), col), device_id_type=MESH)
    for d in range(1, N_HEAD):
        pl.semaphore_signal(
            barrier, inc=1, device_id=(me, lax.rem(col + d, N_HEAD)), device_id_type=MESH
        )

    def load(src, dst, pieces, first):
        size = src.shape[0] // pieces
        copies = []
        for i in range(pieces):
            rows = pl.ds(i * size, size)
            copies.append(pltpu.make_async_copy(src.at[rows], dst.at[rows], io.at[first + i]))
            copies[-1].start()
        return copies

    loads = load(k_hbm, k_ref, 4, 0) + load(v_hbm, v_ref, 4, 4) + load(kept_hbm, kept, 1, 8)
    later = load(q_hbm, q_ref, 4, 9) + load(g_hbm, g_ref, 4, 13) + load(gain_hbm, gain_ref, 1, 17)
    for copy in loads:
        copy.wait()

    for level in range(LEVELS):
        for slot in range(KEEP):
            block = jnp.maximum(kept[level, slot, me], 0)
            kv_out[level, slot * BLOCK : (slot + 1) * BLOCK, 0:COLS] = k_ref[block]
            kv_out[level, slot * BLOCK : (slot + 1) * BLOCK, COLS:] = v_ref[block]
    pl.semaphore_wait(barrier, 4 + N_HEAD - 1)

    def kv_copy(level, c):
        rows = pl.ds(pl.multiple_of(c * CHUNK, CHUNK), CHUNK)
        return pltpu.make_async_remote_copy(
            src_ref=kv_out.at[level, rows],
            dst_ref=kv_in.at[level, rows],
            send_sem=kv_ss.at[level, c],
            recv_sem=kv_rs.at[level, c],
            device_id=(flipped(me, level_bit(level)), col),
            device_id_type=MESH,
        )

    def gr_copy(level, h):
        dst = gr_in2 if level == 2 else gr_hbm.at[level]
        return pltpu.make_async_remote_copy(
            src_ref=gr_out.at[level, h],
            dst_ref=dst.at[h],
            send_sem=gr_ss.at[level, h],
            recv_sem=gr_rs.at[level, h],
            device_id=(flipped(me, level_bit(level)), col),
            device_id_type=MESH,
        )

    for c in range(NCH):
        for level in (1, 0, 2):
            kv_copy(level, c).start()

    for copy in later:
        copy.wait()
    start1 = lengths[0]
    start2 = lengths[0] + lengths[1]

    def doc_of(pos):
        return (pos >= start1).astype(jnp.int32) + (pos >= start2).astype(jnp.int32)

    lane = lax.broadcasted_iota(jnp.int32, (BLOCK, DH), 1)
    row = lax.broadcasted_iota(jnp.int32, (BLOCK, DH), 0)
    for b in range(TOK // BLOCK):
        rows = slice(b * BLOCK, (b + 1) * BLOCK)
        docs = doc_of(me * TOK + b * BLOCK + row)
        same = docs == lane
        mq = jnp.where(same, 1.0, 0.0).astype(BF16)
        mk_loc[rows, :] = jnp.where(same | (lane >= 3), 0.0, -BIG).astype(BF16)
        for h in range(HEADS_DEV):
            qa[h, rows, DH:] = mq
            qa[h, rows, 0:DH] = q_ref[rows, h * DH : (h + 1) * DH]
    for level in range(LEVELS):
        partner = flipped(me, level_bit(level))
        for slot in range(KEEP):
            listed = kept[level, slot, partner]
            docs = doc_of(partner * TOK + jnp.maximum(listed, 0) * BLOCK + row)
            docs = docs - 3 * jnp.minimum(listed, 0)
            same = docs == lane
            mk_far[level, slot * BLOCK : (slot + 1) * BLOCK, :] = jnp.where(
                same | (lane >= 3), 0.0, -BIG
            ).astype(BF16)

    ones = jnp.ones((16, TOK), BF16)
    for h in range(HEADS_DEV):
        vt_loc[h, DH:, :] = ones
        for level in range(LEVELS):
            vt_far[level, h, DH:, :] = ones[:, 0:KEPT]

    for t in range(TOK // TILE):
        cols = slice(t * TILE, (t + 1) * TILE)
        blocks = slice(t * (TILE // BLOCK), (t + 1) * (TILE // BLOCK))
        kt_loc[:, cols] = turned(k_ref[blocks].reshape(TILE, COLS))
        vt = turned(v_ref[blocks].reshape(TILE, COLS))
        for h in range(HEADS_DEV):
            vt_loc[h, 0:DH, cols] = vt[h * DH : (h + 1) * DH]

    coef = SCALE * LOG2E

    @pl.loop(0, TOK // SEG)
    def _(t):
        keys = pl.ds(pl.multiple_of(t * SEG, SEG), SEG)
        blocks = pl.ds(t * (SEG // BLOCK), SEG // BLOCK)
        for h in range(HEADS_DEV):
            k = k_ref[blocks, :, h * DH : (h + 1) * DH].reshape(SEG, DH)
            ka = jnp.concatenate([k, mk_loc[keys, :]], axis=1)
            vt = vt_loc[h, :, keys]
            for j in range(SEG // TILE):
                qs = pl.ds(pl.multiple_of(t * SEG + j * TILE, TILE), TILE)
                s = dot(ka, qa[h, qs, :], 1, 1)
                m = jnp.maximum(jnp.max(s, axis=0, keepdims=True), LOW)
                p = jnp.exp2((s - m) * coef).astype(BF16)
                p_loc[h, :, qs] = p
                m_run[h, :, qs] = m
                m_loc[h, :, qs] = m
                acc[h, :, qs] = dot(vt, p, 1, 0)

    gc[...] = jnp.transpose(jnp.broadcast_to(gain_ref[...], (DH, COLS)))
    for t in range(TOK // TILE):
        cols = slice(t * TILE, (t + 1) * TILE)
        gt[:, cols] = jnp.transpose(g_ref[cols, :].astype(F32))

    for i in range(TOK // DH):
        scaled = gt[:, i * DH : (i + 1) * DH] * gc[...]
        early[0, i : i + 1, :] = jnp.sum(scaled, axis=0, keepdims=True)

    def row_copy(buffer, lane, d):
        return pltpu.make_async_remote_copy(
            src_ref=buffer.at[0],
            dst_ref=buffer.at[d],
            send_sem=st_ss.at[lane, d],
            recv_sem=st_rs.at[lane, d],
            device_id=(me, lax.rem(col + d, N_HEAD)),
            device_id_type=MESH,
        )

    for d in range(1, N_HEAD):
        row_copy(early, 0, d).start()

    @pl.loop(0, TOK // BLOCK)
    def _(b):
        found = jnp.int32(-1)
        for slot in range(KEEP):
            off = kept[2, slot, me] - b
            found = jnp.maximum(found, (slot + 1) * (1 - jnp.minimum(off * off, 1)) - 1)
        inv_slot[b] = found

    @pl.loop(0, LEVELS * NCH)
    def _(t):
        level = 2 - lax.rem(t, 3)
        c = t // 3
        kv_copy(level, c).wait()
        rows = pl.ds(pl.multiple_of(c * CHUNK, CHUNK), CHUNK)
        kt_far[level, :, rows] = turned(kv_in[level, rows, 0:COLS])
        vt = turned(kv_in[level, rows, COLS:])
        for h in range(HEADS_DEV):
            vt_far[level, h, 0:DH, rows] = vt[h * DH : (h + 1) * DH]
        for h in range(HEADS_DEV):
            ka = jnp.concatenate(
                [kv_in[level, rows, h * DH : (h + 1) * DH], mk_far[level, rows, :]], axis=1
            )
            vta = vt_far[level, h, :, rows]
            for j in range(TOK // TILE):
                qs = slice(j * TILE, (j + 1) * TILE)
                s = dot(ka, qa[h, qs, :], 1, 1)
                m_old = m_run[h, :, qs]
                m = jnp.maximum(jnp.max(s, axis=0, keepdims=True), m_old)
                p = jnp.exp2((s - m) * coef).astype(BF16)
                p_far[level, h, rows, qs] = p
                m_run[h, :, qs] = m
                m_far[level, c, h, :, qs] = m
                acc[h, :, qs] = acc[h, :, qs] * jnp.exp2((m_old - m) * coef) + dot(vta, p, 1, 0)

    for i in range(TOK // DH):
        qs = slice(i * DH, (i + 1) * DH)
        total = jnp.zeros((1, DH), F32)
        for h in range(HEADS_DEV):
            inv = 1.0 / acc[h, DH : DH + 1, qs]
            inv_l[h, :, qs] = inv
            a = (acc[h, 0:DH, qs] * inv).astype(BF16).astype(F32)
            at[h * DH : (h + 1) * DH, qs] = a
            total = total + jnp.sum(a, axis=0, keepdims=True)
        mean = total * (1.0 / COLS)
        centred = at[:, qs] - mean
        scaled = gt[:, qs] * gc[...]
        st[0, i : i + 1, 0:128] = mean
        st[0, i : i + 1, 128:256] = jnp.sum(centred * centred, axis=0, keepdims=True)
        st[0, i : i + 1, 256:384] = jnp.sum(scaled * centred, axis=0, keepdims=True)

    for d in (4, 3, 5, 2, 6, 1, 7):
        row_copy(st, 1, d).start()
    for d in range(1, N_HEAD):
        row_copy(early, 0, d).wait()
    for d in range(1, N_HEAD):
        row_copy(st, 1, d).wait()

    mean = st[0, :, 0:128]
    for d in range(1, N_HEAD):
        mean = mean + st[d, :, 0:128]
    mean = mean * (1.0 / N_HEAD)
    square = jnp.zeros((8, DH), F32)
    plain = jnp.zeros((8, DH), F32)
    cross = jnp.zeros((8, DH), F32)
    for d in range(N_HEAD):
        off = st[d, :, 0:128] - mean
        square = square + (st[d, :, 128:256] + COLS * (off * off))
        plain = plain + early[d]
        cross = cross + (st[d, :, 256:384] + off * early[d])
    inv_std = lax.rsqrt(square * (1.0 / WIDTH) + NORM_EPS)
    res[:, 0:128] = mean
    res[:, 128:256] = inv_std
    res[:, 256:384] = plain * (1.0 / WIDTH)
    res[:, 384:512] = inv_std * cross * (1.0 / WIDTH)

    gain_part = jnp.zeros((COLS, DH), F32)
    for i in range(TOK // DH):
        qs = slice(i * DH, (i + 1) * DH)
        inv_std = res[i : i + 1, 128:256]
        normed = (at[:, qs] - res[i : i + 1, 0:128]) * inv_std
        scaled = gt[:, qs] * gc[...]
        do = inv_std * (scaled - res[i : i + 1, 256:384] - normed * res[i : i + 1, 384:512])
        do = do.astype(BF16)
        dot_[:, qs] = do
        gain_part = gain_part + gt[:, qs] * normed
        both = do.astype(F32) * at[:, qs]
        for h in range(HEADS_DEV):
            delta[h, :, qs] = jnp.sum(both[h * DH : (h + 1) * DH], axis=0, keepdims=True)

    def back(h, qs, parts, v, kt):
        probs = jnp.concatenate(
            [
                p.astype(F32) * (jnp.exp2((m - m_run[h, :, qs]) * coef) * inv_l[h, :, qs])
                for p, m in parts
            ],
            axis=0,
        )
        do = dot_[h * DH : (h + 1) * DH, qs]
        dp = dot(v, do, 1, 0)
        ds = (probs * (dp - delta[h, :, qs])).astype(BF16)
        dq = dot(kt, ds, 1, 0)
        dk = dot(ds, qa[h, qs, 0:DH], 1, 0)
        dv = dot(probs.astype(BF16), do, 1, 1)
        return dq, dk, dv

    dqt[...] = jnp.zeros_like(dqt)

    gsum[0] = jnp.broadcast_to(jnp.sum(jnp.transpose(gain_part), axis=0, keepdims=True), (8, COLS))

    def gg_copy(stage):
        return pltpu.make_async_remote_copy(
            src_ref=gsum.at[2 * stage],
            dst_ref=gsum.at[2 * stage + 1],
            send_sem=gg_ss.at[stage],
            recv_sem=gg_rs.at[stage],
            device_id=(flipped(me, 1 << stage), col),
            device_id_type=MESH,
        )

    def gg_end(stage):
        gg_copy(stage).wait()
        gsum[2 * stage + 2] = gsum[2 * stage] + gsum[2 * stage + 1]
        if stage < 3:
            gg_copy(stage + 1).start()

    gg_copy(0).start()

    @pl.loop(0, LEVELS)
    def _(t):
        level = lax.rem(4 - t, 3)
        for h in range(HEADS_DEV):
            hs = slice(h * DH, (h + 1) * DH)
            v = kv_in[level, :, COLS + h * DH : COLS + (h + 1) * DH]
            kt = kt_far[level, hs, :]
            dk_sum = jnp.zeros((KEPT, DH), F32)
            dv_sum = jnp.zeros((KEPT, DH), F32)
            for j in range(TOK // TILE):
                qs = slice(j * TILE, (j + 1) * TILE)
                parts = [
                    (p_far[level, h, c * CHUNK : (c + 1) * CHUNK, qs], m_far[level, c, h, :, qs])
                    for c in range(NCH)
                ]
                dq, dk, dv = back(h, qs, parts, v, kt)
                dqt[hs, qs] += dq
                dk_sum = dk_sum + dk
                dv_sum = dv_sum + dv
            shape = (KEEP, BLOCK, DH)
            gr_out[level, h, :, :, 0:DH] = (dk_sum * SCALE).astype(BF16).reshape(shape)
            gr_out[level, h, :, :, DH:] = dv_sum.astype(BF16).reshape(shape)
            if h == 0:
                pl.when(t == 0)(lambda: gg_end(0))
                pl.when(t == 1)(lambda: gg_end(2))
            else:
                pl.when(t == 0)(lambda: gg_end(1))
            for one in range(LEVELS):
                pl.when(level == one)(lambda one=one, h=h: gr_copy(one, h).start())

    for i in range(TOK // DH):
        qs = slice(i * DH, (i + 1) * DH)
        normed = (at[:, qs] - res[i : i + 1, 0:128]) * res[i : i + 1, 128:256]
        lo_ref[qs, :] = jnp.transpose(normed * gc[...]).astype(BF16)
    lo_copy = pltpu.make_async_copy(lo_ref, lo_hbm, io.at[0])
    lo_copy.start()

    @pl.loop(0, TOK // SEG)
    def _(t):
        keys = pl.ds(pl.multiple_of(t * SEG, SEG), SEG)
        blocks = pl.ds(t * (SEG // BLOCK), SEG // BLOCK)
        for h in range(HEADS_DEV):
            hs = slice(h * DH, (h + 1) * DH)
            v = v_ref[blocks, :, hs].reshape(SEG, DH)
            kt = kt_loc[hs, keys]
            dk_sum = jnp.zeros((SEG, DH), F32)
            dv_sum = jnp.zeros((SEG, DH), F32)
            for j in range(SEG // TILE):
                qs = pl.ds(pl.multiple_of(t * SEG + j * TILE, TILE), TILE)
                dq, dk, dv = back(h, qs, [(p_loc[h, :, qs], m_loc[h, :, qs])], v, kt)
                dqt[hs, qs] += dq
                dk_sum = dk_sum + dk
                dv_sum = dv_sum + dv
            dkv[keys, hs] = dk_sum * SCALE
            dkv[keys, COLS + h * DH : COLS + (h + 1) * DH] = dv_sum

    for t in range(TOK // TILE):
        cols = slice(t * TILE, (t + 1) * TILE)
        dq_ref[cols, :] = jnp.transpose(dqt[:, cols] * SCALE).astype(BF16)
    dq_copy = pltpu.make_async_copy(dq_ref, dq_hbm, io.at[1])
    dq_copy.start()
    gg_end(3)
    gg_ref[...] = gsum[8, 0:1, :]

    for h in range(HEADS_DEV):
        gr_copy(2, h).wait()

    @pl.loop(0, TOK // BLOCK)
    def _(b):
        slot = inv_slot[b]
        rows = pl.ds(pl.multiple_of(b * BLOCK, BLOCK), BLOCK)
        used = jnp.minimum(slot + 1, 1).astype(F32)
        for h in range(HEADS_DEV):
            part = gr_in2[h, jnp.maximum(slot, 0)].astype(F32) * used
            dkv[rows, h * DH : (h + 1) * DH] += part[:, 0:DH]
            dkv[rows, COLS + h * DH : COLS + (h + 1) * DH] += part[:, DH:]

    part_copy = pltpu.make_async_copy(dkv, part_hbm, io.at[2])
    part_copy.start()
    for level in range(2):
        for h in range(HEADS_DEV):
            gr_copy(level, h).wait()
    lo_copy.wait()
    dq_copy.wait()
    part_copy.wait()


def finish(
    kept, lo_in, dq_in, part_in, gr_in, gg_in, lo_ref, dq_ref, dk_ref, dv_ref, gg_ref, dk, dv, sems
):
    me = lax.axis_index("seq")
    gg_ref[...] = gg_in[...]
    copies = []

    def send(src, dst, i, lane):
        rows = pl.ds(i * TILE, TILE)
        copy = pltpu.make_async_copy(src.at[rows], dst.at[rows], sems.at[lane, i])
        copy.start()
        copies.append(copy)

    for i in range(TOK // TILE):
        send(lo_in, lo_ref, i, 0)
        send(dq_in, dq_ref, i, 1)
    for i in range(TOK // TILE):
        for b in range(i * (TILE // BLOCK), (i + 1) * (TILE // BLOCK)):
            rows = slice(b * BLOCK, (b + 1) * BLOCK)
            total = part_in[rows, :]
            key = [total[:, h * DH : (h + 1) * DH] for h in range(HEADS_DEV)]
            value = [total[:, COLS + h * DH : COLS + (h + 1) * DH] for h in range(HEADS_DEV)]
            for level in range(2):
                found = jnp.int32(-1)
                for slot in range(KEEP):
                    found = jnp.where(kept[level, slot, me] == b, jnp.int32(slot), found)
                used = jnp.minimum(found + 1, 1).astype(F32)
                for h in range(HEADS_DEV):
                    part = gr_in[level, h, jnp.maximum(found, 0)].astype(F32) * used
                    key[h] = key[h] + part[:, 0:DH]
                    value[h] = value[h] + part[:, DH:]
            for h in range(HEADS_DEV):
                dk[rows, h * DH : (h + 1) * DH] = key[h].astype(BF16)
                dv[rows, h * DH : (h + 1) * DH] = value[h].astype(BF16)
        send(dk, dk_ref, i, 2)
        send(dv, dv_ref, i, 3)
    for copy in copies:
        copy.wait()


def local(query_rows, key_rows, value_rows, norm_gain, grad_out, doc_lengths, kept_blocks):
    vmem = pl.BlockSpec(memory_space=pltpu.VMEM)
    smem = pl.BlockSpec(memory_space=pltpu.SMEM)
    hbm = pl.BlockSpec(memory_space=pltpu.HBM)
    some = pl.BlockSpec(memory_space=pl.ANY)
    rows = jax.ShapeDtypeStruct((TOK, COLS), BF16)
    dma = pltpu.SemaphoreType.DMA
    scratch = [
        pltpu.SMEM((LEVELS, KEEP, N_SEQ), jnp.int32),
        pltpu.VMEM((TOK, COLS), BF16),
        pltpu.VMEM((TOK // BLOCK, BLOCK, COLS), BF16),
        pltpu.VMEM((TOK // BLOCK, BLOCK, COLS), BF16),
        pltpu.VMEM((1, COLS), F32),
        pltpu.VMEM((TOK, COLS), BF16),
        pltpu.VMEM((TOK, COLS), BF16),
        pltpu.VMEM((TOK, COLS), BF16),
        pltpu.VMEM((HEADS_DEV, TOK, 2 * DH), BF16),
        pltpu.VMEM((TOK, DH), BF16),
        pltpu.VMEM((LEVELS, KEPT, DH), BF16),
        pltpu.VMEM((LEVELS, KEPT, 2 * COLS), BF16),
        pltpu.VMEM((LEVELS, KEPT, 2 * COLS), BF16),
        pltpu.VMEM((LEVELS, HEADS_DEV, KEEP, BLOCK, 2 * DH), BF16),
        pltpu.VMEM((HEADS_DEV, KEEP, BLOCK, 2 * DH), BF16),
        pltpu.VMEM((COLS, TOK), BF16),
        pltpu.VMEM((HEADS_DEV, DH + 16, TOK), BF16),
        pltpu.VMEM((LEVELS, COLS, KEPT), BF16),
        pltpu.VMEM((LEVELS, HEADS_DEV, DH + 16, KEPT), BF16),
        pltpu.VMEM((HEADS_DEV, SEG, TOK), BF16),
        pltpu.VMEM((LEVELS, HEADS_DEV, KEPT, TOK), BF16),
        pltpu.VMEM((HEADS_DEV, 1, TOK), F32),
        pltpu.VMEM((HEADS_DEV, 1, TOK), F32),
        pltpu.VMEM((LEVELS, NCH, HEADS_DEV, 1, TOK), F32),
        pltpu.VMEM((HEADS_DEV, DH + 16, TOK), F32),
        pltpu.VMEM((HEADS_DEV, 1, TOK), F32),
        pltpu.VMEM((COLS, TOK), F32),
        pltpu.VMEM((COLS, TOK), F32),
        pltpu.VMEM((COLS, DH), F32),
        pltpu.VMEM((N_HEAD, 8, 384), F32),
        pltpu.VMEM((N_HEAD, 8, DH), F32),
        pltpu.VMEM((8, 512), F32),
        pltpu.VMEM((COLS, TOK), BF16),
        pltpu.VMEM((HEADS_DEV, 1, TOK), F32),
        pltpu.VMEM((COLS, TOK), F32),
        pltpu.VMEM((TOK, 2 * COLS), F32),
        pltpu.VMEM((9, 8, COLS), F32),
        pltpu.SMEM((TOK // BLOCK,), jnp.int32),
        dma((LEVELS, NCH)),
        dma((LEVELS, NCH)),
        dma((LEVELS, HEADS_DEV)),
        dma((LEVELS, HEADS_DEV)),
        dma((2, N_HEAD)),
        dma((2, N_HEAD)),
        dma((4,)),
        dma((4,)),
        dma((18,)),
    ]
    kept = jnp.transpose(kept_blocks, (1, 2, 0))
    gain_row = jax.ShapeDtypeStruct((1, COLS), F32)
    lo, dq, part, returned, gain = pl.pallas_call(
        kernel,
        out_shape=[
            pltpu.VMEM((TOK, COLS), BF16),
            pltpu.VMEM((TOK, COLS), BF16),
            pltpu.VMEM((TOK, 2 * COLS), F32),
            pltpu.VMEM((2, HEADS_DEV, KEEP, BLOCK, 2 * DH), BF16),
            pltpu.VMEM((1, COLS), F32),
        ],
        in_specs=[hbm, smem] + [hbm] * 5,
        out_specs=[some] * 4 + [vmem],
        scratch_shapes=scratch,
        compiler_params=pltpu.CompilerParams(
            collective_id=0, has_side_effects=True, vmem_limit_bytes=44 * 1024 * 1024
        ),
        name="attention",
    )(
        *(
            pltpu.with_memory_space_constraint(x, pltpu.HBM)
            for x in (
                kept,
                doc_lengths,
                query_rows,
                key_rows.reshape(TOK // BLOCK, BLOCK, COLS),
                value_rows.reshape(TOK // BLOCK, BLOCK, COLS),
                norm_gain.reshape(1, COLS),
                grad_out,
            )
        )
    )
    lo, dq, dk, dv, gain = pl.pallas_call(
        finish,
        out_shape=[rows, rows, rows, rows, gain_row],
        in_specs=[smem] + [vmem] * 5,
        out_specs=[hbm] * 4 + [vmem],
        scratch_shapes=[
            pltpu.VMEM((TOK, COLS), BF16),
            pltpu.VMEM((TOK, COLS), BF16),
            dma((4, TOK // TILE)),
        ],
        compiler_params=pltpu.CompilerParams(vmem_limit_bytes=12 * 1024 * 1024),
        name="finish",
    )(pltpu.with_memory_space_constraint(kept, pltpu.HBM), lo, dq, part, returned, gain)
    return lo, dq, dk, dv, gain.reshape(COLS)


def solution(mesh):
    rows = P("seq", "head")
    in_specs = (rows, rows, rows, P("head"), rows, P(), P())
    out_specs = (rows, rows, rows, rows, P("head"))
    return jax.shard_map(local, mesh=mesh, in_specs=in_specs, out_specs=out_specs, check_vma=False)
```

```python
import functools

import jax
import jax.numpy as jnp
from jax import lax
from jax.experimental import pallas as pl
from jax.experimental.pallas import tpu as pltpu
from jax.sharding import PartitionSpec as P

DH = 128
TOK = 1024
SEG = 512
BLOCK = 64
KEEP = 8
LEVELS = 3
KEPT = KEEP * BLOCK
CHUNK = 256
NCH = KEPT // CHUNK
TILE = 256
WIDTH = 2048
HALVES = 2
HEADS_DEV = 2
COLS = HEADS_DEV * DH
N_SEQ = 16
N_HEAD = 8
NORM_EPS = 1e-05
SCALE = DH**-0.5
LOG2E = 1.4426950408889634
BIG = 2.0**100
LOW = -(2.0**99)
MESH = pl.DeviceIdType.MESH
F32 = jnp.float32
BF16 = jnp.bfloat16


def dot(a, b, ca, cb):
    return lax.dot_general(a, b, (((ca,), (cb,)), ((), ())), preferred_element_type=F32)


def turned(x):
    return jnp.transpose(x.astype(F32)).astype(x.dtype)


def flipped(index, bit):
    return index + bit * (1 - 2 * lax.rem(index // bit, 2))


def level_bit(level):
    return 1 + level + level // 2


def kernel(
    kept_hbm,
    lengths,
    q_hbm,
    k_hbm,
    v_hbm,
    gain_hbm,
    g_hbm,
    lo_hbm,
    dq_hbm,
    part_hbm,
    gr_hbm,
    gg_ref,
    kept,
    q_ref,
    k_ref,
    v_ref,
    gain_ref,
    g_ref,
    lo_ref,
    dq_ref,
    qa,
    mk_loc,
    mk_far,
    kv_out,
    kv_in,
    gr_out,
    gr_in2,
    kt_loc,
    vt_loc,
    kt_far,
    vt_far,
    p_loc,
    p_far,
    m_run,
    m_loc,
    m_far,
    acc,
    inv_l,
    at,
    gt,
    gc,
    st,
    early,
    res,
    dot_,
    delta,
    dqt,
    dkv,
    gsum,
    inv_slot,
    mq_far,
    mk_own,
    q_in,
    do_in,
    rows_out,
    rows_in,
    q_ss,
    q_rs,
    do_ss,
    do_rs,
    ro_ss,
    ro_rs,
    kv_ss,
    kv_rs,
    gr_ss,
    gr_rs,
    st_ss,
    st_rs,
    gg_ss,
    gg_rs,
    io,
):
    me = lax.axis_index("seq")
    col = lax.axis_index("head")

    barrier = pltpu.get_barrier_semaphore()
    beside = flipped(flipped(me, 1), 2)
    for other in [flipped(me, bit) for bit in (1, 2, 4, 8)] + [beside]:
        pl.semaphore_signal(barrier, inc=1, device_id=(other, col), device_id_type=MESH)
    for d in range(1, N_HEAD):
        pl.semaphore_signal(
            barrier, inc=1, device_id=(me, lax.rem(col + d, N_HEAD)), device_id_type=MESH
        )

    def load(src, dst, pieces, first):
        size = src.shape[0] // pieces
        copies = []
        for i in range(pieces):
            rows = pl.ds(i * size, size)
            copies.append(pltpu.make_async_copy(src.at[rows], dst.at[rows], io.at[first + i]))
            copies[-1].start()
        return copies

    loads = load(k_hbm, k_ref, 4, 0) + load(v_hbm, v_ref, 4, 4) + load(kept_hbm, kept, 1, 8)
    later = load(q_hbm, q_ref, 4, 9) + load(g_hbm, g_ref, 4, 13) + load(gain_hbm, gain_ref, 1, 17)
    for copy in loads:
        copy.wait()

    for level in range(LEVELS):
        for slot in range(KEEP):
            block = jnp.maximum(kept[level, slot, me], 0)
            kv_out[level, slot * BLOCK : (slot + 1) * BLOCK, 0:COLS] = k_ref[block]
            kv_out[level, slot * BLOCK : (slot + 1) * BLOCK, COLS:] = v_ref[block]
    pl.semaphore_wait(barrier, 5 + N_HEAD - 1)

    def kv_copy(level, c):
        rows = pl.ds(pl.multiple_of(c * CHUNK, CHUNK), CHUNK)
        return pltpu.make_async_remote_copy(
            src_ref=kv_out.at[level, rows],
            dst_ref=kv_in.at[level, rows],
            send_sem=kv_ss.at[level, c],
            recv_sem=kv_rs.at[level, c],
            device_id=(flipped(me, level_bit(level)), col),
            device_id_type=MESH,
        )

    def gr_copy(level, h):
        dst = gr_in2 if level == 2 else gr_hbm.at[level]
        return pltpu.make_async_remote_copy(
            src_ref=gr_out.at[level, h],
            dst_ref=dst.at[h],
            send_sem=gr_ss.at[level, h],
            recv_sem=gr_rs.at[level, h],
            device_id=(flipped(me, level_bit(level)), col),
            device_id_type=MESH,
        )

    def q_copy(hop, c):
        qs = pl.ds(c * (TOK // HALVES), TOK // HALVES)
        return pltpu.make_async_remote_copy(
            src_ref=q_in.at[0, qs] if hop else q_ref.at[qs, pl.ds(DH, DH)],
            dst_ref=q_in.at[hop, qs],
            send_sem=q_ss.at[hop, c],
            recv_sem=q_rs.at[hop, c],
            device_id=(beside if hop else flipped(me, 1), col),
            device_id_type=MESH,
        )

    def do_copy(hop, c):
        qs = pl.ds(c * (TOK // HALVES), TOK // HALVES)
        return pltpu.make_async_remote_copy(
            src_ref=do_in.at[0, :, qs] if hop else dot_.at[pl.ds(DH, DH), qs],
            dst_ref=do_in.at[hop, :, qs],
            send_sem=do_ss.at[hop, c],
            recv_sem=do_rs.at[hop, c],
            device_id=(beside if hop else flipped(me, 1), col),
            device_id_type=MESH,
        )

    def rows_copy(level):
        return pltpu.make_async_remote_copy(
            src_ref=rows_out,
            dst_ref=rows_in.at[level],
            send_sem=ro_ss.at[level],
            recv_sem=ro_rs.at[level],
            device_id=(flipped(me, 1 << level), col),
            device_id_type=MESH,
        )

    for c in range(NCH):
        for level in (1, 0, 2):
            kv_copy(level, c).start()

    for copy in later:
        copy.wait()
    start1 = lengths[0]
    start2 = lengths[0] + lengths[1]

    def doc_of(pos):
        return (pos >= start1).astype(jnp.int32) + (pos >= start2).astype(jnp.int32)

    lane = lax.broadcasted_iota(jnp.int32, (BLOCK, DH), 1)
    row = lax.broadcasted_iota(jnp.int32, (BLOCK, DH), 0)
    for b in range(TOK // BLOCK):
        rows = slice(b * BLOCK, (b + 1) * BLOCK)
        docs = doc_of(me * TOK + b * BLOCK + row)
        same = docs == lane
        mq = jnp.where(same, 1.0, 0.0).astype(BF16)
        mk_loc[rows, :] = jnp.where(same | (lane >= 3), 0.0, -BIG).astype(BF16)
        for h in range(HEADS_DEV):
            qa[h, rows, DH:] = mq
            qa[h, rows, 0:DH] = q_ref[rows, h * DH : (h + 1) * DH]
    for level in range(LEVELS):
        partner = flipped(me, level_bit(level))
        for slot in range(KEEP):
            listed = kept[level, slot, partner]
            docs = doc_of(partner * TOK + jnp.maximum(listed, 0) * BLOCK + row)
            docs = docs - 3 * jnp.minimum(listed, 0)
            same = docs == lane
            mk_far[level, slot * BLOCK : (slot + 1) * BLOCK, :] = jnp.where(
                same | (lane >= 3), 0.0, -BIG
            ).astype(BF16)

    for level in range(2):
        partner = flipped(me, level_bit(level))
        for b in range(TOK // BLOCK):
            same = doc_of(partner * TOK + b * BLOCK + row) == lane
            mq_far[level, b * BLOCK : (b + 1) * BLOCK, :] = jnp.where(same, 1.0, 0.0).astype(BF16)
        for slot in range(KEEP):
            listed = kept[level, slot, me]
            docs = doc_of(me * TOK + jnp.maximum(listed, 0) * BLOCK + row)
            docs = docs - 3 * jnp.minimum(listed, 0)
            mk_own[level, slot * BLOCK : (slot + 1) * BLOCK, :] = jnp.where(
                (docs == lane) | (lane >= 3), 0.0, -BIG
            ).astype(BF16)

    ones = jnp.ones((16, TOK), BF16)
    for h in range(HEADS_DEV):
        vt_loc[h, DH:, :] = ones
        for level in range(LEVELS):
            vt_far[level, h, DH:, :] = ones[:, 0:KEPT]

    for t in range(TOK // TILE):
        cols = slice(t * TILE, (t + 1) * TILE)
        blocks = slice(t * (TILE // BLOCK), (t + 1) * (TILE // BLOCK))
        kt_loc[:, cols] = turned(k_ref[blocks].reshape(TILE, COLS))
        vt = turned(v_ref[blocks].reshape(TILE, COLS))
        for h in range(HEADS_DEV):
            vt_loc[h, 0:DH, cols] = vt[h * DH : (h + 1) * DH]

    coef = SCALE * LOG2E

    @pl.loop(0, TOK // SEG)
    def _(t):
        keys = pl.ds(pl.multiple_of(t * SEG, SEG), SEG)
        blocks = pl.ds(t * (SEG // BLOCK), SEG // BLOCK)
        for h in range(HEADS_DEV):
            k = k_ref[blocks, :, h * DH : (h + 1) * DH].reshape(SEG, DH)
            ka = jnp.concatenate([k, mk_loc[keys, :]], axis=1)
            vt = vt_loc[h, :, keys]
            for j in range(SEG // TILE):
                qs = pl.ds(pl.multiple_of(t * SEG + j * TILE, TILE), TILE)
                s = dot(ka, qa[h, qs, :], 1, 1)
                m = jnp.maximum(jnp.max(s, axis=0, keepdims=True), LOW)
                p = jnp.exp2((s - m) * coef).astype(BF16)
                p_loc[h, :, qs] = p
                m_run[h, :, qs] = m
                m_loc[h, :, qs] = m
                acc[h, :, qs] = dot(vt, p, 1, 0)

    gc[...] = jnp.transpose(jnp.broadcast_to(gain_ref[...], (DH, COLS)))
    for t in range(TOK // TILE):
        cols = slice(t * TILE, (t + 1) * TILE)
        gt[:, cols] = jnp.transpose(g_ref[cols, :].astype(F32))

    for i in range(TOK // DH):
        scaled = gt[:, i * DH : (i + 1) * DH] * gc[...]
        early[0, i : i + 1, :] = jnp.sum(scaled, axis=0, keepdims=True)

    def row_copy(buffer, lane, d):
        return pltpu.make_async_remote_copy(
            src_ref=buffer.at[0],
            dst_ref=buffer.at[d],
            send_sem=st_ss.at[lane, d],
            recv_sem=st_rs.at[lane, d],
            device_id=(me, lax.rem(col + d, N_HEAD)),
            device_id_type=MESH,
        )

    for d in range(1, N_HEAD):
        row_copy(early, 0, d).start()

    @pl.loop(0, TOK // BLOCK)
    def _(b):
        found = jnp.int32(-1)
        for slot in range(KEEP):
            off = kept[2, slot, me] - b
            found = jnp.maximum(found, (slot + 1) * (1 - jnp.minimum(off * off, 1)) - 1)
        inv_slot[b] = found

    @pl.loop(0, LEVELS * NCH)
    def _(t):
        level = 2 - lax.rem(t, 3)
        c = t // 3
        kv_copy(level, c).wait()

        @pl.when(t == LEVELS * NCH - 1)
        def _():
            for half in range(HALVES):
                q_copy(0, half).start()

        rows = pl.ds(pl.multiple_of(c * CHUNK, CHUNK), CHUNK)
        kt_far[level, :, rows] = turned(kv_in[level, rows, 0:COLS])
        vt = turned(kv_in[level, rows, COLS:])
        for h in range(HEADS_DEV):
            vt_far[level, h, 0:DH, rows] = vt[h * DH : (h + 1) * DH]
        for h in range(HEADS_DEV):
            ka = jnp.concatenate(
                [kv_in[level, rows, h * DH : (h + 1) * DH], mk_far[level, rows, :]], axis=1
            )
            vta = vt_far[level, h, :, rows]
            for j in range(TOK // TILE):
                qs = slice(j * TILE, (j + 1) * TILE)
                s = dot(ka, qa[h, qs, :], 1, 1)
                m_old = m_run[h, :, qs]
                m = jnp.maximum(jnp.max(s, axis=0, keepdims=True), m_old)
                p = jnp.exp2((s - m) * coef).astype(BF16)
                p_far[level, h, rows, qs] = p
                m_run[h, :, qs] = m
                m_far[level, c, h, :, qs] = m
                acc[h, :, qs] = acc[h, :, qs] * jnp.exp2((m_old - m) * coef) + dot(vta, p, 1, 0)

    for i in range(TOK // DH):
        qs = slice(i * DH, (i + 1) * DH)
        total = jnp.zeros((1, DH), F32)
        for h in range(HEADS_DEV):
            inv = 1.0 / acc[h, DH : DH + 1, qs]
            inv_l[h, :, qs] = inv
            a = (acc[h, 0:DH, qs] * inv).astype(BF16).astype(F32)
            at[h * DH : (h + 1) * DH, qs] = a
            total = total + jnp.sum(a, axis=0, keepdims=True)
        mean = total * (1.0 / COLS)
        centred = at[:, qs] - mean
        scaled = gt[:, qs] * gc[...]
        st[0, i : i + 1, 0:128] = mean
        st[0, i : i + 1, 128:256] = jnp.sum(centred * centred, axis=0, keepdims=True)
        st[0, i : i + 1, 256:384] = jnp.sum(scaled * centred, axis=0, keepdims=True)

    for d in (4, 3, 5, 2, 6, 1, 7):
        row_copy(st, 1, d).start()
    for d in range(1, N_HEAD):
        row_copy(early, 0, d).wait()
    for d in range(1, N_HEAD):
        row_copy(st, 1, d).wait()

    mean = st[0, :, 0:128]
    for d in range(1, N_HEAD):
        mean = mean + st[d, :, 0:128]
    mean = mean * (1.0 / N_HEAD)
    square = jnp.zeros((8, DH), F32)
    plain = jnp.zeros((8, DH), F32)
    cross = jnp.zeros((8, DH), F32)
    for d in range(N_HEAD):
        off = st[d, :, 0:128] - mean
        square = square + (st[d, :, 128:256] + COLS * (off * off))
        plain = plain + early[d]
        cross = cross + (st[d, :, 256:384] + off * early[d])
    inv_std = lax.rsqrt(square * (1.0 / WIDTH) + NORM_EPS)
    res[:, 0:128] = mean
    res[:, 128:256] = inv_std
    res[:, 256:384] = plain * (1.0 / WIDTH)
    res[:, 384:512] = inv_std * cross * (1.0 / WIDTH)

    gain_part = jnp.zeros((COLS, DH), F32)
    for i in range(TOK // DH):
        qs = slice(i * DH, (i + 1) * DH)
        inv_std = res[i : i + 1, 128:256]
        normed = (at[:, qs] - res[i : i + 1, 0:128]) * inv_std
        scaled = gt[:, qs] * gc[...]
        do = inv_std * (scaled - res[i : i + 1, 256:384] - normed * res[i : i + 1, 384:512])
        do = do.astype(BF16)
        dot_[:, qs] = do
        gain_part = gain_part + gt[:, qs] * normed
        both = do.astype(F32) * at[:, qs]
        for h in range(HEADS_DEV):
            delta[h, :, qs] = jnp.sum(both[h * DH : (h + 1) * DH], axis=0, keepdims=True)
        log_l = jnp.log(acc[1, DH : DH + 1, qs])
        rows_out[i : i + 1, 0:DH] = m_run[1, :, qs] + log_l * (1.0 / SCALE)
        rows_out[i : i + 1, DH:] = delta[1, :, qs]

    def back(h, qs, parts, v, kt, whole=True):
        probs = jnp.concatenate(
            [
                p.astype(F32) * (jnp.exp2((m - m_run[h, :, qs]) * coef) * inv_l[h, :, qs])
                for p, m in parts
            ],
            axis=0,
        )
        do = dot_[h * DH : (h + 1) * DH, qs]
        dp = dot(v, do, 1, 0)
        ds = (probs * (dp - delta[h, :, qs])).astype(BF16)
        dq = dot(kt, ds, 1, 0)
        if not whole:
            return dq, None, None
        dk = dot(ds, qa[h, qs, 0:DH], 1, 0)
        dv = dot(probs.astype(BF16), do, 1, 1)
        return dq, dk, dv

    dqt[...] = jnp.zeros_like(dqt)

    gsum[0] = jnp.broadcast_to(jnp.sum(jnp.transpose(gain_part), axis=0, keepdims=True), (8, COLS))

    def gg_copy(stage):
        flip, src, dst = ((1, 0, 1), (2, 0, 2), (3, 0, 3), (4, 4, 5), (8, 6, 7))[stage]
        return pltpu.make_async_remote_copy(
            src_ref=gsum.at[src],
            dst_ref=gsum.at[dst],
            send_sem=gg_ss.at[stage],
            recv_sem=gg_rs.at[stage],
            device_id=(beside if flip == 3 else flipped(me, flip), col),
            device_id_type=MESH,
        )

    for stage in range(3):
        gg_copy(stage).start()
    for level in range(2):
        rows_copy(level).start()
    for c in range(HALVES):
        do_copy(0, c).start()

    def back_level(level, h, whole):
        hs = slice(h * DH, (h + 1) * DH)
        v = kv_in[level, :, COLS + h * DH : COLS + (h + 1) * DH]
        kt = kt_far[level, hs, :]
        dk_sum = jnp.zeros((KEPT, DH), F32)
        dv_sum = jnp.zeros((KEPT, DH), F32)
        for j in range(TOK // TILE):
            qs = slice(j * TILE, (j + 1) * TILE)
            parts = [
                (p_far[level, h, c * CHUNK : (c + 1) * CHUNK, qs], m_far[level, c, h, :, qs])
                for c in range(NCH)
            ]
            dq, dk, dv = back(h, qs, parts, v, kt, whole)
            dqt[hs, qs] += dq
            if whole:
                dk_sum = dk_sum + dk
                dv_sum = dv_sum + dv
        if whole:
            keep_grads(level, h, dk_sum, dv_sum)

    def keep_grads(level, h, dk_sum, dv_sum):
        shape = (KEEP, BLOCK, DH)
        gr_out[level, h, :, :, 0:DH] = (dk_sum * SCALE).astype(BF16).reshape(shape)
        gr_out[level, h, :, :, DH:] = dv_sum.astype(BF16).reshape(shape)

    @pl.loop(0, 2)
    def _(t):
        level = 1 - t
        back_level(level, 0, True)
        for one in range(2):

            @pl.when(level == one)
            def _():
                if one == 1:
                    for c in range(HALVES):
                        q_copy(0, c).wait()
                        q_copy(1, c).start()
                else:
                    for stage in range(3):
                        gg_copy(stage).wait()
                    gsum[4] = (gsum[0] + gsum[1]) + (gsum[2] + gsum[3])
                    gg_copy(3).start()
                gr_copy(one, 0).start()

    for h in range(HEADS_DEV):
        back_level(2, h, True)
        do_copy(0, h).wait()
        do_copy(1, h).start()
        if h == 0:
            gg_copy(3).wait()
            gsum[6] = gsum[4] + gsum[5]
            gg_copy(4).start()
        gr_copy(2, h).start()

    @pl.loop(0, 2)
    def _(level):
        back_level(level, 1, False)

    for i in range(TOK // DH):
        qs = slice(i * DH, (i + 1) * DH)
        normed = (at[:, qs] - res[i : i + 1, 0:128]) * res[i : i + 1, 128:256]
        lo_ref[qs, :] = jnp.transpose(normed * gc[...]).astype(BF16)
    lo_copy = pltpu.make_async_copy(lo_ref, lo_hbm, io.at[0])
    lo_copy.start()

    @pl.loop(0, TOK // SEG)
    def _(t):
        keys = pl.ds(pl.multiple_of(t * SEG, SEG), SEG)
        blocks = pl.ds(t * (SEG // BLOCK), SEG // BLOCK)
        for h in range(HEADS_DEV):
            hs = slice(h * DH, (h + 1) * DH)
            v = v_ref[blocks, :, hs].reshape(SEG, DH)
            kt = kt_loc[hs, keys]
            dk_sum = jnp.zeros((SEG, DH), F32)
            dv_sum = jnp.zeros((SEG, DH), F32)
            for j in range(SEG // TILE):
                qs = pl.ds(pl.multiple_of(t * SEG + j * TILE, TILE), TILE)
                dq, dk, dv = back(h, qs, [(p_loc[h, :, qs], m_loc[h, :, qs])], v, kt)
                dqt[hs, qs] += dq
                dk_sum = dk_sum + dk
                dv_sum = dv_sum + dv
            dkv[keys, hs] = dk_sum * SCALE
            dkv[keys, COLS + h * DH : COLS + (h + 1) * DH] = dv_sum

    for t in range(TOK // TILE):
        cols = slice(t * TILE, (t + 1) * TILE)
        dq_ref[cols, :] = jnp.transpose(dqt[:, cols] * SCALE).astype(BF16)
    dq_copy = pltpu.make_async_copy(dq_ref, dq_hbm, io.at[1])
    dq_copy.start()
    gg_copy(4).wait()
    gg_ref[...] = gsum[6, 0:1, :] + gsum[7, 0:1, :]

    @pl.loop(0, 2)
    def _(level):
        for one in range(2):

            @pl.when(level == one)
            def _():
                rows_copy(one).wait()
                if one == 1:
                    for c in range(HALVES):
                        q_copy(1, c).wait()
                        do_copy(1, c).wait()

        ka = jnp.concatenate([kv_out[level, :, DH:COLS], mk_own[level]], axis=1)
        v = kv_out[level, :, COLS + DH :]
        dk_sum = jnp.zeros((KEPT, DH), F32)
        dv_sum = jnp.zeros((KEPT, DH), F32)
        for j in range(TOK // TILE):
            qs = slice(j * TILE, (j + 1) * TILE)
            pieces = range(j * (TILE // DH), (j + 1) * (TILE // DH))
            logs = jnp.concatenate([rows_in[level, i : i + 1, 0:DH] for i in pieces], axis=1)
            deltas = jnp.concatenate([rows_in[level, i : i + 1, DH:] for i in pieces], axis=1)
            q = q_in[level, qs, :]
            do = do_in[level, :, qs]
            s = dot(ka, jnp.concatenate([q, mq_far[level, qs, :]], axis=1), 1, 1)
            probs = jnp.exp2((s - logs) * coef)
            ds = (probs * (dot(v, do, 1, 0) - deltas)).astype(BF16)
            dk_sum = dk_sum + dot(ds, q, 1, 0)
            dv_sum = dv_sum + dot(probs.astype(BF16), do, 1, 1)
        keep_grads(level, 1, dk_sum, dv_sum)

    own_copies = [
        pltpu.make_async_copy(gr_out.at[level, 1], gr_hbm.at[level, 1], io.at[3 + level])
        for level in range(2)
    ]
    for copy in own_copies:
        copy.start()

    for h in range(HEADS_DEV):
        gr_copy(2, h).wait()

    @pl.loop(0, TOK // BLOCK)
    def _(b):
        slot = inv_slot[b]
        rows = pl.ds(pl.multiple_of(b * BLOCK, BLOCK), BLOCK)
        used = jnp.minimum(slot + 1, 1).astype(F32)
        for h in range(HEADS_DEV):
            part = gr_in2[h, jnp.maximum(slot, 0)].astype(F32) * used
            dkv[rows, h * DH : (h + 1) * DH] += part[:, 0:DH]
            dkv[rows, COLS + h * DH : COLS + (h + 1) * DH] += part[:, DH:]

    part_copy = pltpu.make_async_copy(dkv, part_hbm, io.at[2])
    part_copy.start()
    for level in range(2):
        gr_copy(level, 0).wait()
    for copy in own_copies:
        copy.wait()
    lo_copy.wait()
    dq_copy.wait()
    part_copy.wait()


def finish(
    kept, lo_in, dq_in, part_in, gr_in, gg_in, lo_ref, dq_ref, dk_ref, dv_ref, gg_ref, dk, dv, sems
):
    me = lax.axis_index("seq")
    gg_ref[...] = gg_in[...]
    copies = []

    def send(src, dst, i, lane):
        rows = pl.ds(i * TILE, TILE)
        copy = pltpu.make_async_copy(src.at[rows], dst.at[rows], sems.at[lane, i])
        copy.start()
        copies.append(copy)

    for i in range(TOK // TILE):
        send(lo_in, lo_ref, i, 0)
        send(dq_in, dq_ref, i, 1)
    for i in range(TOK // TILE):
        for b in range(i * (TILE // BLOCK), (i + 1) * (TILE // BLOCK)):
            rows = slice(b * BLOCK, (b + 1) * BLOCK)
            total = part_in[rows, :]
            key = [total[:, h * DH : (h + 1) * DH] for h in range(HEADS_DEV)]
            value = [total[:, COLS + h * DH : COLS + (h + 1) * DH] for h in range(HEADS_DEV)]
            for level in range(2):
                found = jnp.int32(-1)
                for slot in range(KEEP):
                    found = jnp.where(kept[level, slot, me] == b, jnp.int32(slot), found)
                used = jnp.minimum(found + 1, 1).astype(F32)
                for h in range(HEADS_DEV):
                    part = gr_in[level, h, jnp.maximum(found, 0)].astype(F32) * used
                    key[h] = key[h] + part[:, 0:DH]
                    value[h] = value[h] + part[:, DH:]
            for h in range(HEADS_DEV):
                dk[rows, h * DH : (h + 1) * DH] = key[h].astype(BF16)
                dv[rows, h * DH : (h + 1) * DH] = value[h].astype(BF16)
        send(dk, dk_ref, i, 2)
        send(dv, dv_ref, i, 3)
    for copy in copies:
        copy.wait()


def local(query_rows, key_rows, value_rows, norm_gain, grad_out, doc_lengths, kept_blocks):
    vmem = pl.BlockSpec(memory_space=pltpu.VMEM)
    smem = pl.BlockSpec(memory_space=pltpu.SMEM)
    hbm = pl.BlockSpec(memory_space=pltpu.HBM)
    some = pl.BlockSpec(memory_space=pl.ANY)
    rows = jax.ShapeDtypeStruct((TOK, COLS), BF16)
    dma = pltpu.SemaphoreType.DMA
    scratch = [
        pltpu.SMEM((LEVELS, KEEP, N_SEQ), jnp.int32),
        pltpu.VMEM((TOK, COLS), BF16),
        pltpu.VMEM((TOK // BLOCK, BLOCK, COLS), BF16),
        pltpu.VMEM((TOK // BLOCK, BLOCK, COLS), BF16),
        pltpu.VMEM((1, COLS), F32),
        pltpu.VMEM((TOK, COLS), BF16),
        pltpu.VMEM((TOK, COLS), BF16),
        pltpu.VMEM((TOK, COLS), BF16),
        pltpu.VMEM((HEADS_DEV, TOK, 2 * DH), BF16),
        pltpu.VMEM((TOK, DH), BF16),
        pltpu.VMEM((LEVELS, KEPT, DH), BF16),
        pltpu.VMEM((LEVELS, KEPT, 2 * COLS), BF16),
        pltpu.VMEM((LEVELS, KEPT, 2 * COLS), BF16),
        pltpu.VMEM((LEVELS, HEADS_DEV, KEEP, BLOCK, 2 * DH), BF16),
        pltpu.VMEM((HEADS_DEV, KEEP, BLOCK, 2 * DH), BF16),
        pltpu.VMEM((COLS, TOK), BF16),
        pltpu.VMEM((HEADS_DEV, DH + 16, TOK), BF16),
        pltpu.VMEM((LEVELS, COLS, KEPT), BF16),
        pltpu.VMEM((LEVELS, HEADS_DEV, DH + 16, KEPT), BF16),
        pltpu.VMEM((HEADS_DEV, SEG, TOK), BF16),
        pltpu.VMEM((LEVELS, HEADS_DEV, KEPT, TOK), BF16),
        pltpu.VMEM((HEADS_DEV, 1, TOK), F32),
        pltpu.VMEM((HEADS_DEV, 1, TOK), F32),
        pltpu.VMEM((LEVELS, NCH, HEADS_DEV, 1, TOK), F32),
        pltpu.VMEM((HEADS_DEV, DH + 16, TOK), F32),
        pltpu.VMEM((HEADS_DEV, 1, TOK), F32),
        pltpu.VMEM((COLS, TOK), F32),
        pltpu.VMEM((COLS, TOK), F32),
        pltpu.VMEM((COLS, DH), F32),
        pltpu.VMEM((N_HEAD, 8, 384), F32),
        pltpu.VMEM((N_HEAD, 8, DH), F32),
        pltpu.VMEM((8, 512), F32),
        pltpu.VMEM((COLS, TOK), BF16),
        pltpu.VMEM((HEADS_DEV, 1, TOK), F32),
        pltpu.VMEM((COLS, TOK), F32),
        pltpu.VMEM((TOK, 2 * COLS), F32),
        pltpu.VMEM((8, 8, COLS), F32),
        pltpu.SMEM((TOK // BLOCK,), jnp.int32),
        pltpu.VMEM((2, TOK, DH), BF16),
        pltpu.VMEM((2, KEPT, DH), BF16),
        pltpu.VMEM((2, TOK, DH), BF16),
        pltpu.VMEM((2, DH, TOK), BF16),
        pltpu.VMEM((8, 2 * DH), F32),
        pltpu.VMEM((2, 8, 2 * DH), F32),
        dma((2, HALVES)),
        dma((2, HALVES)),
        dma((2, HALVES)),
        dma((2, HALVES)),
        dma((2,)),
        dma((2,)),
        dma((LEVELS, NCH)),
        dma((LEVELS, NCH)),
        dma((LEVELS, HEADS_DEV)),
        dma((LEVELS, HEADS_DEV)),
        dma((2, N_HEAD)),
        dma((2, N_HEAD)),
        dma((5,)),
        dma((5,)),
        dma((18,)),
    ]
    kept = jnp.transpose(kept_blocks, (1, 2, 0))
    gain_row = jax.ShapeDtypeStruct((1, COLS), F32)
    lo, dq, part, returned, gain = pl.pallas_call(
        kernel,
        out_shape=[
            pltpu.VMEM((TOK, COLS), BF16),
            pltpu.VMEM((TOK, COLS), BF16),
            pltpu.VMEM((TOK, 2 * COLS), F32),
            pltpu.VMEM((2, HEADS_DEV, KEEP, BLOCK, 2 * DH), BF16),
            pltpu.VMEM((1, COLS), F32),
        ],
        in_specs=[hbm, smem] + [hbm] * 5,
        out_specs=[some] * 4 + [vmem],
        scratch_shapes=scratch,
        compiler_params=pltpu.CompilerParams(
            collective_id=0, has_side_effects=True, vmem_limit_bytes=44 * 1024 * 1024
        ),
        name="attention",
    )(
        *(
            pltpu.with_memory_space_constraint(x, pltpu.HBM)
            for x in (
                kept,
                doc_lengths,
                query_rows,
                key_rows.reshape(TOK // BLOCK, BLOCK, COLS),
                value_rows.reshape(TOK // BLOCK, BLOCK, COLS),
                norm_gain.reshape(1, COLS),
                grad_out,
            )
        )
    )
    lo, dq, dk, dv, gain = pl.pallas_call(
        finish,
        out_shape=[rows, rows, rows, rows, gain_row],
        in_specs=[smem] + [vmem] * 5,
        out_specs=[hbm] * 4 + [vmem],
        scratch_shapes=[
            pltpu.VMEM((TOK, COLS), BF16),
            pltpu.VMEM((TOK, COLS), BF16),
            dma((4, TOK // TILE)),
        ],
        compiler_params=pltpu.CompilerParams(vmem_limit_bytes=12 * 1024 * 1024),
        name="finish",
    )(pltpu.with_memory_space_constraint(kept, pltpu.HBM), lo, dq, part, returned, gain)
    return lo, dq, dk, dv, gain.reshape(COLS)


def solution(mesh):
    rows = P("seq", "head")
    in_specs = (rows, rows, rows, P("head"), rows, P(), P())
    out_specs = (rows, rows, rows, rows, P("head"))
    return jax.shard_map(local, mesh=mesh, in_specs=in_specs, out_specs=out_specs, check_vma=False)
```

```python
import functools

import jax
import jax.numpy as jnp
from jax import lax
from jax.experimental import pallas as pl
from jax.experimental.pallas import tpu as pltpu
from jax.sharding import PartitionSpec as P

DH = 128
TOK = 1024
SEG = 512
BLOCK = 64
KEEP = 8
LEVELS = 3
KEPT = KEEP * BLOCK
CHUNK = 256
NCH = KEPT // CHUNK
TILE = 256
WIDTH = 2048
HALVES = 2
HEADS_DEV = 2
COLS = HEADS_DEV * DH
N_SEQ = 16
N_HEAD = 8
NORM_EPS = 1e-05
SCALE = DH**-0.5
LOG2E = 1.4426950408889634
BIG = 2.0**100
LOW = -(2.0**99)
MESH = pl.DeviceIdType.MESH
F32 = jnp.float32
BF16 = jnp.bfloat16


def dot(a, b, ca, cb):
    return lax.dot_general(a, b, (((ca,), (cb,)), ((), ())), preferred_element_type=F32)


def turned(x):
    return jnp.transpose(x.astype(F32)).astype(x.dtype)


def flipped(index, bit):
    return index + bit * (1 - 2 * lax.rem(index // bit, 2))


def level_bit(level):
    return 1 + level + level // 2


def kernel(
    kept_hbm,
    lengths,
    q_hbm,
    k_hbm,
    v_hbm,
    gain_hbm,
    g_hbm,
    lo_hbm,
    dq_hbm,
    part_hbm,
    gr_hbm,
    gg_ref,
    kept,
    q_ref,
    k_ref,
    v_ref,
    gain_ref,
    g_ref,
    lo_ref,
    dq_ref,
    qa,
    mk_loc,
    mk_far,
    kv_out,
    kv_in,
    gr_out,
    gr_in2,
    kt_loc,
    vt_loc,
    kt_far,
    vt_far,
    p_loc,
    p_far,
    m_run,
    m_loc,
    m_far,
    acc,
    inv_l,
    at,
    gt,
    gc,
    st,
    early,
    res,
    dot_,
    delta,
    dqt,
    dkv,
    gsum,
    inv_slot,
    mq_far,
    mk_own,
    q_in,
    do_in,
    rows_out,
    rows_in,
    q_ss,
    q_rs,
    do_ss,
    do_rs,
    ro_ss,
    ro_rs,
    kv_ss,
    kv_rs,
    gr_ss,
    gr_rs,
    st_ss,
    st_rs,
    gg_ss,
    gg_rs,
    io,
):
    me = lax.axis_index("seq")
    col = lax.axis_index("head")

    barrier = pltpu.get_barrier_semaphore()
    beside = flipped(flipped(me, 1), 2)
    for other in [flipped(me, bit) for bit in (1, 2, 4, 8)] + [beside]:
        pl.semaphore_signal(barrier, inc=1, device_id=(other, col), device_id_type=MESH)
    for d in range(1, N_HEAD):
        pl.semaphore_signal(
            barrier, inc=1, device_id=(me, lax.rem(col + d, N_HEAD)), device_id_type=MESH
        )

    def load(src, dst, pieces, first):
        size = src.shape[0] // pieces
        copies = []
        for i in range(pieces):
            rows = pl.ds(i * size, size)
            copies.append(pltpu.make_async_copy(src.at[rows], dst.at[rows], io.at[first + i]))
            copies[-1].start()
        return copies

    loads = load(k_hbm, k_ref, 4, 0) + load(v_hbm, v_ref, 4, 4) + load(kept_hbm, kept, 1, 8)
    later = load(q_hbm, q_ref, 4, 9) + load(g_hbm, g_ref, 4, 13) + load(gain_hbm, gain_ref, 1, 17)
    for copy in loads:
        copy.wait()

    for level in range(LEVELS):
        for slot in range(KEEP):
            block = jnp.maximum(kept[level, slot, me], 0)
            kv_out[level, slot * BLOCK : (slot + 1) * BLOCK, 0:COLS] = k_ref[block]
            kv_out[level, slot * BLOCK : (slot + 1) * BLOCK, COLS:] = v_ref[block]
    pl.semaphore_wait(barrier, 5 + N_HEAD - 1)

    def kv_copy(level, c):
        rows = pl.ds(pl.multiple_of(c * CHUNK, CHUNK), CHUNK)
        return pltpu.make_async_remote_copy(
            src_ref=kv_out.at[level, rows],
            dst_ref=kv_in.at[level, rows],
            send_sem=kv_ss.at[level, c],
            recv_sem=kv_rs.at[level, c],
            device_id=(flipped(me, level_bit(level)), col),
            device_id_type=MESH,
        )

    def gr_copy(level, h):
        dst = gr_in2 if level == 2 else gr_hbm.at[level]
        return pltpu.make_async_remote_copy(
            src_ref=gr_out.at[level, h],
            dst_ref=dst.at[h],
            send_sem=gr_ss.at[level, h],
            recv_sem=gr_rs.at[level, h],
            device_id=(flipped(me, level_bit(level)), col),
            device_id_type=MESH,
        )

    def q_copy(hop, c):
        qs = pl.ds(c * (TOK // HALVES), TOK // HALVES)
        return pltpu.make_async_remote_copy(
            src_ref=q_in.at[0, qs] if hop else q_ref.at[qs, pl.ds(DH, DH)],
            dst_ref=q_in.at[hop, qs],
            send_sem=q_ss.at[hop, c],
            recv_sem=q_rs.at[hop, c],
            device_id=(beside if hop else flipped(me, 1), col),
            device_id_type=MESH,
        )

    def do_copy(hop, c):
        qs = pl.ds(c * (TOK // HALVES), TOK // HALVES)
        return pltpu.make_async_remote_copy(
            src_ref=do_in.at[0, :, qs] if hop else dot_.at[pl.ds(DH, DH), qs],
            dst_ref=do_in.at[hop, :, qs],
            send_sem=do_ss.at[hop, c],
            recv_sem=do_rs.at[hop, c],
            device_id=(beside if hop else flipped(me, 1), col),
            device_id_type=MESH,
        )

    def rows_copy(level):
        return pltpu.make_async_remote_copy(
            src_ref=rows_out,
            dst_ref=rows_in.at[level],
            send_sem=ro_ss.at[level],
            recv_sem=ro_rs.at[level],
            device_id=(flipped(me, 1 << level), col),
            device_id_type=MESH,
        )

    for c in range(NCH):
        for level in (1, 0, 2):
            kv_copy(level, c).start()

    for copy in later:
        copy.wait()
    start1 = lengths[0]
    start2 = lengths[0] + lengths[1]

    def doc_of(pos):
        return (pos >= start1).astype(jnp.int32) + (pos >= start2).astype(jnp.int32)

    lane = lax.broadcasted_iota(jnp.int32, (BLOCK, DH), 1)
    row = lax.broadcasted_iota(jnp.int32, (BLOCK, DH), 0)
    for b in range(TOK // BLOCK):
        rows = slice(b * BLOCK, (b + 1) * BLOCK)
        docs = doc_of(me * TOK + b * BLOCK + row)
        same = docs == lane
        mq = jnp.where(same, 1.0, 0.0).astype(BF16)
        mk_loc[rows, :] = jnp.where(same | (lane >= 3), 0.0, -BIG).astype(BF16)
        for h in range(HEADS_DEV):
            qa[h, rows, DH:] = mq
            qa[h, rows, 0:DH] = q_ref[rows, h * DH : (h + 1) * DH]
    for level in range(LEVELS):
        partner = flipped(me, level_bit(level))
        for slot in range(KEEP):
            listed = kept[level, slot, partner]
            docs = doc_of(partner * TOK + jnp.maximum(listed, 0) * BLOCK + row)
            docs = docs - 3 * jnp.minimum(listed, 0)
            same = docs == lane
            mk_far[level, slot * BLOCK : (slot + 1) * BLOCK, :] = jnp.where(
                same | (lane >= 3), 0.0, -BIG
            ).astype(BF16)

    for level in range(2):
        partner = flipped(me, level_bit(level))
        for b in range(TOK // BLOCK):
            same = doc_of(partner * TOK + b * BLOCK + row) == lane
            mq_far[level, b * BLOCK : (b + 1) * BLOCK, :] = jnp.where(same, 1.0, 0.0).astype(BF16)
        for slot in range(KEEP):
            listed = kept[level, slot, me]
            docs = doc_of(me * TOK + jnp.maximum(listed, 0) * BLOCK + row)
            docs = docs - 3 * jnp.minimum(listed, 0)
            mk_own[level, slot * BLOCK : (slot + 1) * BLOCK, :] = jnp.where(
                (docs == lane) | (lane >= 3), 0.0, -BIG
            ).astype(BF16)

    ones = jnp.ones((16, TOK), BF16)
    for h in range(HEADS_DEV):
        vt_loc[h, DH:, :] = ones
        for level in range(LEVELS):
            vt_far[level, h, DH:, :] = ones[:, 0:KEPT]

    for t in range(TOK // TILE):
        cols = slice(t * TILE, (t + 1) * TILE)
        blocks = slice(t * (TILE // BLOCK), (t + 1) * (TILE // BLOCK))
        kt_loc[:, cols] = turned(k_ref[blocks].reshape(TILE, COLS))
        vt = turned(v_ref[blocks].reshape(TILE, COLS))
        for h in range(HEADS_DEV):
            vt_loc[h, 0:DH, cols] = vt[h * DH : (h + 1) * DH]

    coef = SCALE * LOG2E

    @pl.loop(0, TOK // SEG)
    def _(t):
        keys = pl.ds(pl.multiple_of(t * SEG, SEG), SEG)
        blocks = pl.ds(t * (SEG // BLOCK), SEG // BLOCK)
        for h in range(HEADS_DEV):
            k = k_ref[blocks, :, h * DH : (h + 1) * DH].reshape(SEG, DH)
            ka = jnp.concatenate([k, mk_loc[keys, :]], axis=1)
            vt = vt_loc[h, :, keys]
            for j in range(SEG // TILE):
                qs = pl.ds(pl.multiple_of(t * SEG + j * TILE, TILE), TILE)
                s = dot(ka, qa[h, qs, :], 1, 1)
                m = jnp.maximum(jnp.max(s, axis=0, keepdims=True), LOW)
                p = jnp.exp2((s - m) * coef).astype(BF16)
                p_loc[h, :, qs] = p
                m_run[h, :, qs] = m
                m_loc[h, :, qs] = m
                acc[h, :, qs] = dot(vt, p, 1, 0)

    gc[...] = jnp.transpose(jnp.broadcast_to(gain_ref[...], (DH, COLS)))
    for t in range(TOK // TILE):
        cols = slice(t * TILE, (t + 1) * TILE)
        gt[:, cols] = jnp.transpose(g_ref[cols, :].astype(F32))

    for i in range(TOK // DH):
        scaled = gt[:, i * DH : (i + 1) * DH] * gc[...]
        early[0, i : i + 1, :] = jnp.sum(scaled, axis=0, keepdims=True)

    def row_copy(buffer, lane, d):
        return pltpu.make_async_remote_copy(
            src_ref=buffer.at[0],
            dst_ref=buffer.at[d],
            send_sem=st_ss.at[lane, d],
            recv_sem=st_rs.at[lane, d],
            device_id=(me, lax.rem(col + d, N_HEAD)),
            device_id_type=MESH,
        )

    for d in range(1, N_HEAD):
        row_copy(early, 0, d).start()

    @pl.loop(0, TOK // BLOCK)
    def _(b):
        found = jnp.int32(-1)
        for slot in range(KEEP):
            off = kept[2, slot, me] - b
            found = jnp.maximum(found, (slot + 1) * (1 - jnp.minimum(off * off, 1)) - 1)
        inv_slot[b] = found

    @pl.loop(0, LEVELS * NCH)
    def _(t):
        level = 2 - lax.rem(t, 3)
        c = t // 3
        kv_copy(level, c).wait()

        @pl.when(t == LEVELS * NCH - 1)
        def _():
            for half in range(HALVES):
                q_copy(0, half).start()

        rows = pl.ds(pl.multiple_of(c * CHUNK, CHUNK), CHUNK)
        kt_far[level, :, rows] = turned(kv_in[level, rows, 0:COLS])
        vt = turned(kv_in[level, rows, COLS:])
        for h in range(HEADS_DEV):
            vt_far[level, h, 0:DH, rows] = vt[h * DH : (h + 1) * DH]
        for h in range(HEADS_DEV):
            ka = jnp.concatenate(
                [kv_in[level, rows, h * DH : (h + 1) * DH], mk_far[level, rows, :]], axis=1
            )
            vta = vt_far[level, h, :, rows]
            for j in range(TOK // TILE):
                qs = slice(j * TILE, (j + 1) * TILE)
                s = dot(ka, qa[h, qs, :], 1, 1)
                m_old = m_run[h, :, qs]
                m = jnp.maximum(jnp.max(s, axis=0, keepdims=True), m_old)
                p = jnp.exp2((s - m) * coef).astype(BF16)
                p_far[level, h, rows, qs] = p
                m_run[h, :, qs] = m
                m_far[level, c, h, :, qs] = m
                acc[h, :, qs] = acc[h, :, qs] * jnp.exp2((m_old - m) * coef) + dot(vta, p, 1, 0)

    for i in range(TOK // DH):
        qs = slice(i * DH, (i + 1) * DH)
        total = jnp.zeros((1, DH), F32)
        for h in range(HEADS_DEV):
            inv = 1.0 / acc[h, DH : DH + 1, qs]
            inv_l[h, :, qs] = inv
            a = (acc[h, 0:DH, qs] * inv).astype(BF16).astype(F32)
            at[h * DH : (h + 1) * DH, qs] = a
            total = total + jnp.sum(a, axis=0, keepdims=True)
        mean = total * (1.0 / COLS)
        centred = at[:, qs] - mean
        scaled = gt[:, qs] * gc[...]
        st[0, i : i + 1, 0:128] = mean
        st[0, i : i + 1, 128:256] = jnp.sum(centred * centred, axis=0, keepdims=True)
        st[0, i : i + 1, 256:384] = jnp.sum(scaled * centred, axis=0, keepdims=True)

    for d in (4, 3, 5, 2, 6, 1, 7):
        row_copy(st, 1, d).start()
    for d in range(1, N_HEAD):
        row_copy(early, 0, d).wait()
    for d in range(1, N_HEAD):
        row_copy(st, 1, d).wait()

    mean = st[0, :, 0:128]
    for d in range(1, N_HEAD):
        mean = mean + st[d, :, 0:128]
    mean = mean * (1.0 / N_HEAD)
    square = jnp.zeros((8, DH), F32)
    plain = jnp.zeros((8, DH), F32)
    cross = jnp.zeros((8, DH), F32)
    for d in range(N_HEAD):
        off = st[d, :, 0:128] - mean
        square = square + (st[d, :, 128:256] + COLS * (off * off))
        plain = plain + early[d]
        cross = cross + (st[d, :, 256:384] + off * early[d])
    inv_std = lax.rsqrt(square * (1.0 / WIDTH) + NORM_EPS)
    res[:, 0:128] = mean
    res[:, 128:256] = inv_std
    res[:, 256:384] = plain * (1.0 / WIDTH)
    res[:, 384:512] = inv_std * cross * (1.0 / WIDTH)

    gain_part = jnp.zeros((COLS, DH), F32)
    for i in range(TOK // DH):
        qs = slice(i * DH, (i + 1) * DH)
        inv_std = res[i : i + 1, 128:256]
        normed = (at[:, qs] - res[i : i + 1, 0:128]) * inv_std
        scaled = gt[:, qs] * gc[...]
        do = inv_std * (scaled - res[i : i + 1, 256:384] - normed * res[i : i + 1, 384:512])
        do = do.astype(BF16)
        dot_[:, qs] = do
        gain_part = gain_part + gt[:, qs] * normed
        both = do.astype(F32) * at[:, qs]
        for h in range(HEADS_DEV):
            delta[h, :, qs] = jnp.sum(both[h * DH : (h + 1) * DH], axis=0, keepdims=True)
        log_l = jnp.log(acc[1, DH : DH + 1, qs])
        rows_out[i : i + 1, 0:DH] = m_run[1, :, qs] + log_l * (1.0 / SCALE)
        rows_out[i : i + 1, DH:] = delta[1, :, qs]

    def back(h, qs, parts, v, kt, whole=True):
        probs = jnp.concatenate(
            [
                p.astype(F32) * (jnp.exp2((m - m_run[h, :, qs]) * coef) * inv_l[h, :, qs])
                for p, m in parts
            ],
            axis=0,
        )
        do = dot_[h * DH : (h + 1) * DH, qs]
        dp = dot(v, do, 1, 0)
        ds = (probs * (dp - delta[h, :, qs])).astype(BF16)
        dq = dot(kt, ds, 1, 0)
        if not whole:
            return dq, None, None
        dk = dot(ds, qa[h, qs, 0:DH], 1, 0)
        dv = dot(probs.astype(BF16), do, 1, 1)
        return dq, dk, dv

    dqt[...] = jnp.zeros_like(dqt)

    gsum[0] = jnp.broadcast_to(jnp.sum(jnp.transpose(gain_part), axis=0, keepdims=True), (8, COLS))

    def gg_copy(stage):
        flip, src, dst = ((1, 0, 1), (2, 0, 2), (3, 0, 3), (4, 4, 5), (8, 6, 7))[stage]
        return pltpu.make_async_remote_copy(
            src_ref=gsum.at[src],
            dst_ref=gsum.at[dst],
            send_sem=gg_ss.at[stage],
            recv_sem=gg_rs.at[stage],
            device_id=(beside if flip == 3 else flipped(me, flip), col),
            device_id_type=MESH,
        )

    for stage in range(3):
        gg_copy(stage).start()
    for level in range(2):
        rows_copy(level).start()
    for c in range(HALVES):
        do_copy(0, c).start()

    def back_level(level, h, whole):
        hs = slice(h * DH, (h + 1) * DH)
        v = kv_in[level, :, COLS + h * DH : COLS + (h + 1) * DH]
        kt = kt_far[level, hs, :]
        dk_sum = jnp.zeros((KEPT, DH), F32)
        dv_sum = jnp.zeros((KEPT, DH), F32)
        for j in range(TOK // TILE):
            qs = slice(j * TILE, (j + 1) * TILE)
            parts = [
                (p_far[level, h, c * CHUNK : (c + 1) * CHUNK, qs], m_far[level, c, h, :, qs])
                for c in range(NCH)
            ]
            dq, dk, dv = back(h, qs, parts, v, kt, whole)
            dqt[hs, qs] += dq
            if whole:
                dk_sum = dk_sum + dk
                dv_sum = dv_sum + dv
        if whole:
            keep_grads(level, h, dk_sum, dv_sum)

    def keep_grads(level, h, dk_sum, dv_sum):
        shape = (KEEP, BLOCK, DH)
        gr_out[level, h, :, :, 0:DH] = (dk_sum * SCALE).astype(BF16).reshape(shape)
        gr_out[level, h, :, :, DH:] = dv_sum.astype(BF16).reshape(shape)

    back_level(0, 0, True)
    for c in range(HALVES):
        q_copy(0, c).wait()
        q_copy(1, c).start()
    gr_copy(0, 0).start()
    back_level(2, 0, True)
    for stage in range(3):
        gg_copy(stage).wait()
    gsum[4] = (gsum[0] + gsum[1]) + (gsum[2] + gsum[3])
    gg_copy(3).start()
    gr_copy(2, 0).start()
    back_level(1, 0, True)
    do_copy(0, 0).wait()
    do_copy(1, 0).start()
    gr_copy(1, 0).start()
    back_level(2, 1, True)
    do_copy(0, 1).wait()
    do_copy(1, 1).start()
    gg_copy(3).wait()
    gsum[6] = gsum[4] + gsum[5]
    gg_copy(4).start()
    gr_copy(2, 1).start()

    @pl.loop(0, 2)
    def _(level):
        back_level(level, 1, False)

    for i in range(TOK // DH):
        qs = slice(i * DH, (i + 1) * DH)
        normed = (at[:, qs] - res[i : i + 1, 0:128]) * res[i : i + 1, 128:256]
        lo_ref[qs, :] = jnp.transpose(normed * gc[...]).astype(BF16)
    lo_copy = pltpu.make_async_copy(lo_ref, lo_hbm, io.at[0])
    lo_copy.start()

    @pl.loop(0, TOK // SEG)
    def _(t):
        keys = pl.ds(pl.multiple_of(t * SEG, SEG), SEG)
        blocks = pl.ds(t * (SEG // BLOCK), SEG // BLOCK)
        for h in range(HEADS_DEV):
            hs = slice(h * DH, (h + 1) * DH)
            v = v_ref[blocks, :, hs].reshape(SEG, DH)
            kt = kt_loc[hs, keys]
            dk_sum = jnp.zeros((SEG, DH), F32)
            dv_sum = jnp.zeros((SEG, DH), F32)
            for j in range(SEG // TILE):
                qs = pl.ds(pl.multiple_of(t * SEG + j * TILE, TILE), TILE)
                dq, dk, dv = back(h, qs, [(p_loc[h, :, qs], m_loc[h, :, qs])], v, kt)
                dqt[hs, qs] += dq
                dk_sum = dk_sum + dk
                dv_sum = dv_sum + dv
            dkv[keys, hs] = dk_sum * SCALE
            dkv[keys, COLS + h * DH : COLS + (h + 1) * DH] = dv_sum

    for t in range(TOK // TILE):
        cols = slice(t * TILE, (t + 1) * TILE)
        dq_ref[cols, :] = jnp.transpose(dqt[:, cols] * SCALE).astype(BF16)
    dq_copy = pltpu.make_async_copy(dq_ref, dq_hbm, io.at[1])
    dq_copy.start()
    gg_copy(4).wait()
    gg_ref[...] = gsum[6, 0:1, :] + gsum[7, 0:1, :]

    for h in range(HEADS_DEV):
        gr_copy(2, h).wait()

    @pl.loop(0, TOK // BLOCK)
    def _(b):
        slot = inv_slot[b]
        rows = pl.ds(pl.multiple_of(b * BLOCK, BLOCK), BLOCK)
        used = jnp.minimum(slot + 1, 1).astype(F32)
        for h in range(HEADS_DEV):
            part = gr_in2[h, jnp.maximum(slot, 0)].astype(F32) * used
            dkv[rows, h * DH : (h + 1) * DH] += part[:, 0:DH]
            dkv[rows, COLS + h * DH : COLS + (h + 1) * DH] += part[:, DH:]

    part_copy = pltpu.make_async_copy(dkv, part_hbm, io.at[2])
    part_copy.start()

    def own_copy(level):
        return pltpu.make_async_copy(gr_out.at[level, 1], gr_hbm.at[level, 1], io.at[3 + level])

    @pl.loop(0, 2)
    def _(level):
        for one in range(2):

            @pl.when(level == one)
            def _():
                rows_copy(one).wait()
                if one == 1:
                    for c in range(HALVES):
                        q_copy(1, c).wait()
                        do_copy(1, c).wait()

        ka = jnp.concatenate([kv_out[level, :, DH:COLS], mk_own[level]], axis=1)
        v = kv_out[level, :, COLS + DH :]
        dk_sum = jnp.zeros((KEPT, DH), F32)
        dv_sum = jnp.zeros((KEPT, DH), F32)
        for j in range(TOK // TILE):
            qs = slice(j * TILE, (j + 1) * TILE)
            pieces = range(j * (TILE // DH), (j + 1) * (TILE // DH))
            logs = jnp.concatenate([rows_in[level, i : i + 1, 0:DH] for i in pieces], axis=1)
            deltas = jnp.concatenate([rows_in[level, i : i + 1, DH:] for i in pieces], axis=1)
            q = q_in[level, qs, :]
            do = do_in[level, :, qs]
            s = dot(ka, jnp.concatenate([q, mq_far[level, qs, :]], axis=1), 1, 1)
            probs = jnp.exp2((s - logs) * coef)
            ds = (probs * (dot(v, do, 1, 0) - deltas)).astype(BF16)
            dk_sum = dk_sum + dot(ds, q, 1, 0)
            dv_sum = dv_sum + dot(probs.astype(BF16), do, 1, 1)
        keep_grads(level, 1, dk_sum, dv_sum)
        for one in range(2):
            pl.when(level == one)(lambda one=one: own_copy(one).start())

    for level in range(2):
        gr_copy(level, 0).wait()
    for level in range(2):
        own_copy(level).wait()
    lo_copy.wait()
    dq_copy.wait()
    part_copy.wait()


def finish(
    kept_hbm,
    lo_in,
    dq_in,
    part_in,
    gr_in,
    gg_in,
    lo_ref,
    dq_ref,
    dk_ref,
    dv_ref,
    gg_ref,
    kept,
    dk,
    dv,
    sems,
    few,
):
    me = lax.axis_index("seq")
    kept_copy = pltpu.make_async_copy(kept_hbm, kept, few.at[0])
    kept_copy.start()
    copies = [pltpu.make_async_copy(gg_in, gg_ref, few.at[1])]
    copies[0].start()

    def send(src, dst, i, lane):
        rows = pl.ds(i * TILE, TILE)
        copy = pltpu.make_async_copy(src.at[rows], dst.at[rows], sems.at[lane, i])
        copy.start()
        copies.append(copy)

    for i in range(TOK // TILE):
        send(lo_in, lo_ref, i, 0)
        send(dq_in, dq_ref, i, 1)
    kept_copy.wait()
    for i in range(TOK // TILE):
        for b in range(i * (TILE // BLOCK), (i + 1) * (TILE // BLOCK)):
            rows = slice(b * BLOCK, (b + 1) * BLOCK)
            total = part_in[rows, :]
            key = [total[:, h * DH : (h + 1) * DH] for h in range(HEADS_DEV)]
            value = [total[:, COLS + h * DH : COLS + (h + 1) * DH] for h in range(HEADS_DEV)]
            for level in range(2):
                found = jnp.int32(-1)
                for slot in range(KEEP):
                    found = jnp.where(kept[level, slot, me] == b, jnp.int32(slot), found)
                used = jnp.minimum(found + 1, 1).astype(F32)
                for h in range(HEADS_DEV):
                    part = gr_in[level, h, jnp.maximum(found, 0)].astype(F32) * used
                    key[h] = key[h] + part[:, 0:DH]
                    value[h] = value[h] + part[:, DH:]
            for h in range(HEADS_DEV):
                dk[rows, h * DH : (h + 1) * DH] = key[h].astype(BF16)
                dv[rows, h * DH : (h + 1) * DH] = value[h].astype(BF16)
        send(dk, dk_ref, i, 2)
        send(dv, dv_ref, i, 3)
    for copy in copies:
        copy.wait()


def local(query_rows, key_rows, value_rows, norm_gain, grad_out, doc_lengths, kept_blocks):
    vmem = pl.BlockSpec(memory_space=pltpu.VMEM)
    smem = pl.BlockSpec(memory_space=pltpu.SMEM)
    hbm = pl.BlockSpec(memory_space=pltpu.HBM)
    some = pl.BlockSpec(memory_space=pl.ANY)
    rows = jax.ShapeDtypeStruct((TOK, COLS), BF16)
    dma = pltpu.SemaphoreType.DMA
    scratch = [
        pltpu.SMEM((LEVELS, KEEP, N_SEQ), jnp.int32),
        pltpu.VMEM((TOK, COLS), BF16),
        pltpu.VMEM((TOK // BLOCK, BLOCK, COLS), BF16),
        pltpu.VMEM((TOK // BLOCK, BLOCK, COLS), BF16),
        pltpu.VMEM((1, COLS), F32),
        pltpu.VMEM((TOK, COLS), BF16),
        pltpu.VMEM((TOK, COLS), BF16),
        pltpu.VMEM((TOK, COLS), BF16),
        pltpu.VMEM((HEADS_DEV, TOK, 2 * DH), BF16),
        pltpu.VMEM((TOK, DH), BF16),
        pltpu.VMEM((LEVELS, KEPT, DH), BF16),
        pltpu.VMEM((LEVELS, KEPT, 2 * COLS), BF16),
        pltpu.VMEM((LEVELS, KEPT, 2 * COLS), BF16),
        pltpu.VMEM((LEVELS, HEADS_DEV, KEEP, BLOCK, 2 * DH), BF16),
        pltpu.VMEM((HEADS_DEV, KEEP, BLOCK, 2 * DH), BF16),
        pltpu.VMEM((COLS, TOK), BF16),
        pltpu.VMEM((HEADS_DEV, DH + 16, TOK), BF16),
        pltpu.VMEM((LEVELS, COLS, KEPT), BF16),
        pltpu.VMEM((LEVELS, HEADS_DEV, DH + 16, KEPT), BF16),
        pltpu.VMEM((HEADS_DEV, SEG, TOK), BF16),
        pltpu.VMEM((LEVELS, HEADS_DEV, KEPT, TOK), BF16),
        pltpu.VMEM((HEADS_DEV, 1, TOK), F32),
        pltpu.VMEM((HEADS_DEV, 1, TOK), F32),
        pltpu.VMEM((LEVELS, NCH, HEADS_DEV, 1, TOK), F32),
        pltpu.VMEM((HEADS_DEV, DH + 16, TOK), F32),
        pltpu.VMEM((HEADS_DEV, 1, TOK), F32),
        pltpu.VMEM((COLS, TOK), F32),
        pltpu.VMEM((COLS, TOK), F32),
        pltpu.VMEM((COLS, DH), F32),
        pltpu.VMEM((N_HEAD, 8, 384), F32),
        pltpu.VMEM((N_HEAD, 8, DH), F32),
        pltpu.VMEM((8, 512), F32),
        pltpu.VMEM((COLS, TOK), BF16),
        pltpu.VMEM((HEADS_DEV, 1, TOK), F32),
        pltpu.VMEM((COLS, TOK), F32),
        pltpu.VMEM((TOK, 2 * COLS), F32),
        pltpu.VMEM((8, 8, COLS), F32),
        pltpu.SMEM((TOK // BLOCK,), jnp.int32),
        pltpu.VMEM((2, TOK, DH), BF16),
        pltpu.VMEM((2, KEPT, DH), BF16),
        pltpu.VMEM((2, TOK, DH), BF16),
        pltpu.VMEM((2, DH, TOK), BF16),
        pltpu.VMEM((8, 2 * DH), F32),
        pltpu.VMEM((2, 8, 2 * DH), F32),
        dma((2, HALVES)),
        dma((2, HALVES)),
        dma((2, HALVES)),
        dma((2, HALVES)),
        dma((2,)),
        dma((2,)),
        dma((LEVELS, NCH)),
        dma((LEVELS, NCH)),
        dma((LEVELS, HEADS_DEV)),
        dma((LEVELS, HEADS_DEV)),
        dma((2, N_HEAD)),
        dma((2, N_HEAD)),
        dma((5,)),
        dma((5,)),
        dma((18,)),
    ]
    kept = jnp.transpose(kept_blocks, (1, 2, 0))
    gain_row = jax.ShapeDtypeStruct((1, COLS), F32)
    lo, dq, part, returned, gain = pl.pallas_call(
        kernel,
        out_shape=[
            pltpu.VMEM((TOK, COLS), BF16),
            pltpu.VMEM((TOK, COLS), BF16),
            pltpu.VMEM((TOK, 2 * COLS), F32),
            pltpu.VMEM((2, HEADS_DEV, KEEP, BLOCK, 2 * DH), BF16),
            pltpu.VMEM((1, COLS), F32),
        ],
        in_specs=[hbm, smem] + [hbm] * 5,
        out_specs=[some] * 4 + [vmem],
        scratch_shapes=scratch,
        compiler_params=pltpu.CompilerParams(
            collective_id=0, has_side_effects=True, vmem_limit_bytes=44 * 1024 * 1024
        ),
        name="attention",
    )(
        *(
            pltpu.with_memory_space_constraint(x, pltpu.HBM)
            for x in (
                kept,
                doc_lengths,
                query_rows,
                key_rows.reshape(TOK // BLOCK, BLOCK, COLS),
                value_rows.reshape(TOK // BLOCK, BLOCK, COLS),
                norm_gain.reshape(1, COLS),
                grad_out,
            )
        )
    )
    lo, dq, dk, dv, gain = pl.pallas_call(
        finish,
        out_shape=[rows, rows, rows, rows, gain_row],
        in_specs=[hbm] + [vmem] * 5,
        out_specs=[hbm] * 5,
        scratch_shapes=[
            pltpu.SMEM((LEVELS, KEEP, N_SEQ), jnp.int32),
            pltpu.VMEM((TOK, COLS), BF16),
            pltpu.VMEM((TOK, COLS), BF16),
            dma((4, TOK // TILE)),
            dma((2,)),
        ],
        compiler_params=pltpu.CompilerParams(vmem_limit_bytes=12 * 1024 * 1024),
        name="finish",
    )(pltpu.with_memory_space_constraint(kept, pltpu.HBM), lo, dq, part, returned, gain)
    return lo, dq, dk, dv, gain.reshape(COLS)


def solution(mesh):
    rows = P("seq", "head")
    in_specs = (rows, rows, rows, P("head"), rows, P(), P())
    out_specs = (rows, rows, rows, rows, P("head"))
    return jax.shard_map(local, mesh=mesh, in_specs=in_specs, out_specs=out_specs, check_vma=False)
```

```python
import functools

import jax
import jax.numpy as jnp
from jax import lax
from jax.experimental import pallas as pl
from jax.experimental.pallas import tpu as pltpu
from jax.sharding import PartitionSpec as P

DH = 128
TOK = 1024
SEG = 512
BLOCK = 64
KEEP = 8
LEVELS = 3
KEPT = KEEP * BLOCK
CHUNK = 256
NCH = KEPT // CHUNK
TILE = 256
WIDTH = 2048
HALVES = 2
HEADS_DEV = 2
COLS = HEADS_DEV * DH
N_SEQ = 16
N_HEAD = 8
NORM_EPS = 1e-05
SCALE = DH**-0.5
LOG2E = 1.4426950408889634
BIG = 2.0**100
LOW = -(2.0**99)
MESH = pl.DeviceIdType.MESH
F32 = jnp.float32
BF16 = jnp.bfloat16


def dot(a, b, ca, cb):
    return lax.dot_general(a, b, (((ca,), (cb,)), ((), ())), preferred_element_type=F32)


def turned(x):
    return jnp.transpose(x.astype(F32)).astype(x.dtype)


def flipped(index, bit):
    return index + bit * (1 - 2 * lax.rem(index // bit, 2))


def level_bit(level):
    return 1 + level + level // 2


def kernel(
    kept_hbm,
    lengths_hbm,
    q_hbm,
    k_hbm,
    v_hbm,
    gain_hbm,
    g_hbm,
    lo_hbm,
    dq_hbm,
    part_hbm,
    gr_hbm,
    gg_ref,
    kept,
    lengths,
    q_ref,
    k_ref,
    v_ref,
    gain_ref,
    g_ref,
    lo_ref,
    dq_ref,
    qa,
    mk_loc,
    mk_far,
    kv_out,
    kv_in,
    gr_out,
    gr_in2,
    kt_loc,
    vt_loc,
    kt_far,
    vt_far,
    p_loc,
    p_far,
    m_run,
    m_loc,
    m_far,
    acc,
    inv_l,
    at,
    gt,
    gc,
    st,
    early,
    res,
    dot_,
    delta,
    dqt,
    dkv,
    gsum,
    inv_slot,
    mq_far,
    mk_own,
    q_in,
    do_in,
    rows_out,
    rows_in,
    q_ss,
    q_rs,
    do_ss,
    do_rs,
    ro_ss,
    ro_rs,
    kv_ss,
    kv_rs,
    gr_ss,
    gr_rs,
    st_ss,
    st_rs,
    gg_ss,
    gg_rs,
    io,
):
    me = lax.axis_index("seq")
    col = lax.axis_index("head")

    barrier = pltpu.get_barrier_semaphore()
    beside = flipped(flipped(me, 1), 2)
    for other in [flipped(me, bit) for bit in (1, 2, 4, 8)] + [beside]:
        pl.semaphore_signal(barrier, inc=1, device_id=(other, col), device_id_type=MESH)
    for d in range(1, N_HEAD):
        pl.semaphore_signal(
            barrier, inc=1, device_id=(me, lax.rem(col + d, N_HEAD)), device_id_type=MESH
        )

    def load(src, dst, pieces, first):
        size = src.shape[0] // pieces
        copies = []
        for i in range(pieces):
            rows = pl.ds(i * size, size)
            copies.append(pltpu.make_async_copy(src.at[rows], dst.at[rows], io.at[first + i]))
            copies[-1].start()
        return copies

    loads = load(k_hbm, k_ref, 4, 0) + load(v_hbm, v_ref, 4, 4) + load(kept_hbm, kept, 1, 8)
    later = load(q_hbm, q_ref, 4, 9) + load(g_hbm, g_ref, 4, 13) + load(gain_hbm, gain_ref, 1, 17)
    lengths_copy = pltpu.make_async_copy(lengths_hbm, lengths, io.at[18])
    lengths_copy.start()
    for copy in loads:
        copy.wait()

    def kv_copy(level, c):
        rows = pl.ds(pl.multiple_of(c * CHUNK, CHUNK), CHUNK)
        return pltpu.make_async_remote_copy(
            src_ref=kv_out.at[level, rows],
            dst_ref=kv_in.at[level, rows],
            send_sem=kv_ss.at[level, c],
            recv_sem=kv_rs.at[level, c],
            device_id=(flipped(me, level_bit(level)), col),
            device_id_type=MESH,
        )

    def gr_copy(level, h):
        dst = gr_in2 if level == 2 else gr_hbm.at[level]
        return pltpu.make_async_remote_copy(
            src_ref=gr_out.at[level, h],
            dst_ref=dst.at[h],
            send_sem=gr_ss.at[level, h],
            recv_sem=gr_rs.at[level, h],
            device_id=(flipped(me, level_bit(level)), col),
            device_id_type=MESH,
        )

    def q_copy(hop, c):
        qs = pl.ds(c * (TOK // HALVES), TOK // HALVES)
        return pltpu.make_async_remote_copy(
            src_ref=q_in.at[0, qs] if hop else q_ref.at[qs, pl.ds(DH, DH)],
            dst_ref=q_in.at[hop, qs],
            send_sem=q_ss.at[hop, c],
            recv_sem=q_rs.at[hop, c],
            device_id=(beside if hop else flipped(me, 1), col),
            device_id_type=MESH,
        )

    def do_copy(hop, c):
        qs = pl.ds(c * (TOK // HALVES), TOK // HALVES)
        return pltpu.make_async_remote_copy(
            src_ref=do_in.at[0, :, qs] if hop else dot_.at[pl.ds(DH, DH), qs],
            dst_ref=do_in.at[hop, :, qs],
            send_sem=do_ss.at[hop, c],
            recv_sem=do_rs.at[hop, c],
            device_id=(beside if hop else flipped(me, 1), col),
            device_id_type=MESH,
        )

    def rows_copy(level):
        return pltpu.make_async_remote_copy(
            src_ref=rows_out,
            dst_ref=rows_in.at[level],
            send_sem=ro_ss.at[level],
            recv_sem=ro_rs.at[level],
            device_id=(flipped(me, 1 << level), col),
            device_id_type=MESH,
        )

    for c in range(NCH):
        for level in (1, 0, 2):
            for slot in range(c * KEEP // NCH, (c + 1) * KEEP // NCH):
                block = jnp.maximum(kept[level, slot, me], 0)
                kv_out[level, slot * BLOCK : (slot + 1) * BLOCK, 0:COLS] = k_ref[block]
                kv_out[level, slot * BLOCK : (slot + 1) * BLOCK, COLS:] = v_ref[block]
            if c == 0 and level == 1:
                pl.semaphore_wait(barrier, 5 + N_HEAD - 1)
            kv_copy(level, c).start()

    lengths_copy.wait()
    for copy in later:
        copy.wait()
    start1 = lengths[0]
    start2 = lengths[0] + lengths[1]

    def doc_of(pos):
        return (pos >= start1).astype(jnp.int32) + (pos >= start2).astype(jnp.int32)

    lane = lax.broadcasted_iota(jnp.int32, (BLOCK, DH), 1)
    row = lax.broadcasted_iota(jnp.int32, (BLOCK, DH), 0)
    for b in range(TOK // BLOCK):
        rows = slice(b * BLOCK, (b + 1) * BLOCK)
        docs = doc_of(me * TOK + b * BLOCK + row)
        same = docs == lane
        mq = jnp.where(same, 1.0, 0.0).astype(BF16)
        mk_loc[rows, :] = jnp.where(same | (lane >= 3), 0.0, -BIG).astype(BF16)
        for h in range(HEADS_DEV):
            qa[h, rows, DH:] = mq
            qa[h, rows, 0:DH] = q_ref[rows, h * DH : (h + 1) * DH]
    for level in range(LEVELS):
        partner = flipped(me, level_bit(level))
        for slot in range(KEEP):
            listed = kept[level, slot, partner]
            docs = doc_of(partner * TOK + jnp.maximum(listed, 0) * BLOCK + row)
            docs = docs - 3 * jnp.minimum(listed, 0)
            same = docs == lane
            mk_far[level, slot * BLOCK : (slot + 1) * BLOCK, :] = jnp.where(
                same | (lane >= 3), 0.0, -BIG
            ).astype(BF16)

    for level in range(2):
        partner = flipped(me, level_bit(level))
        for b in range(TOK // BLOCK):
            same = doc_of(partner * TOK + b * BLOCK + row) == lane
            mq_far[level, b * BLOCK : (b + 1) * BLOCK, :] = jnp.where(same, 1.0, 0.0).astype(BF16)
        for slot in range(KEEP):
            listed = kept[level, slot, me]
            docs = doc_of(me * TOK + jnp.maximum(listed, 0) * BLOCK + row)
            docs = docs - 3 * jnp.minimum(listed, 0)
            mk_own[level, slot * BLOCK : (slot + 1) * BLOCK, :] = jnp.where(
                (docs == lane) | (lane >= 3), 0.0, -BIG
            ).astype(BF16)

    ones = jnp.ones((16, TOK), BF16)
    for h in range(HEADS_DEV):
        vt_loc[h, DH:, :] = ones
        for level in range(LEVELS):
            vt_far[level, h, DH:, :] = ones[:, 0:KEPT]

    for t in range(TOK // TILE):
        cols = slice(t * TILE, (t + 1) * TILE)
        blocks = slice(t * (TILE // BLOCK), (t + 1) * (TILE // BLOCK))
        kt_loc[:, cols] = turned(k_ref[blocks].reshape(TILE, COLS))
        vt = turned(v_ref[blocks].reshape(TILE, COLS))
        for h in range(HEADS_DEV):
            vt_loc[h, 0:DH, cols] = vt[h * DH : (h + 1) * DH]

    coef = SCALE * LOG2E

    @pl.loop(0, TOK // SEG)
    def _(t):
        keys = pl.ds(pl.multiple_of(t * SEG, SEG), SEG)
        blocks = pl.ds(t * (SEG // BLOCK), SEG // BLOCK)
        for h in range(HEADS_DEV):
            k = k_ref[blocks, :, h * DH : (h + 1) * DH].reshape(SEG, DH)
            ka = jnp.concatenate([k, mk_loc[keys, :]], axis=1)
            vt = vt_loc[h, :, keys]
            for j in range(SEG // TILE):
                qs = pl.ds(pl.multiple_of(t * SEG + j * TILE, TILE), TILE)
                s = dot(ka, qa[h, qs, :], 1, 1)
                m = jnp.maximum(jnp.max(s, axis=0, keepdims=True), LOW)
                p = jnp.exp2((s - m) * coef).astype(BF16)
                p_loc[h, :, qs] = p
                m_run[h, :, qs] = m
                m_loc[h, :, qs] = m
                acc[h, :, qs] = dot(vt, p, 1, 0)

    gc[...] = jnp.transpose(jnp.broadcast_to(gain_ref[...], (DH, COLS)))
    for t in range(TOK // TILE):
        cols = slice(t * TILE, (t + 1) * TILE)
        gt[:, cols] = jnp.transpose(g_ref[cols, :].astype(F32))

    for i in range(TOK // DH):
        scaled = gt[:, i * DH : (i + 1) * DH] * gc[...]
        early[0, i : i + 1, :] = jnp.sum(scaled, axis=0, keepdims=True)

    def row_copy(buffer, lane, d):
        return pltpu.make_async_remote_copy(
            src_ref=buffer.at[0],
            dst_ref=buffer.at[d],
            send_sem=st_ss.at[lane, d],
            recv_sem=st_rs.at[lane, d],
            device_id=(me, lax.rem(col + d, N_HEAD)),
            device_id_type=MESH,
        )

    for d in range(1, N_HEAD):
        row_copy(early, 0, d).start()

    @pl.loop(0, TOK // BLOCK)
    def _(b):
        found = jnp.int32(-1)
        for slot in range(KEEP):
            off = kept[2, slot, me] - b
            found = jnp.maximum(found, (slot + 1) * (1 - jnp.minimum(off * off, 1)) - 1)
        inv_slot[b] = found

    @pl.loop(0, LEVELS * NCH)
    def _(t):
        level = 2 - lax.rem(t, 3)
        c = t // 3
        kv_copy(level, c).wait()

        @pl.when(t == LEVELS * NCH - 1)
        def _():
            for half in range(HALVES):
                q_copy(0, half).start()

        rows = pl.ds(pl.multiple_of(c * CHUNK, CHUNK), CHUNK)
        kt_far[level, :, rows] = turned(kv_in[level, rows, 0:COLS])
        vt = turned(kv_in[level, rows, COLS:])
        for h in range(HEADS_DEV):
            vt_far[level, h, 0:DH, rows] = vt[h * DH : (h + 1) * DH]
        for h in range(HEADS_DEV):
            ka = jnp.concatenate(
                [kv_in[level, rows, h * DH : (h + 1) * DH], mk_far[level, rows, :]], axis=1
            )
            vta = vt_far[level, h, :, rows]
            for j in range(TOK // TILE):
                qs = slice(j * TILE, (j + 1) * TILE)
                s = dot(ka, qa[h, qs, :], 1, 1)
                m_old = m_run[h, :, qs]
                m = jnp.maximum(jnp.max(s, axis=0, keepdims=True), m_old)
                p = jnp.exp2((s - m) * coef).astype(BF16)
                p_far[level, h, rows, qs] = p
                m_run[h, :, qs] = m
                m_far[level, c, h, :, qs] = m
                acc[h, :, qs] = acc[h, :, qs] * jnp.exp2((m_old - m) * coef) + dot(vta, p, 1, 0)

    for i in range(TOK // DH):
        qs = slice(i * DH, (i + 1) * DH)
        total = jnp.zeros((1, DH), F32)
        for h in range(HEADS_DEV):
            inv = 1.0 / acc[h, DH : DH + 1, qs]
            inv_l[h, :, qs] = inv
            a = (acc[h, 0:DH, qs] * inv).astype(BF16).astype(F32)
            at[h * DH : (h + 1) * DH, qs] = a
            total = total + jnp.sum(a, axis=0, keepdims=True)
        mean = total * (1.0 / COLS)
        centred = at[:, qs] - mean
        scaled = gt[:, qs] * gc[...]
        st[0, i : i + 1, 0:128] = mean
        st[0, i : i + 1, 128:256] = jnp.sum(centred * centred, axis=0, keepdims=True)
        st[0, i : i + 1, 256:384] = jnp.sum(scaled * centred, axis=0, keepdims=True)

    for d in (4, 3, 5, 2, 6, 1, 7):
        row_copy(st, 1, d).start()
    for d in range(1, N_HEAD):
        row_copy(early, 0, d).wait()
    for d in range(1, N_HEAD):
        row_copy(st, 1, d).wait()

    mean = st[0, :, 0:128]
    for d in range(1, N_HEAD):
        mean = mean + st[d, :, 0:128]
    mean = mean * (1.0 / N_HEAD)
    square = jnp.zeros((8, DH), F32)
    plain = jnp.zeros((8, DH), F32)
    cross = jnp.zeros((8, DH), F32)
    for d in range(N_HEAD):
        off = st[d, :, 0:128] - mean
        square = square + (st[d, :, 128:256] + COLS * (off * off))
        plain = plain + early[d]
        cross = cross + (st[d, :, 256:384] + off * early[d])
    inv_std = lax.rsqrt(square * (1.0 / WIDTH) + NORM_EPS)
    res[:, 0:128] = mean
    res[:, 128:256] = inv_std
    res[:, 256:384] = plain * (1.0 / WIDTH)
    res[:, 384:512] = inv_std * cross * (1.0 / WIDTH)

    gain_part = jnp.zeros((COLS, DH), F32)
    for i in range(TOK // DH):
        qs = slice(i * DH, (i + 1) * DH)
        inv_std = res[i : i + 1, 128:256]
        normed = (at[:, qs] - res[i : i + 1, 0:128]) * inv_std
        scaled = gt[:, qs] * gc[...]
        do = inv_std * (scaled - res[i : i + 1, 256:384] - normed * res[i : i + 1, 384:512])
        do = do.astype(BF16)
        dot_[:, qs] = do
        gain_part = gain_part + gt[:, qs] * normed
        both = do.astype(F32) * at[:, qs]
        for h in range(HEADS_DEV):
            delta[h, :, qs] = jnp.sum(both[h * DH : (h + 1) * DH], axis=0, keepdims=True)
        log_l = jnp.log(acc[1, DH : DH + 1, qs])
        rows_out[i : i + 1, 0:DH] = m_run[1, :, qs] + log_l * (1.0 / SCALE)
        rows_out[i : i + 1, DH:] = delta[1, :, qs]

    def back(h, qs, parts, v, kt, whole=True):
        probs = jnp.concatenate(
            [
                p.astype(F32) * (jnp.exp2((m - m_run[h, :, qs]) * coef) * inv_l[h, :, qs])
                for p, m in parts
            ],
            axis=0,
        )
        do = dot_[h * DH : (h + 1) * DH, qs]
        dp = dot(v, do, 1, 0)
        ds = (probs * (dp - delta[h, :, qs])).astype(BF16)
        dq = dot(kt, ds, 1, 0)
        if not whole:
            return dq, None, None
        dk = dot(ds, qa[h, qs, 0:DH], 1, 0)
        dv = dot(probs.astype(BF16), do, 1, 1)
        return dq, dk, dv

    dqt[...] = jnp.zeros_like(dqt)

    gsum[0] = jnp.broadcast_to(jnp.sum(jnp.transpose(gain_part), axis=0, keepdims=True), (8, COLS))

    def gg_copy(stage):
        flip, src, dst = ((1, 0, 1), (2, 0, 2), (3, 0, 3), (4, 4, 5), (8, 6, 7))[stage]
        return pltpu.make_async_remote_copy(
            src_ref=gsum.at[src],
            dst_ref=gsum.at[dst],
            send_sem=gg_ss.at[stage],
            recv_sem=gg_rs.at[stage],
            device_id=(beside if flip == 3 else flipped(me, flip), col),
            device_id_type=MESH,
        )

    for stage in range(3):
        gg_copy(stage).start()
    for level in range(2):
        rows_copy(level).start()
    for c in range(HALVES):
        do_copy(0, c).start()

    def back_level(level, h, whole):
        hs = slice(h * DH, (h + 1) * DH)
        v = kv_in[level, :, COLS + h * DH : COLS + (h + 1) * DH]
        kt = kt_far[level, hs, :]
        dk_sum = jnp.zeros((KEPT, DH), F32)
        dv_sum = jnp.zeros((KEPT, DH), F32)
        for j in range(TOK // TILE):
            qs = slice(j * TILE, (j + 1) * TILE)
            parts = [
                (p_far[level, h, c * CHUNK : (c + 1) * CHUNK, qs], m_far[level, c, h, :, qs])
                for c in range(NCH)
            ]
            dq, dk, dv = back(h, qs, parts, v, kt, whole)
            dqt[hs, qs] += dq
            if whole:
                dk_sum = dk_sum + dk
                dv_sum = dv_sum + dv
        if whole:
            keep_grads(level, h, dk_sum, dv_sum)

    def keep_grads(level, h, dk_sum, dv_sum):
        shape = (KEEP, BLOCK, DH)
        gr_out[level, h, :, :, 0:DH] = (dk_sum * SCALE).astype(BF16).reshape(shape)
        gr_out[level, h, :, :, DH:] = dv_sum.astype(BF16).reshape(shape)

    back_level(0, 0, True)
    for c in range(HALVES):
        q_copy(0, c).wait()
        q_copy(1, c).start()
    gr_copy(0, 0).start()
    back_level(2, 0, True)
    for stage in range(3):
        gg_copy(stage).wait()
    gsum[4] = (gsum[0] + gsum[1]) + (gsum[2] + gsum[3])
    gg_copy(3).start()
    gr_copy(2, 0).start()
    back_level(1, 0, True)
    do_copy(0, 0).wait()
    do_copy(1, 0).start()
    gr_copy(1, 0).start()
    back_level(2, 1, True)
    do_copy(0, 1).wait()
    do_copy(1, 1).start()
    gg_copy(3).wait()
    gsum[6] = gsum[4] + gsum[5]
    gg_copy(4).start()
    gr_copy(2, 1).start()

    @pl.loop(0, 2)
    def _(level):
        back_level(level, 1, False)

    for i in range(TOK // DH):
        qs = slice(i * DH, (i + 1) * DH)
        normed = (at[:, qs] - res[i : i + 1, 0:128]) * res[i : i + 1, 128:256]
        lo_ref[qs, :] = jnp.transpose(normed * gc[...]).astype(BF16)
    lo_copy = pltpu.make_async_copy(lo_ref, lo_hbm, io.at[0])
    lo_copy.start()

    @pl.loop(0, TOK // SEG)
    def _(t):
        keys = pl.ds(pl.multiple_of(t * SEG, SEG), SEG)
        blocks = pl.ds(t * (SEG // BLOCK), SEG // BLOCK)
        for h in range(HEADS_DEV):
            hs = slice(h * DH, (h + 1) * DH)
            v = v_ref[blocks, :, hs].reshape(SEG, DH)
            kt = kt_loc[hs, keys]
            dk_sum = jnp.zeros((SEG, DH), F32)
            dv_sum = jnp.zeros((SEG, DH), F32)
            for j in range(SEG // TILE):
                qs = pl.ds(pl.multiple_of(t * SEG + j * TILE, TILE), TILE)
                dq, dk, dv = back(h, qs, [(p_loc[h, :, qs], m_loc[h, :, qs])], v, kt)
                dqt[hs, qs] += dq
                dk_sum = dk_sum + dk
                dv_sum = dv_sum + dv
            dkv[keys, hs] = dk_sum * SCALE
            dkv[keys, COLS + h * DH : COLS + (h + 1) * DH] = dv_sum

    for t in range(TOK // TILE):
        cols = slice(t * TILE, (t + 1) * TILE)
        dq_ref[cols, :] = jnp.transpose(dqt[:, cols] * SCALE).astype(BF16)
    dq_copy = pltpu.make_async_copy(dq_ref, dq_hbm, io.at[1])
    dq_copy.start()
    gg_copy(4).wait()
    gg_ref[...] = gsum[6, 0:1, :] + gsum[7, 0:1, :]

    for h in range(HEADS_DEV):
        gr_copy(2, h).wait()

    @pl.loop(0, TOK // BLOCK)
    def _(b):
        slot = inv_slot[b]
        rows = pl.ds(pl.multiple_of(b * BLOCK, BLOCK), BLOCK)
        used = jnp.minimum(slot + 1, 1).astype(F32)
        for h in range(HEADS_DEV):
            part = gr_in2[h, jnp.maximum(slot, 0)].astype(F32) * used
            dkv[rows, h * DH : (h + 1) * DH] += part[:, 0:DH]
            dkv[rows, COLS + h * DH : COLS + (h + 1) * DH] += part[:, DH:]

    part_copy = pltpu.make_async_copy(dkv, part_hbm, io.at[2])
    part_copy.start()

    def own_copy(level):
        return pltpu.make_async_copy(gr_out.at[level, 1], gr_hbm.at[level, 1], io.at[3 + level])

    @pl.loop(0, 2)
    def _(level):
        for one in range(2):

            @pl.when(level == one)
            def _():
                rows_copy(one).wait()
                if one == 1:
                    for c in range(HALVES):
                        q_copy(1, c).wait()
                        do_copy(1, c).wait()

        ka = jnp.concatenate([kv_out[level, :, DH:COLS], mk_own[level]], axis=1)
        v = kv_out[level, :, COLS + DH :]
        dk_sum = jnp.zeros((KEPT, DH), F32)
        dv_sum = jnp.zeros((KEPT, DH), F32)
        for j in range(TOK // TILE):
            qs = slice(j * TILE, (j + 1) * TILE)
            pieces = range(j * (TILE // DH), (j + 1) * (TILE // DH))
            logs = jnp.concatenate([rows_in[level, i : i + 1, 0:DH] for i in pieces], axis=1)
            deltas = jnp.concatenate([rows_in[level, i : i + 1, DH:] for i in pieces], axis=1)
            q = q_in[level, qs, :]
            do = do_in[level, :, qs]
            s = dot(ka, jnp.concatenate([q, mq_far[level, qs, :]], axis=1), 1, 1)
            probs = jnp.exp2((s - logs) * coef)
            ds = (probs * (dot(v, do, 1, 0) - deltas)).astype(BF16)
            dk_sum = dk_sum + dot(ds, q, 1, 0)
            dv_sum = dv_sum + dot(probs.astype(BF16), do, 1, 1)
        keep_grads(level, 1, dk_sum, dv_sum)
        for one in range(2):
            pl.when(level == one)(lambda one=one: own_copy(one).start())

    for level in range(2):
        gr_copy(level, 0).wait()
    for level in range(2):
        own_copy(level).wait()
    lo_copy.wait()
    dq_copy.wait()
    part_copy.wait()


def finish(
    kept_hbm,
    lo_in,
    dq_in,
    part_in,
    gr_in,
    gg_in,
    lo_ref,
    dq_ref,
    dk_ref,
    dv_ref,
    gg_ref,
    kept,
    dk,
    dv,
    sems,
    few,
):
    me = lax.axis_index("seq")
    kept_copy = pltpu.make_async_copy(kept_hbm, kept, few.at[0])
    kept_copy.start()
    copies = [pltpu.make_async_copy(gg_in, gg_ref, few.at[1])]
    copies[0].start()

    def send(src, dst, i, lane):
        rows = pl.ds(i * TILE, TILE)
        copy = pltpu.make_async_copy(src.at[rows], dst.at[rows], sems.at[lane, i])
        copy.start()
        copies.append(copy)

    for i in range(TOK // TILE):
        send(lo_in, lo_ref, i, 0)
        send(dq_in, dq_ref, i, 1)
    kept_copy.wait()
    for i in range(TOK // TILE):
        for b in range(i * (TILE // BLOCK), (i + 1) * (TILE // BLOCK)):
            rows = slice(b * BLOCK, (b + 1) * BLOCK)
            total = part_in[rows, :]
            key = [total[:, h * DH : (h + 1) * DH] for h in range(HEADS_DEV)]
            value = [total[:, COLS + h * DH : COLS + (h + 1) * DH] for h in range(HEADS_DEV)]
            for level in range(2):
                found = jnp.int32(-1)
                for slot in range(KEEP):
                    found = jnp.where(kept[level, slot, me] == b, jnp.int32(slot), found)
                used = jnp.minimum(found + 1, 1).astype(F32)
                for h in range(HEADS_DEV):
                    part = gr_in[level, h, jnp.maximum(found, 0)].astype(F32) * used
                    key[h] = key[h] + part[:, 0:DH]
                    value[h] = value[h] + part[:, DH:]
            for h in range(HEADS_DEV):
                dk[rows, h * DH : (h + 1) * DH] = key[h].astype(BF16)
                dv[rows, h * DH : (h + 1) * DH] = value[h].astype(BF16)
        send(dk, dk_ref, i, 2)
        send(dv, dv_ref, i, 3)
    for copy in copies:
        copy.wait()


def local(query_rows, key_rows, value_rows, norm_gain, grad_out, doc_lengths, kept_blocks):
    vmem = pl.BlockSpec(memory_space=pltpu.VMEM)
    hbm = pl.BlockSpec(memory_space=pltpu.HBM)
    some = pl.BlockSpec(memory_space=pl.ANY)
    rows = jax.ShapeDtypeStruct((TOK, COLS), BF16)
    dma = pltpu.SemaphoreType.DMA
    scratch = [
        pltpu.SMEM((LEVELS, KEEP, N_SEQ), jnp.int32),
        pltpu.SMEM((3,), jnp.int32),
        pltpu.VMEM((TOK, COLS), BF16),
        pltpu.VMEM((TOK // BLOCK, BLOCK, COLS), BF16),
        pltpu.VMEM((TOK // BLOCK, BLOCK, COLS), BF16),
        pltpu.VMEM((1, COLS), F32),
        pltpu.VMEM((TOK, COLS), BF16),
        pltpu.VMEM((TOK, COLS), BF16),
        pltpu.VMEM((TOK, COLS), BF16),
        pltpu.VMEM((HEADS_DEV, TOK, 2 * DH), BF16),
        pltpu.VMEM((TOK, DH), BF16),
        pltpu.VMEM((LEVELS, KEPT, DH), BF16),
        pltpu.VMEM((LEVELS, KEPT, 2 * COLS), BF16),
        pltpu.VMEM((LEVELS, KEPT, 2 * COLS), BF16),
        pltpu.VMEM((LEVELS, HEADS_DEV, KEEP, BLOCK, 2 * DH), BF16),
        pltpu.VMEM((HEADS_DEV, KEEP, BLOCK, 2 * DH), BF16),
        pltpu.VMEM((COLS, TOK), BF16),
        pltpu.VMEM((HEADS_DEV, DH + 16, TOK), BF16),
        pltpu.VMEM((LEVELS, COLS, KEPT), BF16),
        pltpu.VMEM((LEVELS, HEADS_DEV, DH + 16, KEPT), BF16),
        pltpu.VMEM((HEADS_DEV, SEG, TOK), BF16),
        pltpu.VMEM((LEVELS, HEADS_DEV, KEPT, TOK), BF16),
        pltpu.VMEM((HEADS_DEV, 1, TOK), F32),
        pltpu.VMEM((HEADS_DEV, 1, TOK), F32),
        pltpu.VMEM((LEVELS, NCH, HEADS_DEV, 1, TOK), F32),
        pltpu.VMEM((HEADS_DEV, DH + 16, TOK), F32),
        pltpu.VMEM((HEADS_DEV, 1, TOK), F32),
        pltpu.VMEM((COLS, TOK), F32),
        pltpu.VMEM((COLS, TOK), F32),
        pltpu.VMEM((COLS, DH), F32),
        pltpu.VMEM((N_HEAD, 8, 384), F32),
        pltpu.VMEM((N_HEAD, 8, DH), F32),
        pltpu.VMEM((8, 512), F32),
        pltpu.VMEM((COLS, TOK), BF16),
        pltpu.VMEM((HEADS_DEV, 1, TOK), F32),
        pltpu.VMEM((COLS, TOK), F32),
        pltpu.VMEM((TOK, 2 * COLS), F32),
        pltpu.VMEM((8, 8, COLS), F32),
        pltpu.SMEM((TOK // BLOCK,), jnp.int32),
        pltpu.VMEM((2, TOK, DH), BF16),
        pltpu.VMEM((2, KEPT, DH), BF16),
        pltpu.VMEM((2, TOK, DH), BF16),
        pltpu.VMEM((2, DH, TOK), BF16),
        pltpu.VMEM((8, 2 * DH), F32),
        pltpu.VMEM((2, 8, 2 * DH), F32),
        dma((2, HALVES)),
        dma((2, HALVES)),
        dma((2, HALVES)),
        dma((2, HALVES)),
        dma((2,)),
        dma((2,)),
        dma((LEVELS, NCH)),
        dma((LEVELS, NCH)),
        dma((LEVELS, HEADS_DEV)),
        dma((LEVELS, HEADS_DEV)),
        dma((2, N_HEAD)),
        dma((2, N_HEAD)),
        dma((5,)),
        dma((5,)),
        dma((19,)),
    ]
    kept = jnp.transpose(kept_blocks, (1, 2, 0))
    gain_row = jax.ShapeDtypeStruct((1, COLS), F32)
    lo, dq, part, returned, gain = pl.pallas_call(
        kernel,
        out_shape=[
            pltpu.VMEM((TOK, COLS), BF16),
            pltpu.VMEM((TOK, COLS), BF16),
            pltpu.VMEM((TOK, 2 * COLS), F32),
            pltpu.VMEM((2, HEADS_DEV, KEEP, BLOCK, 2 * DH), BF16),
            pltpu.VMEM((1, COLS), F32),
        ],
        in_specs=[hbm] * 7,
        out_specs=[some] * 4 + [vmem],
        scratch_shapes=scratch,
        compiler_params=pltpu.CompilerParams(
            collective_id=0, has_side_effects=True, vmem_limit_bytes=44 * 1024 * 1024
        ),
        name="attention",
    )(
        *(
            pltpu.with_memory_space_constraint(x, pltpu.HBM)
            for x in (
                kept,
                doc_lengths,
                query_rows,
                key_rows.reshape(TOK // BLOCK, BLOCK, COLS),
                value_rows.reshape(TOK // BLOCK, BLOCK, COLS),
                norm_gain.reshape(1, COLS),
                grad_out,
            )
        )
    )
    lo, dq, dk, dv, gain = pl.pallas_call(
        finish,
        out_shape=[rows, rows, rows, rows, gain_row],
        in_specs=[hbm] + [vmem] * 5,
        out_specs=[hbm] * 5,
        scratch_shapes=[
            pltpu.SMEM((LEVELS, KEEP, N_SEQ), jnp.int32),
            pltpu.VMEM((TOK, COLS), BF16),
            pltpu.VMEM((TOK, COLS), BF16),
            dma((4, TOK // TILE)),
            dma((2,)),
        ],
        compiler_params=pltpu.CompilerParams(vmem_limit_bytes=12 * 1024 * 1024),
        name="finish",
    )(pltpu.with_memory_space_constraint(kept, pltpu.HBM), lo, dq, part, returned, gain)
    return lo, dq, dk, dv, gain.reshape(COLS)


def solution(mesh):
    rows = P("seq", "head")
    in_specs = (rows, rows, rows, P("head"), rows, P(), P())
    out_specs = (rows, rows, rows, rows, P("head"))
    return jax.shard_map(local, mesh=mesh, in_specs=in_specs, out_specs=out_specs, check_vma=False)
```

```python
import functools

import jax
import jax.numpy as jnp
from jax import lax
from jax.experimental import pallas as pl
from jax.experimental.pallas import tpu as pltpu
from jax.sharding import PartitionSpec as P

DH = 128
TOK = 1024
SEG = 512
BLOCK = 64
KEEP = 8
LEVELS = 3
KEPT = KEEP * BLOCK
CHUNK = 256
NCH = KEPT // CHUNK
TILE = 256
WIDTH = 2048
HALVES = 2
HEADS_DEV = 2
COLS = HEADS_DEV * DH
N_SEQ = 16
N_HEAD = 8
NORM_EPS = 1e-05
SCALE = DH**-0.5
LOG2E = 1.4426950408889634
BIG = 2.0**100
LOW = -(2.0**99)
MESH = pl.DeviceIdType.MESH
F32 = jnp.float32
BF16 = jnp.bfloat16


def dot(a, b, ca, cb):
    return lax.dot_general(a, b, (((ca,), (cb,)), ((), ())), preferred_element_type=F32)


def turned(x):
    return jnp.transpose(x.astype(F32)).astype(x.dtype)


def flipped(index, bit):
    return index + bit * (1 - 2 * lax.rem(index // bit, 2))


def level_bit(level):
    return 1 + level + level // 2


def kernel(
    kept_hbm,
    lengths_hbm,
    q_hbm,
    k_hbm,
    v_hbm,
    gain_hbm,
    g_hbm,
    lo_hbm,
    dq_hbm,
    part_hbm,
    gr_hbm,
    gg_ref,
    kept,
    lengths,
    q_ref,
    k_ref,
    v_ref,
    gain_ref,
    g_ref,
    lo_ref,
    dq_ref,
    qa,
    mk_loc,
    mk_far,
    kv_out,
    kv_in,
    gr_out,
    gr_in2,
    kt_loc,
    vt_loc,
    kt_far,
    vt_far,
    p_loc,
    p_far,
    m_run,
    m_loc,
    m_far,
    acc,
    inv_l,
    at,
    gt,
    gc,
    st,
    early,
    res,
    dot_,
    delta,
    dqt,
    dkv,
    gsum,
    inv_slot,
    mq_far,
    mk_own,
    q_in,
    do_in,
    rows_out,
    rows_in,
    q_ss,
    q_rs,
    do_ss,
    do_rs,
    ro_ss,
    ro_rs,
    kv_ss,
    kv_rs,
    gr_ss,
    gr_rs,
    st_ss,
    st_rs,
    gg_ss,
    gg_rs,
    io,
):
    me = lax.axis_index("seq")
    col = lax.axis_index("head")

    barrier = pltpu.get_barrier_semaphore()
    beside = flipped(flipped(me, 1), 2)
    for other in [flipped(me, bit) for bit in (1, 2, 4, 8)] + [beside]:
        pl.semaphore_signal(barrier, inc=1, device_id=(other, col), device_id_type=MESH)
    for d in range(1, N_HEAD):
        pl.semaphore_signal(
            barrier, inc=1, device_id=(me, lax.rem(col + d, N_HEAD)), device_id_type=MESH
        )

    def load(src, dst, pieces, first):
        size = src.shape[0] // pieces
        copies = []
        for i in range(pieces):
            rows = pl.ds(i * size, size)
            copies.append(pltpu.make_async_copy(src.at[rows], dst.at[rows], io.at[first + i]))
            copies[-1].start()
        return copies

    loads = load(k_hbm, k_ref, 4, 0) + load(v_hbm, v_ref, 4, 4) + load(kept_hbm, kept, 1, 8)
    later = load(q_hbm, q_ref, 4, 9) + load(g_hbm, g_ref, 4, 13) + load(gain_hbm, gain_ref, 1, 17)
    lengths_copy = pltpu.make_async_copy(lengths_hbm, lengths, io.at[18])
    lengths_copy.start()
    for copy in loads:
        copy.wait()

    def kv_copy(level, c):
        rows = pl.ds(pl.multiple_of(c * CHUNK, CHUNK), CHUNK)
        return pltpu.make_async_remote_copy(
            src_ref=kv_out.at[level, rows],
            dst_ref=kv_in.at[level, rows],
            send_sem=kv_ss.at[level, c],
            recv_sem=kv_rs.at[level, c],
            device_id=(flipped(me, level_bit(level)), col),
            device_id_type=MESH,
        )

    def gr_copy(level, h):
        dst = gr_in2 if level == 2 else gr_hbm.at[level]
        return pltpu.make_async_remote_copy(
            src_ref=gr_out.at[level, h],
            dst_ref=dst.at[h],
            send_sem=gr_ss.at[level, h],
            recv_sem=gr_rs.at[level, h],
            device_id=(flipped(me, level_bit(level)), col),
            device_id_type=MESH,
        )

    def q_copy(hop, c):
        qs = pl.ds(c * (TOK // HALVES), TOK // HALVES)
        return pltpu.make_async_remote_copy(
            src_ref=q_in.at[0, qs] if hop else q_ref.at[qs, pl.ds(DH, DH)],
            dst_ref=q_in.at[hop, qs],
            send_sem=q_ss.at[hop, c],
            recv_sem=q_rs.at[hop, c],
            device_id=(beside if hop else flipped(me, 1), col),
            device_id_type=MESH,
        )

    def do_copy(hop, c):
        qs = pl.ds(c * (TOK // HALVES), TOK // HALVES)
        return pltpu.make_async_remote_copy(
            src_ref=do_in.at[0, :, qs] if hop else dot_.at[pl.ds(DH, DH), qs],
            dst_ref=do_in.at[hop, :, qs],
            send_sem=do_ss.at[hop, c],
            recv_sem=do_rs.at[hop, c],
            device_id=(beside if hop else flipped(me, 1), col),
            device_id_type=MESH,
        )

    def rows_copy(level):
        return pltpu.make_async_remote_copy(
            src_ref=rows_out,
            dst_ref=rows_in.at[level],
            send_sem=ro_ss.at[level],
            recv_sem=ro_rs.at[level],
            device_id=(flipped(me, 1 << level), col),
            device_id_type=MESH,
        )

    for c in range(NCH):
        for level in (1, 0, 2):
            for slot in range(c * KEEP // NCH, (c + 1) * KEEP // NCH):
                block = jnp.maximum(kept[level, slot, me], 0)
                kv_out[level, slot * BLOCK : (slot + 1) * BLOCK, 0:COLS] = k_ref[block]
                kv_out[level, slot * BLOCK : (slot + 1) * BLOCK, COLS:] = v_ref[block]
            if c == 0 and level == 1:
                pl.semaphore_wait(barrier, 5 + N_HEAD - 1)
            kv_copy(level, c).start()

    lengths_copy.wait()
    for copy in later:
        copy.wait()
    start1 = lengths[0]
    start2 = lengths[0] + lengths[1]

    def doc_of(pos):
        return (pos >= start1).astype(jnp.int32) + (pos >= start2).astype(jnp.int32)

    lane = lax.broadcasted_iota(jnp.int32, (BLOCK, DH), 1)
    row = lax.broadcasted_iota(jnp.int32, (BLOCK, DH), 0)
    for b in range(TOK // BLOCK):
        rows = slice(b * BLOCK, (b + 1) * BLOCK)
        docs = doc_of(me * TOK + b * BLOCK + row)
        same = docs == lane
        mq = jnp.where(same, 1.0, 0.0).astype(BF16)
        mk_loc[rows, :] = jnp.where(same | (lane >= 3), 0.0, -BIG).astype(BF16)
        for h in range(HEADS_DEV):
            qa[h, rows, DH:] = mq
            qa[h, rows, 0:DH] = q_ref[rows, h * DH : (h + 1) * DH]
    for level in range(LEVELS):
        partner = flipped(me, level_bit(level))
        for slot in range(KEEP):
            listed = kept[level, slot, partner]
            docs = doc_of(partner * TOK + jnp.maximum(listed, 0) * BLOCK + row)
            docs = docs - 3 * jnp.minimum(listed, 0)
            same = docs == lane
            mk_far[level, slot * BLOCK : (slot + 1) * BLOCK, :] = jnp.where(
                same | (lane >= 3), 0.0, -BIG
            ).astype(BF16)

    for level in range(2):
        partner = flipped(me, level_bit(level))
        for b in range(TOK // BLOCK):
            same = doc_of(partner * TOK + b * BLOCK + row) == lane
            mq_far[level, b * BLOCK : (b + 1) * BLOCK, :] = jnp.where(same, 1.0, 0.0).astype(BF16)
        for slot in range(KEEP):
            listed = kept[level, slot, me]
            docs = doc_of(me * TOK + jnp.maximum(listed, 0) * BLOCK + row)
            docs = docs - 3 * jnp.minimum(listed, 0)
            mk_own[level, slot * BLOCK : (slot + 1) * BLOCK, :] = jnp.where(
                (docs == lane) | (lane >= 3), 0.0, -BIG
            ).astype(BF16)

    ones = jnp.ones((16, TOK), BF16)
    for h in range(HEADS_DEV):
        vt_loc[h, DH:, :] = ones
        for level in range(LEVELS):
            vt_far[level, h, DH:, :] = ones[:, 0:KEPT]

    for t in range(TOK // TILE):
        cols = slice(t * TILE, (t + 1) * TILE)
        blocks = slice(t * (TILE // BLOCK), (t + 1) * (TILE // BLOCK))
        kt_loc[:, cols] = turned(k_ref[blocks].reshape(TILE, COLS))
        vt = turned(v_ref[blocks].reshape(TILE, COLS))
        for h in range(HEADS_DEV):
            vt_loc[h, 0:DH, cols] = vt[h * DH : (h + 1) * DH]

    coef = SCALE * LOG2E

    @pl.loop(0, TOK // SEG)
    def _(t):
        keys = pl.ds(pl.multiple_of(t * SEG, SEG), SEG)
        blocks = pl.ds(t * (SEG // BLOCK), SEG // BLOCK)
        for h in range(HEADS_DEV):
            k = k_ref[blocks, :, h * DH : (h + 1) * DH].reshape(SEG, DH)
            ka = jnp.concatenate([k, mk_loc[keys, :]], axis=1)
            vt = vt_loc[h, :, keys]
            for j in range(SEG // TILE):
                qs = pl.ds(pl.multiple_of(t * SEG + j * TILE, TILE), TILE)
                s = dot(ka, qa[h, qs, :], 1, 1)
                m = jnp.maximum(jnp.max(s, axis=0, keepdims=True), LOW)
                p = jnp.exp2((s - m) * coef).astype(BF16)
                p_loc[h, :, qs] = p
                m_run[h, :, qs] = m
                m_loc[h, :, qs] = m
                acc[h, :, qs] = dot(vt, p, 1, 0)

    gc[...] = jnp.transpose(jnp.broadcast_to(gain_ref[...], (DH, COLS)))
    for t in range(TOK // TILE):
        cols = slice(t * TILE, (t + 1) * TILE)
        gt[:, cols] = jnp.transpose(g_ref[cols, :].astype(F32))

    for i in range(TOK // DH):
        scaled = gt[:, i * DH : (i + 1) * DH] * gc[...]
        early[0, i : i + 1, :] = jnp.sum(scaled, axis=0, keepdims=True)

    def row_copy(buffer, lane, d):
        return pltpu.make_async_remote_copy(
            src_ref=buffer.at[0],
            dst_ref=buffer.at[d],
            send_sem=st_ss.at[lane, d],
            recv_sem=st_rs.at[lane, d],
            device_id=(me, lax.rem(col + d, N_HEAD)),
            device_id_type=MESH,
        )

    for d in range(1, N_HEAD):
        row_copy(early, 0, d).start()

    @pl.loop(0, TOK // BLOCK)
    def _(b):
        found = jnp.int32(-1)
        for slot in range(KEEP):
            off = kept[2, slot, me] - b
            found = jnp.maximum(found, (slot + 1) * (1 - jnp.minimum(off * off, 1)) - 1)
        inv_slot[b] = found

    @pl.loop(0, LEVELS * NCH)
    def _(t):
        level = 2 - lax.rem(t, 3)
        c = t // 3
        kv_copy(level, c).wait()

        @pl.when(t == LEVELS * NCH - 1)
        def _():
            for half in range(HALVES):
                q_copy(0, half).start()

        rows = pl.ds(pl.multiple_of(c * CHUNK, CHUNK), CHUNK)
        kt_far[level, :, rows] = turned(kv_in[level, rows, 0:COLS])
        vt = turned(kv_in[level, rows, COLS:])
        for h in range(HEADS_DEV):
            vt_far[level, h, 0:DH, rows] = vt[h * DH : (h + 1) * DH]
        for h in range(HEADS_DEV):
            ka = jnp.concatenate(
                [kv_in[level, rows, h * DH : (h + 1) * DH], mk_far[level, rows, :]], axis=1
            )
            vta = vt_far[level, h, :, rows]
            for j in range(TOK // TILE):
                qs = slice(j * TILE, (j + 1) * TILE)
                s = dot(ka, qa[h, qs, :], 1, 1)
                m_old = m_run[h, :, qs]
                m = jnp.maximum(jnp.max(s, axis=0, keepdims=True), m_old)
                p = jnp.exp2((s - m) * coef).astype(BF16)
                p_far[level, h, rows, qs] = p
                m_run[h, :, qs] = m
                m_far[level, c, h, :, qs] = m
                acc[h, :, qs] = acc[h, :, qs] * jnp.exp2((m_old - m) * coef) + dot(vta, p, 1, 0)

    for i in range(TOK // DH):
        qs = slice(i * DH, (i + 1) * DH)
        total = jnp.zeros((1, DH), F32)
        for h in range(HEADS_DEV):
            inv = 1.0 / acc[h, DH : DH + 1, qs]
            inv_l[h, :, qs] = inv
            a = (acc[h, 0:DH, qs] * inv).astype(BF16).astype(F32)
            at[h * DH : (h + 1) * DH, qs] = a
            total = total + jnp.sum(a, axis=0, keepdims=True)
        mean = total * (1.0 / COLS)
        centred = at[:, qs] - mean
        scaled = gt[:, qs] * gc[...]
        st[0, i : i + 1, 0:128] = mean
        st[0, i : i + 1, 128:256] = jnp.sum(centred * centred, axis=0, keepdims=True)
        st[0, i : i + 1, 256:384] = jnp.sum(scaled * centred, axis=0, keepdims=True)

    for d in (4, 3, 5, 2, 6, 1, 7):
        row_copy(st, 1, d).start()
    for d in range(1, N_HEAD):
        row_copy(early, 0, d).wait()
    for d in range(1, N_HEAD):
        row_copy(st, 1, d).wait()

    mean = st[0, :, 0:128]
    for d in range(1, N_HEAD):
        mean = mean + st[d, :, 0:128]
    mean = mean * (1.0 / N_HEAD)
    square = jnp.zeros((8, DH), F32)
    plain = jnp.zeros((8, DH), F32)
    cross = jnp.zeros((8, DH), F32)
    for d in range(N_HEAD):
        off = st[d, :, 0:128] - mean
        square = square + (st[d, :, 128:256] + COLS * (off * off))
        plain = plain + early[d]
        cross = cross + (st[d, :, 256:384] + off * early[d])
    inv_std = lax.rsqrt(square * (1.0 / WIDTH) + NORM_EPS)
    res[:, 0:128] = mean
    res[:, 128:256] = inv_std
    res[:, 256:384] = plain * (1.0 / WIDTH)
    res[:, 384:512] = inv_std * cross * (1.0 / WIDTH)

    gain_part = jnp.zeros((COLS, DH), F32)
    for i in range(TOK // DH):
        qs = slice(i * DH, (i + 1) * DH)
        inv_std = res[i : i + 1, 128:256]
        normed = (at[:, qs] - res[i : i + 1, 0:128]) * inv_std
        scaled = gt[:, qs] * gc[...]
        do = inv_std * (scaled - res[i : i + 1, 256:384] - normed * res[i : i + 1, 384:512])
        do = do.astype(BF16)
        dot_[:, qs] = do
        gain_part = gain_part + gt[:, qs] * normed
        both = do.astype(F32) * at[:, qs]
        for h in range(HEADS_DEV):
            delta[h, :, qs] = jnp.sum(both[h * DH : (h + 1) * DH], axis=0, keepdims=True)
        log_l = jnp.log(acc[1, DH : DH + 1, qs])
        rows_out[i : i + 1, 0:DH] = m_run[1, :, qs] + log_l * (1.0 / SCALE)
        rows_out[i : i + 1, DH:] = delta[1, :, qs]

    def back(h, qs, parts, v, kt, whole=True):
        probs = jnp.concatenate(
            [
                p.astype(F32) * (jnp.exp2((m - m_run[h, :, qs]) * coef) * inv_l[h, :, qs])
                for p, m in parts
            ],
            axis=0,
        )
        do = dot_[h * DH : (h + 1) * DH, qs]
        dp = dot(v, do, 1, 0)
        ds = (probs * (dp - delta[h, :, qs])).astype(BF16)
        dq = dot(kt, ds, 1, 0)
        if not whole:
            return dq, None, None
        dk = dot(ds, qa[h, qs, 0:DH], 1, 0)
        dv = dot(probs.astype(BF16), do, 1, 1)
        return dq, dk, dv

    dqt[...] = jnp.zeros_like(dqt)

    gsum[0] = jnp.broadcast_to(jnp.sum(jnp.transpose(gain_part), axis=0, keepdims=True), (8, COLS))

    def gg_copy(stage):
        flip, src, dst = ((1, 0, 1), (2, 0, 2), (3, 0, 3), (4, 4, 5), (8, 6, 7))[stage]
        return pltpu.make_async_remote_copy(
            src_ref=gsum.at[src],
            dst_ref=gsum.at[dst],
            send_sem=gg_ss.at[stage],
            recv_sem=gg_rs.at[stage],
            device_id=(beside if flip == 3 else flipped(me, flip), col),
            device_id_type=MESH,
        )

    for stage in range(3):
        gg_copy(stage).start()
    for level in range(2):
        rows_copy(level).start()
    for c in range(HALVES):
        do_copy(0, c).start()

    def back_level(level, h, whole):
        hs = slice(h * DH, (h + 1) * DH)
        v = kv_in[level, :, COLS + h * DH : COLS + (h + 1) * DH]
        kt = kt_far[level, hs, :]
        dk_sum = jnp.zeros((KEPT, DH), F32)
        dv_sum = jnp.zeros((KEPT, DH), F32)
        for j in range(TOK // TILE):
            qs = slice(j * TILE, (j + 1) * TILE)
            parts = [
                (p_far[level, h, c * CHUNK : (c + 1) * CHUNK, qs], m_far[level, c, h, :, qs])
                for c in range(NCH)
            ]
            dq, dk, dv = back(h, qs, parts, v, kt, whole)
            dqt[hs, qs] += dq
            if whole:
                dk_sum = dk_sum + dk
                dv_sum = dv_sum + dv
        if whole:
            keep_grads(level, h, dk_sum, dv_sum)

    def keep_grads(level, h, dk_sum, dv_sum):
        shape = (KEEP, BLOCK, DH)
        gr_out[level, h, :, :, 0:DH] = (dk_sum * SCALE).astype(BF16).reshape(shape)
        gr_out[level, h, :, :, DH:] = dv_sum.astype(BF16).reshape(shape)

    back_level(0, 0, True)
    for c in range(HALVES):
        q_copy(0, c).wait()
        q_copy(1, c).start()
    gr_copy(0, 0).start()
    back_level(2, 0, True)
    for stage in range(3):
        gg_copy(stage).wait()
    gsum[4] = (gsum[0] + gsum[1]) + (gsum[2] + gsum[3])
    gg_copy(3).start()
    gr_copy(2, 0).start()
    back_level(1, 0, True)
    do_copy(0, 0).wait()
    do_copy(1, 0).start()
    gr_copy(1, 0).start()
    back_level(2, 1, True)
    do_copy(0, 1).wait()
    do_copy(1, 1).start()
    gg_copy(3).wait()
    gsum[6] = gsum[4] + gsum[5]
    gg_copy(4).start()
    gr_copy(2, 1).start()

    @pl.loop(0, 2)
    def _(level):
        back_level(level, 1, False)

    for i in range(TOK // DH):
        qs = slice(i * DH, (i + 1) * DH)
        normed = (at[:, qs] - res[i : i + 1, 0:128]) * res[i : i + 1, 128:256]
        lo_ref[qs, :] = jnp.transpose(normed * gc[...]).astype(BF16)
    lo_copy = pltpu.make_async_copy(lo_ref, lo_hbm, io.at[0])
    lo_copy.start()

    @pl.loop(0, TOK // SEG)
    def _(t):
        keys = pl.ds(pl.multiple_of(t * SEG, SEG), SEG)
        blocks = pl.ds(t * (SEG // BLOCK), SEG // BLOCK)
        for h in range(HEADS_DEV):
            hs = slice(h * DH, (h + 1) * DH)
            v = v_ref[blocks, :, hs].reshape(SEG, DH)
            kt = kt_loc[hs, keys]
            dk_sum = jnp.zeros((SEG, DH), F32)
            dv_sum = jnp.zeros((SEG, DH), F32)
            for j in range(SEG // TILE):
                qs = pl.ds(pl.multiple_of(t * SEG + j * TILE, TILE), TILE)
                dq, dk, dv = back(h, qs, [(p_loc[h, :, qs], m_loc[h, :, qs])], v, kt)
                dqt[hs, qs] += dq
                dk_sum = dk_sum + dk
                dv_sum = dv_sum + dv
            dkv[keys, hs] = dk_sum * SCALE
            dkv[keys, COLS + h * DH : COLS + (h + 1) * DH] = dv_sum

    for t in range(TOK // TILE):
        cols = slice(t * TILE, (t + 1) * TILE)
        dq_ref[cols, :] = jnp.transpose(dqt[:, cols] * SCALE).astype(BF16)
    dq_copy = pltpu.make_async_copy(dq_ref, dq_hbm, io.at[1])
    dq_copy.start()
    gg_copy(4).wait()
    gg_ref[...] = gsum[6, 0:1, :] + gsum[7, 0:1, :]

    for h in range(HEADS_DEV):
        gr_copy(2, h).wait()

    @pl.loop(0, TOK // BLOCK)
    def _(b):
        slot = inv_slot[b]
        rows = pl.ds(pl.multiple_of(b * BLOCK, BLOCK), BLOCK)
        used = jnp.minimum(slot + 1, 1).astype(F32)
        for h in range(HEADS_DEV):
            part = gr_in2[h, jnp.maximum(slot, 0)].astype(F32) * used
            dkv[rows, h * DH : (h + 1) * DH] += part[:, 0:DH]
            dkv[rows, COLS + h * DH : COLS + (h + 1) * DH] += part[:, DH:]

    part_copy = pltpu.make_async_copy(dkv, part_hbm, io.at[2])
    part_copy.start()

    def own_copy(level):
        return pltpu.make_async_copy(gr_out.at[level, 1], gr_hbm.at[level, 1], io.at[3 + level])

    @pl.loop(0, 2)
    def _(level):
        for one in range(2):

            @pl.when(level == one)
            def _():
                rows_copy(one).wait()
                if one == 1:
                    for c in range(HALVES):
                        q_copy(1, c).wait()
                        do_copy(1, c).wait()

        ka = jnp.concatenate([kv_out[level, :, DH:COLS], mk_own[level]], axis=1)
        v = kv_out[level, :, COLS + DH :]
        dk_sum = jnp.zeros((KEPT, DH), F32)
        dv_sum = jnp.zeros((KEPT, DH), F32)
        for j in range(TOK // TILE):
            qs = slice(j * TILE, (j + 1) * TILE)
            pieces = range(j * (TILE // DH), (j + 1) * (TILE // DH))
            logs = jnp.concatenate([rows_in[level, i : i + 1, 0:DH] for i in pieces], axis=1)
            deltas = jnp.concatenate([rows_in[level, i : i + 1, DH:] for i in pieces], axis=1)
            q = q_in[level, qs, :]
            do = do_in[level, :, qs]
            s = dot(ka, jnp.concatenate([q, mq_far[level, qs, :]], axis=1), 1, 1)
            probs = jnp.exp2((s - logs) * coef)
            ds = (probs * (dot(v, do, 1, 0) - deltas)).astype(BF16)
            dk_sum = dk_sum + dot(ds, q, 1, 0)
            dv_sum = dv_sum + dot(probs.astype(BF16), do, 1, 1)
        keep_grads(level, 1, dk_sum, dv_sum)
        for one in range(2):
            pl.when(level == one)(lambda one=one: own_copy(one).start())

    for level in range(2):
        gr_copy(level, 0).wait()
    for level in range(2):
        own_copy(level).wait()
    lo_copy.wait()
    dq_copy.wait()
    part_copy.wait()


def finish(
    kept_hbm,
    lo_in,
    dq_in,
    part_in,
    gr_in,
    gg_in,
    lo_ref,
    dq_ref,
    dk_ref,
    dv_ref,
    gg_ref,
    kept,
    dk,
    dv,
    sems,
    few,
):
    me = lax.axis_index("seq")
    kept_copy = pltpu.make_async_copy(kept_hbm, kept, few.at[0])
    kept_copy.start()
    copies = [pltpu.make_async_copy(gg_in, gg_ref, few.at[1])]
    copies[0].start()

    def send(src, dst, i, lane, size=TILE):
        rows = pl.ds(i * size, size)
        copy = pltpu.make_async_copy(src.at[rows], dst.at[rows], sems.at[lane, i])
        copy.start()
        copies.append(copy)

    for i in range(TOK // TILE):
        send(lo_in, lo_ref, i, 0)
        send(dq_in, dq_ref, i, 1)
    kept_copy.wait()
    for i in range(TOK // DH):
        for b in range(i * (DH // BLOCK), (i + 1) * (DH // BLOCK)):
            rows = slice(b * BLOCK, (b + 1) * BLOCK)
            total = part_in[rows, :]
            key = [total[:, h * DH : (h + 1) * DH] for h in range(HEADS_DEV)]
            value = [total[:, COLS + h * DH : COLS + (h + 1) * DH] for h in range(HEADS_DEV)]
            for level in range(2):
                found = jnp.int32(-1)
                for slot in range(KEEP):
                    found = jnp.where(kept[level, slot, me] == b, jnp.int32(slot), found)
                used = jnp.minimum(found + 1, 1).astype(F32)
                for h in range(HEADS_DEV):
                    part = gr_in[level, h, jnp.maximum(found, 0)].astype(F32) * used
                    key[h] = key[h] + part[:, 0:DH]
                    value[h] = value[h] + part[:, DH:]
            for h in range(HEADS_DEV):
                dk[rows, h * DH : (h + 1) * DH] = key[h].astype(BF16)
                dv[rows, h * DH : (h + 1) * DH] = value[h].astype(BF16)
        send(dk, dk_ref, i, 2, DH)
        send(dv, dv_ref, i, 3, DH)
    for copy in copies:
        copy.wait()


def local(query_rows, key_rows, value_rows, norm_gain, grad_out, doc_lengths, kept_blocks):
    vmem = pl.BlockSpec(memory_space=pltpu.VMEM)
    hbm = pl.BlockSpec(memory_space=pltpu.HBM)
    some = pl.BlockSpec(memory_space=pl.ANY)
    rows = jax.ShapeDtypeStruct((TOK, COLS), BF16)
    dma = pltpu.SemaphoreType.DMA
    scratch = [
        pltpu.SMEM((LEVELS, KEEP, N_SEQ), jnp.int32),
        pltpu.SMEM((3,), jnp.int32),
        pltpu.VMEM((TOK, COLS), BF16),
        pltpu.VMEM((TOK // BLOCK, BLOCK, COLS), BF16),
        pltpu.VMEM((TOK // BLOCK, BLOCK, COLS), BF16),
        pltpu.VMEM((1, COLS), F32),
        pltpu.VMEM((TOK, COLS), BF16),
        pltpu.VMEM((TOK, COLS), BF16),
        pltpu.VMEM((TOK, COLS), BF16),
        pltpu.VMEM((HEADS_DEV, TOK, 2 * DH), BF16),
        pltpu.VMEM((TOK, DH), BF16),
        pltpu.VMEM((LEVELS, KEPT, DH), BF16),
        pltpu.VMEM((LEVELS, KEPT, 2 * COLS), BF16),
        pltpu.VMEM((LEVELS, KEPT, 2 * COLS), BF16),
        pltpu.VMEM((LEVELS, HEADS_DEV, KEEP, BLOCK, 2 * DH), BF16),
        pltpu.VMEM((HEADS_DEV, KEEP, BLOCK, 2 * DH), BF16),
        pltpu.VMEM((COLS, TOK), BF16),
        pltpu.VMEM((HEADS_DEV, DH + 16, TOK), BF16),
        pltpu.VMEM((LEVELS, COLS, KEPT), BF16),
        pltpu.VMEM((LEVELS, HEADS_DEV, DH + 16, KEPT), BF16),
        pltpu.VMEM((HEADS_DEV, SEG, TOK), BF16),
        pltpu.VMEM((LEVELS, HEADS_DEV, KEPT, TOK), BF16),
        pltpu.VMEM((HEADS_DEV, 1, TOK), F32),
        pltpu.VMEM((HEADS_DEV, 1, TOK), F32),
        pltpu.VMEM((LEVELS, NCH, HEADS_DEV, 1, TOK), F32),
        pltpu.VMEM((HEADS_DEV, DH + 16, TOK), F32),
        pltpu.VMEM((HEADS_DEV, 1, TOK), F32),
        pltpu.VMEM((COLS, TOK), F32),
        pltpu.VMEM((COLS, TOK), F32),
        pltpu.VMEM((COLS, DH), F32),
        pltpu.VMEM((N_HEAD, 8, 384), F32),
        pltpu.VMEM((N_HEAD, 8, DH), F32),
        pltpu.VMEM((8, 512), F32),
        pltpu.VMEM((COLS, TOK), BF16),
        pltpu.VMEM((HEADS_DEV, 1, TOK), F32),
        pltpu.VMEM((COLS, TOK), F32),
        pltpu.VMEM((TOK, 2 * COLS), F32),
        pltpu.VMEM((8, 8, COLS), F32),
        pltpu.SMEM((TOK // BLOCK,), jnp.int32),
        pltpu.VMEM((2, TOK, DH), BF16),
        pltpu.VMEM((2, KEPT, DH), BF16),
        pltpu.VMEM((2, TOK, DH), BF16),
        pltpu.VMEM((2, DH, TOK), BF16),
        pltpu.VMEM((8, 2 * DH), F32),
        pltpu.VMEM((2, 8, 2 * DH), F32),
        dma((2, HALVES)),
        dma((2, HALVES)),
        dma((2, HALVES)),
        dma((2, HALVES)),
        dma((2,)),
        dma((2,)),
        dma((LEVELS, NCH)),
        dma((LEVELS, NCH)),
        dma((LEVELS, HEADS_DEV)),
        dma((LEVELS, HEADS_DEV)),
        dma((2, N_HEAD)),
        dma((2, N_HEAD)),
        dma((5,)),
        dma((5,)),
        dma((19,)),
    ]
    kept = jnp.transpose(kept_blocks, (1, 2, 0))
    gain_row = jax.ShapeDtypeStruct((1, COLS), F32)
    lo, dq, part, returned, gain = pl.pallas_call(
        kernel,
        out_shape=[
            pltpu.VMEM((TOK, COLS), BF16),
            pltpu.VMEM((TOK, COLS), BF16),
            pltpu.VMEM((TOK, 2 * COLS), F32),
            pltpu.VMEM((2, HEADS_DEV, KEEP, BLOCK, 2 * DH), BF16),
            pltpu.VMEM((1, COLS), F32),
        ],
        in_specs=[hbm] * 7,
        out_specs=[some] * 4 + [vmem],
        scratch_shapes=scratch,
        compiler_params=pltpu.CompilerParams(
            collective_id=0, has_side_effects=True, vmem_limit_bytes=44 * 1024 * 1024
        ),
        name="attention",
    )(
        *(
            pltpu.with_memory_space_constraint(x, pltpu.HBM)
            for x in (
                kept,
                doc_lengths,
                query_rows,
                key_rows.reshape(TOK // BLOCK, BLOCK, COLS),
                value_rows.reshape(TOK // BLOCK, BLOCK, COLS),
                norm_gain.reshape(1, COLS),
                grad_out,
            )
        )
    )
    lo, dq, dk, dv, gain = pl.pallas_call(
        finish,
        out_shape=[rows, rows, rows, rows, gain_row],
        in_specs=[hbm] + [vmem] * 5,
        out_specs=[hbm] * 5,
        scratch_shapes=[
            pltpu.SMEM((LEVELS, KEEP, N_SEQ), jnp.int32),
            pltpu.VMEM((TOK, COLS), BF16),
            pltpu.VMEM((TOK, COLS), BF16),
            dma((4, TOK // DH)),
            dma((2,)),
        ],
        compiler_params=pltpu.CompilerParams(vmem_limit_bytes=12 * 1024 * 1024),
        name="finish",
    )(pltpu.with_memory_space_constraint(kept, pltpu.HBM), lo, dq, part, returned, gain)
    return lo, dq, dk, dv, gain.reshape(COLS)


def solution(mesh):
    rows = P("seq", "head")
    in_specs = (rows, rows, rows, P("head"), rows, P(), P())
    out_specs = (rows, rows, rows, rows, P("head"))
    return jax.shard_map(local, mesh=mesh, in_specs=in_specs, out_specs=out_specs, check_vma=False)
```
